32 devices in a mesh: dp: 8 (over z, y), blk: 4 (over x, core).
Axes of the slice: x: 2, y: 2, z: 4, core: 2. Of those that a mesh axis runs over, the one named last changes fastest.
Arguments:
- tokens: bfloat16 [768, 8, 768], P('blk', 'dp'), may hold values from -6 to 6
- w_query: bfloat16 [768, 768], replicated, may hold values from -0.3125 to 0.3125
- w_key: bfloat16 [768, 768], replicated, may hold values from -0.21875 to 0.21875
- w_value: bfloat16 [768, 768], replicated, may hold values from -0.21875 to 0.21875
- w_out: bfloat16 [768, 768], replicated, may hold values from -1.75 to 1.75
- w_inner: bfloat16 [768, 3072], replicated, may hold values from -0.21875 to 0.21875
- w_outer: bfloat16 [3072, 768], replicated, may hold values from -0.109375 to 0.109375
- down_one: bfloat16 [768, 64], replicated, may hold values from -0.21875 to 0.21875
- dbias_one: float32 [64], replicated, may hold values from -3 to 3
- up_one: bfloat16 [64, 768], replicated, may hold values from -0.75 to 0.75
- ubias_one: float32 [768], replicated, may hold values from -2 to 2
- gain_one: float32 [768], replicated, may hold values from 0.25 to 1.75
- shift_one: float32 [768], replicated, may hold values from -2 to 2
- down_two: bfloat16 [768, 64], replicated, may hold values from -0.21875 to 0.21875
- dbias_two: float32 [64], replicated, may hold values from -3 to 3
- up_two: bfloat16 [64, 768], replicated, may hold values from -0.75 to 0.75
- ubias_two: float32 [768], replicated, may hold values from -2 to 2
- gain_two: float32 [768], replicated, may hold values from 0.25 to 1.75
- shift_two: float32 [768], replicated, may hold values from -2 to 2
- seg_len: int32 [8, 6], P('dp'), may hold values from 0 to 512, as said below
- seg_valid: int32 [8, 6], P('dp'), may hold values from 0 to 512, as said below
- cotangent: bfloat16 [768, 8, 768], P('blk', 'dp'), may hold values from -6 to 6
Outputs:
- mixed: bfloat16 [768, 8, 768], P('blk', 'dp')
- input_grad: bfloat16 [768, 8, 768], P('blk', 'dp')
- grad_down_one: float32 [768, 64], replicated
- grad_dbias_one: float32 [64], replicated
- grad_up_one: float32 [64, 768], replicated
- grad_ubias_one: float32 [768], replicated
- grad_gain_one: float32 [768], replicated
- grad_shift_one: float32 [768], replicated
- grad_down_two: float32 [768, 64], replicated
- grad_dbias_two: float32 [64], replicated
- grad_up_two: float32 [64, 768], replicated
- grad_ubias_two: float32 [768], replicated
- grad_gain_two: float32 [768], replicated
- grad_shift_two: float32 [768], replicated
The draws below stay inside these ranges and needn't reach their ends.
Inputs may be any that keep to these rules, and one draw needn't show every extreme that they name: `seg_len`: each row packs three or four sequences in order into its 6 slots, used slots first, the last two slots always unused (0). Used lengths are 64, 128 or 512 and sum to 768; exactly one slot has 512 and it begins at position 128. `seg_valid`: real tokens at the start of each slot, the rest of the slot being padding: 0 for an unused slot, else from half the slot's length to its length; for the slot of 512 more than 448.
All inputs are finite; a program needn't handle non-finite values.
Results may differ from the reference program's by a relative error of at most 0.02.
Values may be sent and summed in bfloat16 or wider, within the bound.
No kernel may reach another device: no remote copies, remote signals or barrier semaphores. Data moves between devices by JAX's collectives and lax.ppermute only.
A program may use at most 128 MiB of HBM per device.

```python
import jax
import jax.numpy as jnp
import numpy as np
from jax import lax

D = 768
HEADS = 12
HEAD = 64
FF = 3072
ADAPT = 64
LMIN = 64
ROW_LEN = 768
ROWS = 8


LAYOUTS = np.array([[2, 8, 2, 0, 0, 0], [2, 8, 1, 1, 0, 0], [1, 1, 8, 2, 0, 0]], np.int32)


def slot_units(key):
    layout_pick = jax.random.randint(jax.random.fold_in(key, 11), (ROWS,), 0, 3)
    return jnp.asarray(LAYOUTS)[layout_pick]


def draw_seg_len(key, part):
    unit_counts = slot_units(key)
    return (unit_counts * LMIN).astype(jnp.int32)


def draw_seg_valid(key, part):
    unit_counts = slot_units(key)
    key = jax.random.fold_in(key, 5)
    lengths = unit_counts * LMIN
    longest = unit_counts == 8
    lowest = jnp.where(longest, 7 * LMIN + 1, lengths // 2)
    raw_draw = jax.random.randint(key, lengths.shape, 0, 1 << 20)
    counts = lowest + raw_draw % (lengths - lowest + 1)
    first_row = jnp.arange(ROWS)[:, None] == 0
    counts = jnp.where(longest & first_row, lengths, counts)
    return counts.astype(jnp.int32)


def shard_levels(rng, extent, split, least, largest):
    factor_of, own = 1.0, jax.random.fold_in(rng, 6)
    for position, shards_of in split:
        draws = jnp.exp(jax.random.uniform(jax.random.fold_in(own, position), (shards_of,), jnp.float32, least / len(split), largest / len(split)))
        factor_of = factor_of * jnp.repeat(draws, extent[position] // shards_of).reshape([-1 if axis == position else 1 for axis in range(len(extent))])
    return factor_of


def gaussian(stream_key, shape, scale, most, pieces=(), kind=jnp.bfloat16):
    factor_of = shard_levels(stream_key, shape, pieces, -0.22, 0.18) if pieces else 1.0
    values = jax.random.normal(stream_key, shape, jnp.float32) * scale * factor_of
    return jnp.minimum(jnp.maximum(values, -most), most).astype(kind)


def setup_inputs(seed: int = 0) -> dict:
    arg_keys = jax.random.split(jax.random.key(seed), 23)
    tokens = gaussian(arg_keys[0], (ROW_LEN, ROWS, D), 1.0, 6.0, ((0, 4), (1, 8)))
    w_query = gaussian(arg_keys[1], (D, D), (D // 2) ** -0.5, 0.3125)
    w_key = gaussian(arg_keys[2], (D, D), D ** -0.5, 0.21875)
    w_value = gaussian(arg_keys[3], (D, D), D ** -0.5, 0.21875)
    w_out = gaussian(arg_keys[4], (D, D), (D // 64) ** -0.5, 1.75)
    w_inner = gaussian(arg_keys[5], (D, FF), D ** -0.5, 0.21875)
    w_outer = gaussian(arg_keys[6], (FF, D), FF ** -0.5, 0.109375)
    down_one = gaussian(arg_keys[7], (D, ADAPT), D ** -0.5, 0.21875)
    dbias_one = gaussian(arg_keys[8], (ADAPT,), 0.5, 3.0, (), jnp.float32)
    up_one = gaussian(arg_keys[9], (ADAPT, D), ADAPT ** -0.5, 0.75)
    ubias_one = gaussian(arg_keys[10], (D,), 0.3, 2.0, (), jnp.float32)
    gain_one = jnp.clip(1.0 + 0.15 * jax.random.normal(arg_keys[11], (D,), jnp.float32), 0.25, 1.75)
    shift_one = gaussian(arg_keys[12], (D,), 0.3, 2.0, (), jnp.float32)
    down_two = gaussian(arg_keys[13], (D, ADAPT), D ** -0.5, 0.21875)
    dbias_two = gaussian(arg_keys[14], (ADAPT,), 0.5, 3.0, (), jnp.float32)
    up_two = gaussian(arg_keys[15], (ADAPT, D), ADAPT ** -0.5, 0.75)
    ubias_two = gaussian(arg_keys[16], (D,), 0.3, 2.0, (), jnp.float32)
    gain_two = jnp.clip(1.0 + 0.15 * jax.random.normal(arg_keys[17], (D,), jnp.float32), 0.25, 1.75)
    shift_two = gaussian(arg_keys[18], (D,), 0.3, 2.0, (), jnp.float32)
    seg_len = draw_seg_len(jax.random.fold_in(arg_keys[22], 71), 0)
    seg_valid = draw_seg_valid(jax.random.fold_in(arg_keys[22], 71), 0)
    cotangent = gaussian(arg_keys[21], (ROW_LEN, ROWS, D), 1.0, 6.0, ((0, 4), (1, 8)))
    return {"tokens": tokens, "w_query": w_query, "w_key": w_key, "w_value": w_value, "w_out": w_out, "w_inner": w_inner, "w_outer": w_outer, "down_one": down_one, "dbias_one": dbias_one, "up_one": up_one, "ubias_one": ubias_one, "gain_one": gain_one, "shift_one": shift_one, "down_two": down_two, "dbias_two": dbias_two, "up_two": up_two, "ubias_two": ubias_two, "gain_two": gain_two, "shift_two": shift_two, "seg_len": seg_len, "seg_valid": seg_valid, "cotangent": cotangent}


@jax.custom_vjp
def low(v):
    return lax.optimization_barrier(v.astype(jnp.bfloat16)).astype(jnp.float32)

@jax.custom_vjp
def low_back(v):
    return v

def low_keep(v):
    return (low(v), None)

def low_pass(kept, grad):
    return (grad,)

def back_keep(v):
    return (v, None)

def back_low(kept, grad):
    return (low(grad),)
low.defvjp(low_keep, low_pass)
low_back.defvjp(back_keep, back_low)

def rounded_both(value):
    return low(low_back(value))

def matmul(left, right):
    return jnp.dot(left, right, precision=lax.Precision.HIGHEST, preferred_element_type=jnp.float32)

def layer_norm(values, gain, shift):
    centre = lax.optimization_barrier(jnp.mean(values, axis=-1, keepdims=True))
    centred = values - centre
    spread = lax.optimization_barrier(jnp.mean(centred * centred, axis=-1, keepdims=True))
    return centred * lax.rsqrt(spread + 1e-06) * gain + shift

def gelu_exact(values):
    return jax.nn.gelu(values, approximate=False)

def adapter(values, down, down_bias, up_proj, up_bias):
    inner = low_back(matmul(values, down) + down_bias)
    inner = low(gelu_exact(inner))
    return low_back(matmul(inner, up_proj) + up_bias)

def row_mask(lengths, counts):
    positions = jnp.arange(ROW_LEN, dtype=jnp.int32)[:, None]
    slot_ends = jnp.cumsum(lengths).astype(jnp.int32)[None, :]
    slot_starts = slot_ends - lengths[None, :]
    segment = lax.optimization_barrier(jnp.sum((positions >= slot_ends).astype(jnp.int32), axis=1))
    inside = (positions >= slot_starts) & (positions < slot_starts + counts[None, :])
    is_live = lax.optimization_barrier(jnp.sum(inside.astype(jnp.int32), axis=1)) > 0
    return (segment[:, None] == segment[None, :]) & is_live[None, :]

def layer_forward(tokens_f, trainable, frozen, allowed):
    w_query, w_key, w_value, w_out, w_inner, w_outer = frozen
    down_one, dbias_one, up_one, ubias_one, gain_one, shift_one, down_two, dbias_two, up_two, ubias_two, gain_two, shift_two = trainable
    length = tokens_f.shape[0]
    query = rounded_both(matmul(tokens_f, w_query) * 0.125).reshape(length, HEADS, HEAD)
    keys = rounded_both(matmul(tokens_f, w_key)).reshape(length, HEADS, HEAD)
    values = rounded_both(matmul(tokens_f, w_value)).reshape(length, HEADS, HEAD)
    scores = low_back(jnp.einsum('qhe,khe->hqk', query, keys, precision=lax.Precision.HIGHEST))
    scores = jnp.where(allowed[None], scores, -1e+30)
    weights = low(jax.nn.softmax(scores, axis=-1))
    attended = jnp.einsum('hqk,khe->qhe', weights, values, precision=lax.Precision.HIGHEST).reshape(length, D)
    attended = rounded_both(attended)
    branch = rounded_both(matmul(attended, w_out))
    summed = tokens_f + branch + adapter(branch, down_one, dbias_one, up_one, ubias_one)
    mid = low(layer_norm(summed, gain_one, shift_one))
    hidden = low(gelu_exact(low_back(matmul(mid, w_inner))))
    ffn = rounded_both(matmul(hidden, w_outer))
    second = mid + ffn + adapter(ffn, down_two, dbias_two, up_two, ubias_two)
    return layer_norm(second, gain_two, shift_two)

def reference(tokens, w_query, w_key, w_value, w_out, w_inner, w_outer, down_one, dbias_one, up_one, ubias_one, gain_one, shift_one, down_two, dbias_two, up_two, ubias_two, gain_two, shift_two, seg_len, seg_valid, cotangent):
    frozen = tuple((weight.astype(jnp.float32) for weight in (w_query, w_key, w_value, w_out, w_inner, w_outer)))
    trainable = tuple((element.astype(jnp.float32) for element in (down_one, dbias_one, up_one, ubias_one, gain_one, shift_one, down_two, dbias_two, up_two, ubias_two, gain_two, shift_two)))
    rows_in = jnp.transpose(tokens, (1, 0, 2)).astype(jnp.float32)
    rows_grad = jnp.transpose(cotangent, (1, 0, 2)).astype(jnp.float32)

    def one_row(grad_sums, row_items):
        row_tokens, row_cot, lengths, counts = row_items
        allowed = row_mask(lengths, counts)
        result, pull_back = jax.vjp(lambda row_given, row_params: layer_forward(row_given, row_params, frozen, allowed), row_tokens, trainable)
        grad_tokens, grad_params = pull_back(row_cot)
        grad_sums = jax.tree.map(lambda held_sum, extra_sum: held_sum + extra_sum, grad_sums, grad_params)
        return (grad_sums, (result.astype(jnp.bfloat16), grad_tokens.astype(jnp.bfloat16)))
    start_sums = jax.tree.map(jnp.zeros_like, trainable)
    grad_sums, (results, row_grads) = lax.scan(one_row, start_sums, (rows_in, rows_grad, seg_len, seg_valid))
    mixed = jnp.transpose(results, (1, 0, 2))
    input_grad = jnp.transpose(row_grads, (1, 0, 2))
    return (mixed, input_grad, grad_sums[0], grad_sums[1], grad_sums[2], grad_sums[3], grad_sums[4], grad_sums[5], grad_sums[6], grad_sums[7], grad_sums[8], grad_sums[9], grad_sums[10], grad_sums[11])
```

```python
import functools

import jax
import jax.numpy as jnp
from jax import lax
from jax.experimental import pallas as pl
from jax.experimental.pallas import tpu as pltpu
from jax.sharding import PartitionSpec as P

HEAD = 64
GROUP = 4
LONG_AT = 128
LONG = 512
ROWS_A = 64
ROWS_B = 128
NEG = -1e30
F32 = jnp.float32
BF16 = jnp.bfloat16

VMEM = pl.BlockSpec(memory_space=pltpu.VMEM)
SMEM = pl.BlockSpec(memory_space=pltpu.SMEM)
ANY = pl.BlockSpec(memory_space=pl.ANY)


def nn(left, right):
    return lax.dot_general(left, right, (((1,), (0,)), ((), ())), preferred_element_type=F32)


def nt(left, right):
    return lax.dot_general(left, right, (((1,), (1,)), ((), ())), preferred_element_type=F32)


def tn(left, right):
    return lax.dot_general(left, right, (((0,), (0,)), ((), ())), preferred_element_type=F32)


def gelu_both(values):
    size = jnp.abs(values) * 0.7071067811865476
    inv = 1.0 / (1.0 + 0.3275911 * size)
    bell = jnp.exp(-size * size)
    poly = inv * (
        0.254829592
        + inv * (-0.284496736 + inv * (1.421413741 + inv * (-1.453152027 + inv * 1.061405429)))
    )
    tail = 0.5 * poly * bell
    phi = jnp.where(values >= 0, 1.0 - tail, tail)
    return values * phi, phi + values * bell * 0.3989422804014327


def normed(values):
    centre = jnp.mean(values, axis=-1, keepdims=True)
    centred = values - centre
    spread = jnp.mean(centred * centred, axis=-1, keepdims=True)
    scale = lax.rsqrt(spread + 1e-06)
    return centred * scale, scale


def norm_back(incoming, gain, normal, scale):
    scaled = incoming * gain
    first = jnp.mean(scaled, axis=-1, keepdims=True)
    second = jnp.mean(scaled * normal, axis=-1, keepdims=True)
    return scale * (scaled - first - normal * second)


def row_of(ref):
    return ref[...].reshape(1, ref.shape[0])


def own_rows(block):
    return (
        pl.multiple_of(jnp.where(block == 0, 128, 0), 64),
        pl.multiple_of(jnp.where(block == 0, 0, 64), 64),
    )


def partner_offset(block):
    return pl.multiple_of(jnp.where(block == 0, 0, jnp.where(block == 3, 256, 128)), 128)


def bounds(len_ref, valid_ref, places):
    low = jnp.zeros(places.shape, jnp.int32)
    high = jnp.zeros(places.shape, jnp.int32)
    start = jnp.int32(0)
    for slot in range(len_ref.shape[1]):
        end = start + len_ref[0, slot]
        inside = (places >= start) & (places < end)
        low = jnp.where(inside, start, low)
        high = jnp.where(inside, start + valid_ref[0, slot], high)
        start = end
    return low, high


def bias_of(len_ref, valid_ref, query_at, key_at, rows):
    places = query_at + lax.broadcasted_iota(jnp.int32, (rows, 1), 0)
    low, high = bounds(len_ref, valid_ref, places)
    keys = key_at + lax.broadcasted_iota(jnp.int32, (rows, LONG), 1)
    return jnp.where((keys >= low) & (keys < high), 0.0, NEG)


def bias_back_of(len_ref, valid_ref, key_at, query_at, rows):
    places = query_at + lax.broadcasted_iota(jnp.int32, (1, LONG), 1)
    low, high = bounds(len_ref, valid_ref, places)
    keys = key_at + lax.broadcasted_iota(jnp.int32, (rows, LONG), 0)
    return jnp.where((keys >= low) & (keys < high), 0.0, NEG)


def spread_heads(part):
    lane = lax.broadcasted_iota(jnp.int32, part.shape, 1) // HEAD
    return jnp.concatenate(
        [jnp.where(lane == head, part, jnp.zeros_like(part)) for head in range(GROUP)], axis=0
    )


def join_heads(stacked):
    rows = stacked.shape[0] // GROUP
    lane = lax.broadcasted_iota(jnp.int32, (rows, stacked.shape[1]), 1) // HEAD
    out = stacked[:rows]
    for head in range(1, GROUP):
        out = jnp.where(lane == head, stacked[head * rows : (head + 1) * rows], out)
    return out


def four(array):
    return jnp.concatenate([array] * GROUP, axis=0)


def project_kernel(block_ref, own_ref, mate_ref, wq_ref, wk_ref, wv_ref, q_ref, k_ref, v_ref):
    core = block_ref[0] % 2
    rows = own_ref.shape[0]
    own = own_ref[...]
    mate = mate_ref[...]
    q_ref[...] = (nn(own, wq_ref[...]) * 0.125).astype(BF16)
    mine = pl.multiple_of(core * rows, rows)
    other = pl.multiple_of((1 - core) * rows, rows)
    both = jnp.concatenate([own, mate], axis=0)
    keys = nn(both, wk_ref[...]).astype(BF16)
    values = nn(both, wv_ref[...]).astype(BF16)
    k_ref[pl.ds(mine, rows), :] = keys[:rows]
    k_ref[pl.ds(other, rows), :] = keys[rows:]
    v_ref[pl.ds(mine, rows), :] = values[:rows]
    v_ref[pl.ds(other, rows), :] = values[rows:]


def main_kernel(
    block_ref,
    len_ref,
    valid_ref,
    own_ref,
    far_ref,
    far_mate_ref,
    q_ref,
    kpair_ref,
    vpair_ref,
    cot_ref,
    down1_ref,
    dbias1_ref,
    up1_ref,
    ubias1_ref,
    gain1_ref,
    shift1_ref,
    down2_ref,
    dbias2_ref,
    up2_ref,
    ubias2_ref,
    gain2_ref,
    shift2_ref,
    wk_hbm,
    wv_hbm,
    wout_hbm,
    winner_hbm,
    wouter_hbm,
    mixed_ref,
    kbuf,
    vbuf,
    lse_ref,
    du1_ref,
    pack_ref,
    keep_ref,
    send_ref,
    wk_ref,
    wv_ref,
    wout_ref,
    winner_ref,
    wouter_ref,
    slope_ref,
    sems,
):
    copies = []
    for index, (source, target) in enumerate(
        (
            (wk_hbm, wk_ref),
            (wv_hbm, wv_ref),
            (wout_hbm, wout_ref),
            (winner_hbm, winner_ref),
            (wouter_hbm, wouter_ref),
        )
    ):
        copy = pltpu.make_async_copy(source, target, sems.at[index])
        copy.start()
        copies.append(copy)
    block = block_ref[0]
    core = block % 2
    chip = block // 2
    rows, width = own_ref.shape
    at_a, at_b = own_rows(block)
    meet_b = partner_offset(block)
    first = block * rows

    def mine(ref):
        return jnp.concatenate([ref[pl.ds(at_a, ROWS_A), :], ref[pl.ds(at_b, ROWS_B), :]], axis=0)

    def put(ref, value):
        ref[pl.ds(at_a, ROWS_A), :] = value[:ROWS_A]
        ref[pl.ds(at_b, ROWS_B), :] = value[ROWS_A:]

    def natural(value):
        rolled = jnp.concatenate([value[:, ROWS_A:], value[:, :ROWS_A]], axis=1)
        return jnp.where(block == 0, rolled, value)

    near = pl.multiple_of(chip * 2 * rows, 2 * rows)
    kbuf[pl.ds(near, 2 * rows), :] = kpair_ref[...]
    vbuf[pl.ds(near, 2 * rows), :] = vpair_ref[...]
    far_first = pl.multiple_of((1 - chip) * 2 * rows + core * rows, rows)
    far_second = pl.multiple_of((1 - chip) * 2 * rows + (1 - core) * rows, rows)
    both = jnp.concatenate([far_ref[...], far_mate_ref[...]], axis=0)
    copies[0].wait()
    keys = nn(both, wk_ref[...]).astype(BF16)
    kbuf[pl.ds(far_first, rows), :] = keys[:rows]
    kbuf[pl.ds(far_second, rows), :] = keys[rows:]
    copies[1].wait()
    values = nn(both, wv_ref[...]).astype(BF16)
    vbuf[pl.ds(far_first, rows), :] = values[:rows]
    vbuf[pl.ds(far_second, rows), :] = values[rows:]

    bias_a = four(bias_of(len_ref, valid_ref, first + at_a, LONG_AT, ROWS_A))
    bias_b = four(bias_of(len_ref, valid_ref, first + at_b, meet_b, ROWS_B))
    lane = lax.broadcasted_iota(jnp.int32, (1, 128), 1)
    attended_parts = []
    lse_parts = []
    for at, count, meet, bias in (
        (at_a, ROWS_A, LONG_AT, bias_a),
        (at_b, ROWS_B, meet_b, bias_b),
    ):
        pieces = []
        lse = jnp.zeros((count, 128), F32)
        for group in range(width // (GROUP * HEAD)):
            columns = slice(group * GROUP * HEAD, (group + 1) * GROUP * HEAD)
            queries = spread_heads(q_ref[pl.ds(at, count), columns])
            scores = nt(queries, kbuf[pl.ds(meet, LONG), columns]) + bias
            top = jnp.max(scores, axis=-1, keepdims=True)
            weights = jnp.exp(scores - top)
            total = jnp.sum(weights, axis=-1, keepdims=True)
            mixed_values = nn(weights.astype(BF16), vbuf[pl.ds(meet, LONG), columns])
            pieces.append(join_heads(mixed_values * (1.0 / total)))
            log_total = top + jnp.log(total)
            for head in range(GROUP):
                lse = jnp.where(
                    lane == group * GROUP + head, log_total[head * count : (head + 1) * count], lse
                )
        attended_parts.append(jnp.concatenate(pieces, axis=1))
        lse_parts.append(lse)
    attended_f = jnp.concatenate(attended_parts, axis=0)
    lse_own = jnp.concatenate(lse_parts, axis=0)
    put(lse_ref, lse_own)
    attended = attended_f.astype(BF16)
    copies[2].wait()
    branch = nn(attended, wout_ref[...]).astype(BF16)

    pre1 = nt(branch, down1_ref[...]) + row_of(dbias1_ref)
    inner1_f, slope1 = gelu_both(pre1)
    inner1 = inner1_f.astype(BF16)
    summed = (
        mine(own_ref).astype(F32) + branch.astype(F32) + nn(inner1, up1_ref[...]) + row_of(ubias1_ref)
    )
    normal1, scale1 = normed(summed)
    gain1 = row_of(gain1_ref)
    mid = (normal1 * gain1 + row_of(shift1_ref)).astype(BF16)

    copies[3].wait()
    copies[4].wait()
    hidden_units = winner_ref.shape[1]
    chunk = 512
    ffn_f = jnp.zeros((rows, width), F32)
    for at in range(0, hidden_units, chunk):
        hidden_f, slope = gelu_both(nn(mid, winner_ref[:, at : at + chunk]))
        slope_ref[:, at : at + chunk] = slope
        ffn_f = ffn_f + nn(hidden_f.astype(BF16), wouter_ref[at : at + chunk, :])
    ffn = ffn_f.astype(BF16)

    pre2 = nt(ffn, down2_ref[...]) + row_of(dbias2_ref)
    inner2_f, slope2 = gelu_both(pre2)
    inner2 = inner2_f.astype(BF16)
    summed = mid.astype(F32) + ffn.astype(F32) + nn(inner2, up2_ref[...]) + row_of(ubias2_ref)
    normal2, scale2 = normed(summed)
    gain2 = row_of(gain2_ref)
    put(mixed_ref, (normal2 * gain2 + row_of(shift2_ref)).astype(BF16))

    cot = mine(cot_ref).astype(F32)
    grad_gain2 = jnp.sum(cot * normal2, axis=0, keepdims=True)
    grad_shift2 = jnp.sum(cot, axis=0, keepdims=True)
    du2 = norm_back(cot, gain2, normal2, scale2)

    def adapter_back(source, down, up, inner, slope, incoming):
        out_grad = incoming.astype(BF16)
        grad_up = tn(inner, out_grad)
        grad_ubias = jnp.sum(out_grad.astype(F32), axis=0, keepdims=True)
        grad_pre = (nt(out_grad, up) * slope).astype(BF16)
        grad_down = tn(grad_pre, source)
        grad_dbias = jnp.sum(grad_pre.astype(F32), axis=0, keepdims=True)
        return nn(grad_pre, down), grad_down, grad_dbias, grad_up, grad_ubias

    back2, grad_down2, grad_dbias2, grad_up2, grad_ubias2 = adapter_back(
        ffn, down2_ref[...], up2_ref[...], inner2, slope2, du2
    )
    dffn = (du2 + back2).astype(BF16)
    dmid = du2
    for at in range(0, hidden_units, chunk):
        dhidden = (nt(dffn, wouter_ref[at : at + chunk, :]) * slope_ref[:, at : at + chunk]).astype(
            BF16
        )
        dmid = dmid + nt(dhidden, winner_ref[:, at : at + chunk])

    grad_gain1 = jnp.sum(dmid * normal1, axis=0, keepdims=True)
    grad_shift1 = jnp.sum(dmid, axis=0, keepdims=True)
    du1 = norm_back(dmid, gain1, normal1, scale1)
    back1, grad_down1, grad_dbias1, grad_up1, grad_ubias1 = adapter_back(
        branch, down1_ref[...], up1_ref[...], inner1, slope1, du1
    )
    put(du1_ref, du1)

    blank = jnp.zeros((1, width), F32)
    both_dbias = jnp.concatenate(
        [grad_dbias1, grad_dbias2, jnp.zeros((1, width - 2 * grad_dbias1.shape[1]), F32)], axis=1
    )
    quarters = (
        (grad_up1, grad_ubias1, both_dbias),
        (grad_down1, grad_gain1, grad_shift1),
        (grad_up2, grad_ubias2, blank),
        (grad_down2, grad_gain2, grad_shift2),
    )
    for index, (matrix, one, two) in enumerate(quarters):
        small = jnp.concatenate([one, two, jnp.zeros((14, width), F32)], axis=0)
        whole = jnp.concatenate([matrix, small], axis=0).astype(BF16)
        place = jnp.where(chip == index // 2, 0, 1)

        @pl.when(core == index % 2)
        def _(place=place, whole=whole):
            keep_ref[place] = whole

        @pl.when(core != index % 2)
        def _(place=place, whole=whole):
            send_ref[place] = whole

    dbranch = (du1 + back1).astype(BF16)
    dattended = nt(dbranch, wout_ref[...]).astype(BF16)
    pack_ref[pl.ds(at_a, ROWS_A), :] = dattended[:ROWS_A]
    pack_ref[pl.ds(at_b, ROWS_B), :] = dattended[ROWS_A:]
    product = dattended.astype(F32) * attended_f
    product_hi = product.astype(BF16)
    product_lo = (product - product_hi.astype(F32)).astype(BF16)
    head_of = lax.broadcasted_iota(jnp.int32, (16, width), 1) // HEAD
    picks = (head_of == lax.broadcasted_iota(jnp.int32, (16, width), 0)).astype(BF16)
    delta = natural(nt(picks, product_hi) + nt(picks, product_lo))
    lse_rows = natural(
        jnp.transpose(jnp.concatenate([lse_own, jnp.zeros((256 - rows, 128), F32)], axis=0))[
            :16, :rows
        ]
    )

    def pieces_of(value, count):
        out = []
        for _ in range(count):
            piece = value.astype(BF16)
            value = value - piece.astype(F32)
            out.append(jnp.concatenate([piece, jnp.zeros((16, 256 - rows), BF16)], axis=1))
        return out

    pack_ref[rows : rows + 16, :] = jnp.concatenate(pieces_of(lse_rows, 3), axis=1)
    pack_ref[rows + 16 : rows + 32, :] = jnp.concatenate(
        pieces_of(delta, 2) + [jnp.zeros((16, 256), BF16)], axis=1
    )


def query_back_kernel(
    block_ref,
    len_ref,
    valid_ref,
    own_ref,
    mate_ref,
    far_ref,
    far_mate_ref,
    q_ref,
    kbuf,
    vbuf,
    lse_ref,
    pack_ref,
    du1_ref,
    wq_ref,
    qbuf,
    part_ref,
):
    block = block_ref[0]
    rows, width = own_ref.shape
    at_a, at_b = own_rows(block)
    meet_b = partner_offset(block)
    first = block * rows
    wq = wq_ref[...]
    tokens = jnp.concatenate(
        [mate_ref[...], far_ref[...], far_mate_ref[...]], axis=0
    )
    queries_all = (nn(tokens, wq) * 0.125).astype(BF16)
    qbuf[pl.ds(pl.multiple_of(block * rows, rows), rows), :] = q_ref[...]
    for index in range(3):
        spot = pl.multiple_of((block ^ (index + 1)) * rows, rows)
        qbuf[pl.ds(spot, rows), :] = queries_all[index * rows : (index + 1) * rows]
    bias_a = four(bias_of(len_ref, valid_ref, first + at_a, LONG_AT, ROWS_A))
    bias_b = four(bias_of(len_ref, valid_ref, first + at_b, meet_b, ROWS_B))
    lane = lax.broadcasted_iota(jnp.int32, (1, 128), 1)
    for at, count, meet, bias in (
        (at_a, ROWS_A, LONG_AT, bias_a),
        (at_b, ROWS_B, meet_b, bias_b),
    ):
        pieces = []
        lse = lse_ref[pl.ds(at, count), :]
        for group in range(width // (GROUP * HEAD)):
            columns = slice(group * GROUP * HEAD, (group + 1) * GROUP * HEAD)
            log_total = jnp.concatenate(
                [
                    jnp.sum(
                        jnp.where(lane == group * GROUP + head, lse, 0.0), axis=-1, keepdims=True
                    )
                    for head in range(GROUP)
                ],
                axis=0,
            )
            keys = kbuf[pl.ds(meet, LONG), columns]
            scores = nt(spread_heads(q_ref[pl.ds(at, count), columns]), keys) + bias
            probs = jnp.exp(scores - log_total)
            dprobs = nt(
                spread_heads(pack_ref[pl.ds(at, count), columns]), vbuf[pl.ds(meet, LONG), columns]
            )
            delta = jnp.sum(probs * dprobs, axis=-1, keepdims=True)
            dscores = (probs * (dprobs - delta)).astype(BF16)
            pieces.append(join_heads(nn(dscores, keys)))
        dquery = jnp.concatenate(pieces, axis=1).astype(BF16)
        part_ref[pl.ds(at, count), :] = du1_ref[pl.ds(at, count), :] + nt(dquery, wq) * 0.125


def key_back_kernel(
    block_ref,
    len_ref,
    valid_ref,
    own_ref,
    mate_ref,
    far_ref,
    far_mate_ref,
    qbuf,
    kbuf,
    vbuf,
    part_ref,
    wk_ref,
    wv_ref,
    out_ref,
    abuf,
    lse_ref,
    delta_ref,
):
    block = block_ref[0]
    rows, width = out_ref.shape
    at_a, at_b = own_rows(block)
    meet_b = partner_offset(block)
    first = block * rows
    for index, ref in enumerate((own_ref, mate_ref, far_ref, far_mate_ref)):
        source = block ^ index
        abuf[pl.ds(pl.multiple_of(source * rows, rows), rows), :] = ref[:rows, :]
        lse = ref[rows : rows + 16, :].astype(F32)
        delta = ref[rows + 16 : rows + 32, :].astype(F32)
        lse_ref[source] = lse[:, :256] + (lse[:, 256:512] + lse[:, 512:])
        delta_ref[source] = delta[:, :256] + delta[:, 256:512]
    lse_all = jnp.concatenate([lse_ref[index][:, :rows] for index in range(4)], axis=1)
    delta_all = jnp.concatenate([delta_ref[index][:, :rows] for index in range(4)], axis=1)
    bias_a = four(bias_back_of(len_ref, valid_ref, first + at_a, LONG_AT, ROWS_A))
    bias_b = four(bias_back_of(len_ref, valid_ref, first + at_b, meet_b, ROWS_B))

    def window(stat, meet):
        if isinstance(meet, int):
            return stat[:, meet : meet + LONG]
        out = stat[:, :LONG]
        for start in (128, 256):
            out = jnp.where(meet == start, stat[:, start : start + LONG], out)
        return out

    for at, count, meet, bias in (
        (at_a, ROWS_A, LONG_AT, bias_a),
        (at_b, ROWS_B, meet_b, bias_b),
    ):
        lse_here = window(lse_all, meet)
        delta_here = window(delta_all, meet)
        dkeys = []
        dvalues = []
        for group in range(width // (GROUP * HEAD)):
            columns = slice(group * GROUP * HEAD, (group + 1) * GROUP * HEAD)

            def per_head(stat):
                return jnp.concatenate(
                    [
                        jnp.broadcast_to(
                            stat[group * GROUP + head : group * GROUP + head + 1], (count, LONG)
                        )
                        for head in range(GROUP)
                    ],
                    axis=0,
                )

            queries = qbuf[pl.ds(meet, LONG), columns]
            grads = abuf[pl.ds(meet, LONG), columns]
            own_at = pl.multiple_of(first + at, 64)
            scores = nt(spread_heads(kbuf[pl.ds(own_at, count), columns]), queries) + bias
            probs = jnp.exp(scores - per_head(lse_here))
            dprobs = nt(spread_heads(vbuf[pl.ds(own_at, count), columns]), grads)
            dscores = (probs * (dprobs - per_head(delta_here))).astype(BF16)
            dkeys.append(join_heads(nn(dscores, queries)))
            dvalues.append(join_heads(nn(probs.astype(BF16), grads)))
        dkey = jnp.concatenate(dkeys, axis=1).astype(BF16)
        dvalue = jnp.concatenate(dvalues, axis=1).astype(BF16)
        out_ref[pl.ds(at, count), :] = (
            part_ref[pl.ds(at, count), :] + nt(dkey, wk_ref[...]) + nt(dvalue, wv_ref[...])
        ).astype(BF16)


def params(megabytes):
    return pltpu.CompilerParams(vmem_limit_bytes=megabytes << 20)


def cost(gigaflop, megabytes):
    return pl.CostEstimate(
        flops=int(gigaflop * 1e9), bytes_accessed=int(megabytes * 1e6), transcendentals=0
    )


def shape(dims, dtype):
    return jax.ShapeDtypeStruct(dims, dtype)


def body(
    dp_size,
    tokens,
    w_query,
    w_key,
    w_value,
    w_out,
    w_inner,
    w_outer,
    down_one,
    dbias_one,
    up_one,
    ubias_one,
    gain_one,
    shift_one,
    down_two,
    dbias_two,
    up_two,
    ubias_two,
    gain_two,
    shift_two,
    seg_len,
    seg_valid,
    cotangent,
):
    rows, _, width = tokens.shape
    adapt = up_one.shape[0]
    hidden = w_inner.shape[1]
    block = lax.axis_index("blk")
    core, chip = block % 2, block // 2
    block_arr = block.reshape(1).astype(jnp.int32)
    own = tokens.reshape(rows, width)
    cot = cotangent.reshape(rows, width)

    def swap(array, mask):
        return lax.ppermute(array, "blk", [(i, i ^ mask) for i in range(4)])

    def swap_all(array, mask):
        return lax.ppermute(
            array, ("dp", "blk"), [(i, i ^ mask) for i in range(4 * dp_size)]
        )

    far = swap(own, 2)
    mate = swap(own, 1)
    far_mate = swap(far, 1)

    q, kpair, vpair = pl.pallas_call(
        project_kernel,
        in_specs=[SMEM] + [VMEM] * 5,
        out_specs=[VMEM] * 3,
        out_shape=[shape((rows, width), BF16)] + [shape((2 * rows, width), BF16)] * 2,
        compiler_params=params(24),
        cost_estimate=cost(1.2, 5.0),
        name="project",
    )(block_arr, own, mate, w_query, w_key, w_value)

    pack_rows = rows + 32
    part_rows = adapt + 16
    mixed, kbuf, vbuf, lse, du1, pack, keep, send = pl.pallas_call(
        main_kernel,
        in_specs=[SMEM] * 3 + [VMEM] * 19 + [ANY] * 5,
        out_specs=[VMEM] * 8,
        out_shape=[
            shape((rows, width), BF16),
            shape((4 * rows, width), BF16),
            shape((4 * rows, width), BF16),
            shape((rows, 128), F32),
            shape((rows, width), F32),
            shape((pack_rows, width), BF16),
            shape((2, part_rows, width), BF16),
            shape((2, part_rows, width), BF16),
        ],
        scratch_shapes=[
            pltpu.VMEM((width, width), BF16),
            pltpu.VMEM((width, width), BF16),
            pltpu.VMEM((width, width), BF16),
            pltpu.VMEM((width, hidden), BF16),
            pltpu.VMEM((hidden, width), BF16),
            pltpu.VMEM((rows, hidden), F32),
            pltpu.SemaphoreType.DMA((5,)),
        ],
        compiler_params=params(48),
        cost_estimate=cost(8.0, 20.0),
        name="layer",
    )(
        block_arr,
        seg_len,
        seg_valid,
        own,
        far,
        far_mate,
        q,
        kpair,
        vpair,
        cot,
        down_one.T,
        dbias_one,
        up_one,
        ubias_one,
        gain_one,
        shift_one,
        down_two.T,
        dbias_two,
        up_two,
        ubias_two,
        gain_two,
        shift_two,
        w_key,
        w_value,
        w_out,
        w_inner,
        w_outer,
    )

    pack_far = swap(pack, 2)
    pack_mate = swap(pack, 1)
    pack_far_mate = swap(pack_far, 1)

    def add(left, right):
        return (left.astype(F32) + right.astype(F32)).astype(BF16)

    total = add(keep, swap_all(send, 1))
    total = add(total[0], swap_all(total[1], 2))
    mask = 4
    while mask < 4 * dp_size:
        total = add(total, swap_all(total, mask))
        mask *= 2
    half = jnp.stack([total, swap_all(total, 2)])
    other_half = swap_all(half, 1)

    qbuf, part = pl.pallas_call(
        query_back_kernel,
        in_specs=[SMEM] * 3 + [VMEM] * 11,
        out_specs=[VMEM] * 2,
        out_shape=[shape((4 * rows, width), BF16), shape((rows, width), F32)],
        compiler_params=params(40),
        cost_estimate=cost(2.0, 6.0),
        name="query_back",
    )(
        block_arr,
        seg_len,
        seg_valid,
        own,
        mate,
        far,
        far_mate,
        q,
        kbuf,
        vbuf,
        lse,
        pack,
        du1,
        w_query,
    )
    input_grad = pl.pallas_call(
        key_back_kernel,
        in_specs=[SMEM] * 3 + [VMEM] * 10,
        out_specs=VMEM,
        out_shape=shape((rows, width), BF16),
        scratch_shapes=[
            pltpu.VMEM((4 * rows, width), BF16),
            pltpu.VMEM((4, 16, 256), F32),
            pltpu.VMEM((4, 16, 256), F32),
        ],
        compiler_params=params(40),
        cost_estimate=cost(2.5, 6.0),
        name="key_back",
    )(
        block_arr,
        seg_len,
        seg_valid,
        pack,
        pack_mate,
        pack_far,
        pack_far_mate,
        qbuf,
        kbuf,
        vbuf,
        part,
        w_key,
        w_value,
    )

    def quarter(index):
        same = jnp.where(chip == index // 2, half[0], half[1])
        flipped = jnp.where(chip == index // 2, other_half[0], other_half[1])
        return jnp.where(core == index % 2, same, flipped).astype(F32)

    up1, down1, up2, down2 = (quarter(index) for index in range(4))
    return (
        mixed.reshape(tokens.shape),
        input_grad.reshape(tokens.shape),
        down1[:adapt].T,
        up1[adapt + 1, :adapt],
        up1[:adapt],
        up1[adapt],
        down1[adapt],
        down1[adapt + 1],
        down2[:adapt].T,
        up1[adapt + 1, adapt : 2 * adapt],
        up2[:adapt],
        up2[adapt],
        down2[adapt],
        down2[adapt + 1],
    )


def solution(mesh):
    in_specs = (
        (P("blk", "dp", None),) + (P(),) * 18 + (P("dp", None),) * 2 + (P("blk", "dp", None),)
    )
    out_specs = (P("blk", "dp", None),) * 2 + (P(),) * 12
    return jax.shard_map(
        functools.partial(body, mesh.shape["dp"]),
        mesh=mesh,
        in_specs=in_specs,
        out_specs=out_specs,
        check_vma=False,
    )
```

```python
import functools

import jax
import jax.numpy as jnp
from jax import lax
from jax.experimental import pallas as pl
from jax.experimental.pallas import tpu as pltpu
from jax.sharding import PartitionSpec as P

HEAD = 64
GROUP = 4
LONG_AT = 128
LONG = 512
ROWS_A = 64
SHARE = 128
CHUNK = 512
SMALL = 8
ROWS_B = 128
NEG = -1e30
F32 = jnp.float32
BF16 = jnp.bfloat16

VMEM = pl.BlockSpec(memory_space=pltpu.VMEM)
SMEM = pl.BlockSpec(memory_space=pltpu.SMEM)
HBM = pl.BlockSpec(memory_space=pltpu.HBM)


def nn(left, right):
    return lax.dot_general(left, right, (((1,), (0,)), ((), ())), preferred_element_type=F32)


def nt(left, right):
    return lax.dot_general(left, right, (((1,), (1,)), ((), ())), preferred_element_type=F32)


def tn(left, right):
    return lax.dot_general(left, right, (((0,), (0,)), ((), ())), preferred_element_type=F32)


def gelu_both(values):
    size = jnp.abs(values) * 0.7071067811865476
    inv = 1.0 / (1.0 + 0.3275911 * size)
    bell = jnp.exp(-size * size)
    poly = inv * (
        0.254829592
        + inv * (-0.284496736 + inv * (1.421413741 + inv * (-1.453152027 + inv * 1.061405429)))
    )
    tail = 0.5 * poly * bell
    phi = jnp.where(values >= 0, 1.0 - tail, tail)
    return values * phi, phi + values * bell * 0.3989422804014327


def normed(values):
    centre = jnp.mean(values, axis=-1, keepdims=True)
    centred = values - centre
    spread = jnp.mean(centred * centred, axis=-1, keepdims=True)
    scale = lax.rsqrt(spread + 1e-06)
    return centred * scale, scale


def norm_back(incoming, gain, normal, scale):
    scaled = incoming * gain
    first = jnp.mean(scaled, axis=-1, keepdims=True)
    second = jnp.mean(scaled * normal, axis=-1, keepdims=True)
    return scale * (scaled - first - normal * second)


def row_of(ref):
    return ref[...].reshape(1, ref.shape[0])


def own_rows(block):
    return (
        pl.multiple_of(jnp.where(block == 0, 128, 0), 64),
        pl.multiple_of(jnp.where(block == 0, 0, 64), 64),
    )


def far_place(chip):
    return pl.multiple_of(LONG_AT + 2 * SHARE * (1 - chip), 128)


def far_tokens(core, far_ref, far_mate_ref):
    far, far_mate = far_ref[...], far_mate_ref[...]
    first = core == 0
    return jnp.concatenate(
        [jnp.where(first, far, far_mate), jnp.where(first, far_mate, far)], axis=0
    )


def partner_offset(block):
    return pl.multiple_of(jnp.where(block == 0, 0, jnp.where(block == 3, 256, 128)), 128)


def bounds(len_ref, valid_ref, places):
    low = jnp.zeros(places.shape, jnp.int32)
    high = jnp.zeros(places.shape, jnp.int32)
    start = jnp.int32(0)
    for slot in range(len_ref.shape[1]):
        end = start + len_ref[0, slot]
        inside = (places >= start) & (places < end)
        low = jnp.where(inside, start, low)
        high = jnp.where(inside, start + valid_ref[0, slot], high)
        start = end
    return low, high


def bias_of(len_ref, valid_ref, query_at, key_at, rows):
    places = query_at + lax.broadcasted_iota(jnp.int32, (rows, 1), 0)
    low, high = bounds(len_ref, valid_ref, places)
    keys = key_at + lax.broadcasted_iota(jnp.int32, (rows, LONG), 1)
    return jnp.where((keys >= low) & (keys < high), 0.0, NEG)


def bias_back_of(len_ref, valid_ref, key_at, query_at, rows):
    places = query_at + lax.broadcasted_iota(jnp.int32, (1, LONG), 1)
    low, high = bounds(len_ref, valid_ref, places)
    keys = key_at + lax.broadcasted_iota(jnp.int32, (rows, LONG), 0)
    return jnp.where((keys >= low) & (keys < high), 0.0, NEG)


def spread_heads(part):
    lane = lax.broadcasted_iota(jnp.int32, part.shape, 1) // HEAD
    return jnp.concatenate(
        [jnp.where(lane == head, part, jnp.zeros_like(part)) for head in range(GROUP)], axis=0
    )


def join_heads(stacked):
    rows = stacked.shape[0] // GROUP
    lane = lax.broadcasted_iota(jnp.int32, (rows, stacked.shape[1]), 1) // HEAD
    out = stacked[:rows]
    for head in range(1, GROUP):
        out = jnp.where(lane == head, stacked[head * rows : (head + 1) * rows], out)
    return out


def masked(scores, bias):
    split = scores.reshape((GROUP,) + bias.shape)
    return (split + bias).reshape(scores.shape)


def less_rows(stacked, rows):
    count = stacked.shape[0] // GROUP
    return jnp.concatenate(
        [stacked[head * count : (head + 1) * count] - rows[head : head + 1] for head in range(GROUP)],
        axis=0,
    )


def project_kernel(
    len_ref,
    valid_ref,
    own_hbm,
    mate_ref,
    wq_hbm,
    wk_hbm,
    wv_hbm,
    wout_hbm,
    winner_hbm,
    q_ref,
    k_ref,
    v_ref,
    bias_a_ref,
    bias_b_ref,
    back_a_ref,
    back_b_ref,
    wq_ref,
    wk_ref,
    wv_ref,
    wout_ref,
    winner_ref,
    own_ref,
    sems,
):
    moves = (
        (own_hbm, own_ref),
        (wq_hbm, wq_ref),
        (wk_hbm, wk_ref),
        (wv_hbm, wv_ref),
        (wout_hbm, wout_ref),
        (winner_hbm, winner_ref),
    )
    copies = [
        pltpu.make_async_copy(source, target, sems.at[index])
        for index, (source, target) in enumerate(moves)
    ]
    for copy in copies:
        copy.start()
    block = lax.axis_index("blk")
    core = block % 2
    rows = own_ref.shape[0]
    first = block * rows
    at_a, at_b = own_rows(block)
    meet_b = partner_offset(block)
    bias_a_ref[...] = bias_of(len_ref, valid_ref, first + at_a, LONG_AT, ROWS_A)
    bias_b_ref[...] = bias_of(len_ref, valid_ref, first + at_b, meet_b, ROWS_B)
    back_a_ref[...] = bias_back_of(len_ref, valid_ref, first + at_a, LONG_AT, ROWS_A)
    back_b_ref[...] = bias_back_of(len_ref, valid_ref, first + at_b, meet_b, ROWS_B)
    mine = pl.multiple_of(core * rows, rows)
    other = pl.multiple_of((1 - core) * rows, rows)
    copies[0].wait()
    both = jnp.concatenate([own_ref[...], mate_ref[...]], axis=0)
    for copy, weight, out, scale in (
        (copies[1], wq_ref, q_ref, 0.125),
        (copies[2], wk_ref, k_ref, 1.0),
        (copies[3], wv_ref, v_ref, 1.0),
    ):
        copy.wait()
        product = (nn(both, weight[...]) * scale).astype(BF16)
        out[pl.ds(mine, rows), :] = product[:rows]
        out[pl.ds(other, rows), :] = product[rows:]
    copies[4].wait()
    copies[5].wait()


def main_kernel(
    own_ref,
    far_ref,
    far_mate_ref,
    q_ref,
    kpair_ref,
    vpair_ref,
    bias_a_ref,
    bias_b_ref,
    cot_ref,
    down1_ref,
    dbias1_ref,
    up1_ref,
    ubias1_ref,
    gain1_ref,
    shift1_ref,
    down2_ref,
    dbias2_ref,
    up2_ref,
    ubias2_ref,
    gain2_ref,
    shift2_ref,
    wk_ref,
    wv_ref,
    wout_ref,
    winner_ref,
    wouter_hbm,
    mixed_hbm,
    kbuf,
    vbuf,
    lse_ref,
    du1_ref,
    pack_ref,
    keep_ref,
    send_ref,
    wouter_ref,
    slope_ref,
    mixed_ref,
    sems,
):
    hidden_units = winner_ref.shape[1]
    outer_copies = []
    for index in range(hidden_units // CHUNK):
        part = pl.ds(index * CHUNK, CHUNK)
        copy = pltpu.make_async_copy(wouter_hbm.at[part], wouter_ref.at[part], sems.at[1 + index])
        copy.start()
        outer_copies.append(copy)
    mixed_copy = pltpu.make_async_copy(mixed_ref, mixed_hbm, sems.at[0])
    block = lax.axis_index("blk")
    core = block % 2
    chip = block // 2
    rows, width = own_ref.shape
    at_a, at_b = own_rows(block)
    meet_b = partner_offset(block)

    def mine(ref):
        return jnp.concatenate([ref[pl.ds(at_a, ROWS_A), :], ref[pl.ds(at_b, ROWS_B), :]], axis=0)

    def put(ref, value):
        ref[pl.ds(at_a, ROWS_A), :] = value[:ROWS_A]
        ref[pl.ds(at_b, ROWS_B), :] = value[ROWS_A:]

    def natural(value):
        rolled = jnp.concatenate([value[:, ROWS_A:], value[:, :ROWS_A]], axis=1)
        return jnp.where(block == 0, rolled, value)

    near = pl.multiple_of(chip * 2 * rows, 2 * rows)
    kbuf[pl.ds(near, 2 * rows), :] = kpair_ref[...]
    vbuf[pl.ds(near, 2 * rows), :] = vpair_ref[...]
    far = far_tokens(core, far_ref, far_mate_ref)
    kbuf[pl.ds(far_place(chip), 2 * SHARE), :] = nn(far, wk_ref[...]).astype(BF16)
    vbuf[pl.ds(far_place(chip), 2 * SHARE), :] = nn(far, wv_ref[...]).astype(BF16)

    lane = lax.broadcasted_iota(jnp.int32, (1, 128), 1)
    attended_parts = []
    lse_parts = []
    for at, count, meet, bias_ref in (
        (at_a, ROWS_A, LONG_AT, bias_a_ref),
        (at_b, ROWS_B, meet_b, bias_b_ref),
    ):
        pieces = []
        lse = jnp.zeros((count, 128), F32)
        for group in range(width // (GROUP * HEAD)):
            columns = slice(group * GROUP * HEAD, (group + 1) * GROUP * HEAD)
            queries = spread_heads(q_ref[pl.ds(core * rows + at, count), columns])
            scores = masked(nt(queries, kbuf[pl.ds(meet, LONG), columns]), bias_ref[...])
            top = jnp.max(scores, axis=-1, keepdims=True)
            weights = jnp.exp(scores - top)
            total = jnp.sum(weights, axis=-1, keepdims=True)
            mixed_values = nn(weights.astype(BF16), vbuf[pl.ds(meet, LONG), columns])
            pieces.append(join_heads(mixed_values * (1.0 / total)))
            log_total = top + jnp.log(total)
            for head in range(GROUP):
                lse = jnp.where(
                    lane == group * GROUP + head, log_total[head * count : (head + 1) * count], lse
                )
        attended_parts.append(jnp.concatenate(pieces, axis=1))
        lse_parts.append(lse)
    attended_f = jnp.concatenate(attended_parts, axis=0)
    lse_own = jnp.concatenate(lse_parts, axis=0)
    put(lse_ref, lse_own)
    attended = attended_f.astype(BF16)
    branch = nn(attended, wout_ref[...]).astype(BF16)

    pre1 = nt(branch, down1_ref[...]) + row_of(dbias1_ref)
    inner1_f, slope1 = gelu_both(pre1)
    inner1 = inner1_f.astype(BF16)
    summed = (
        mine(own_ref).astype(F32) + branch.astype(F32) + nn(inner1, up1_ref[...]) + row_of(ubias1_ref)
    )
    normal1, scale1 = normed(summed)
    gain1 = row_of(gain1_ref)
    mid = (normal1 * gain1 + row_of(shift1_ref)).astype(BF16)

    ffn_f = jnp.zeros((rows, width), F32)
    for at in range(0, hidden_units, CHUNK):
        hidden_f, slope = gelu_both(nn(mid, winner_ref[:, at : at + CHUNK]))
        slope_ref[:, at : at + CHUNK] = slope
        outer_copies[at // CHUNK].wait()
        ffn_f = ffn_f + nn(hidden_f.astype(BF16), wouter_ref[at : at + CHUNK, :])
    ffn = ffn_f.astype(BF16)

    pre2 = nt(ffn, down2_ref[...]) + row_of(dbias2_ref)
    inner2_f, slope2 = gelu_both(pre2)
    inner2 = inner2_f.astype(BF16)
    summed = mid.astype(F32) + ffn.astype(F32) + nn(inner2, up2_ref[...]) + row_of(ubias2_ref)
    normal2, scale2 = normed(summed)
    gain2 = row_of(gain2_ref)
    put(mixed_ref, (normal2 * gain2 + row_of(shift2_ref)).astype(BF16))
    mixed_copy.start()

    cot = mine(cot_ref).astype(F32)
    grad_gain2 = jnp.sum(cot * normal2, axis=0, keepdims=True)
    grad_shift2 = jnp.sum(cot, axis=0, keepdims=True)
    du2 = norm_back(cot, gain2, normal2, scale2)

    def adapter_back(source, down, up, inner, slope, incoming):
        out_grad = incoming.astype(BF16)
        grad_up = tn(inner, out_grad)
        grad_ubias = jnp.sum(out_grad.astype(F32), axis=0, keepdims=True)
        grad_pre = (nt(out_grad, up) * slope).astype(BF16)
        grad_down = tn(grad_pre, source)
        grad_dbias = jnp.sum(grad_pre.astype(F32), axis=0, keepdims=True)
        return nn(grad_pre, down), grad_down, grad_dbias, grad_up, grad_ubias

    back2, grad_down2, grad_dbias2, grad_up2, grad_ubias2 = adapter_back(
        ffn, down2_ref[...], up2_ref[...], inner2, slope2, du2
    )
    dffn = (du2 + back2).astype(BF16)
    dmid = du2
    for at in range(0, hidden_units, CHUNK):
        dhidden = (nt(dffn, wouter_ref[at : at + CHUNK, :]) * slope_ref[:, at : at + CHUNK]).astype(
            BF16
        )
        dmid = dmid + nt(dhidden, winner_ref[:, at : at + CHUNK])

    grad_gain1 = jnp.sum(dmid * normal1, axis=0, keepdims=True)
    grad_shift1 = jnp.sum(dmid, axis=0, keepdims=True)
    du1 = norm_back(dmid, gain1, normal1, scale1)
    back1, grad_down1, grad_dbias1, grad_up1, grad_ubias1 = adapter_back(
        branch, down1_ref[...], up1_ref[...], inner1, slope1, du1
    )
    put(du1_ref, du1)

    blank = jnp.zeros((1, width), F32)
    both_dbias = jnp.concatenate(
        [
            grad_dbias1,
            jnp.zeros((1, 128 - grad_dbias1.shape[1]), F32),
            grad_dbias2,
            jnp.zeros((1, width - 128 - grad_dbias2.shape[1]), F32),
        ],
        axis=1,
    )
    quarters = (
        (grad_up1, grad_ubias1, both_dbias),
        (grad_down1, grad_gain1, grad_shift1),
        (grad_up2, grad_ubias2, blank),
        (grad_down2, grad_gain2, grad_shift2),
    )
    for index, (matrix, one, two) in enumerate(quarters):
        small = jnp.concatenate([one, two, jnp.zeros((SMALL - 2, width), F32)], axis=0)
        whole = jnp.concatenate([matrix, small], axis=0).astype(BF16)
        place = jnp.where(chip == index // 2, 0, 1)

        @pl.when(core == index % 2)
        def _(place=place, whole=whole):
            keep_ref[place] = whole

        @pl.when(core != index % 2)
        def _(place=place, whole=whole):
            send_ref[place] = whole

    dbranch = (du1 + back1).astype(BF16)
    dattended = nt(dbranch, wout_ref[...]).astype(BF16)
    put(pack_ref, dattended)
    product = dattended.astype(F32) * attended_f
    product_hi = product.astype(BF16)
    product_lo = (product - product_hi.astype(F32)).astype(BF16)
    head_of = lax.broadcasted_iota(jnp.int32, (16, width), 1) // HEAD
    picks = (head_of == lax.broadcasted_iota(jnp.int32, (16, width), 0)).astype(BF16)
    delta = natural(nt(picks, product_hi) + nt(picks, product_lo))
    lse_rows = natural(
        jnp.transpose(jnp.concatenate([lse_own, jnp.zeros((256 - rows, 128), F32)], axis=0))[
            :16, :rows
        ]
    )

    def pieces_of(value, count):
        out = []
        for _ in range(count):
            piece = value.astype(BF16)
            value = value - piece.astype(F32)
            out.append(jnp.concatenate([piece, jnp.zeros((16, 256 - rows), BF16)], axis=1))
        return out

    pack_ref[rows : rows + 16, :] = jnp.concatenate(pieces_of(lse_rows, 3), axis=1)
    pack_ref[rows + 16 : rows + 32, :] = jnp.concatenate(
        pieces_of(delta, 2) + [jnp.zeros((16, 256), BF16)], axis=1
    )
    mixed_copy.wait()


def query_back_kernel(
    group,
    far_ref,
    far_mate_ref,
    q_ref,
    kbuf,
    vbuf,
    bias_a_ref,
    bias_b_ref,
    lse_ref,
    pack_ref,
    part_in_ref,
    wq_ref,
    qbuf,
    part_ref,
):
    block = lax.axis_index("blk")
    rows = q_ref.shape[0] // 2
    core, chip = block % 2, block // 2
    at_a, at_b = own_rows(block)
    meet_b = partner_offset(block)
    columns = slice(group * GROUP * HEAD, (group + 1) * GROUP * HEAD)
    wq = wq_ref[:, columns]
    queries_far = (nn(far_tokens(core, far_ref, far_mate_ref), wq) * 0.125).astype(BF16)
    qbuf[pl.ds(pl.multiple_of(chip * 2 * rows, rows), 2 * rows), :] = q_ref[:, columns]
    qbuf[pl.ds(far_place(chip), 2 * SHARE), :] = queries_far
    lane = lax.broadcasted_iota(jnp.int32, (1, 128), 1)
    for at, count, meet, bias_ref in (
        (at_a, ROWS_A, LONG_AT, bias_a_ref),
        (at_b, ROWS_B, meet_b, bias_b_ref),
    ):
        lse = lse_ref[pl.ds(at, count), :]
        log_total = jnp.concatenate(
            [
                jnp.sum(jnp.where(lane == group * GROUP + head, lse, 0.0), axis=-1, keepdims=True)
                for head in range(GROUP)
            ],
            axis=0,
        )
        keys = kbuf[pl.ds(meet, LONG), columns]
        scores = nt(spread_heads(q_ref[pl.ds(core * rows + at, count), columns]), keys)
        scores = masked(scores, bias_ref[...])
        probs = jnp.exp(scores - log_total)
        dprobs = nt(
            spread_heads(pack_ref[pl.ds(at, count), columns]), vbuf[pl.ds(meet, LONG), columns]
        )
        delta = jnp.sum(probs * dprobs, axis=-1, keepdims=True)
        dscores = (probs * (dprobs - delta)).astype(BF16)
        dquery = join_heads(nn(dscores, keys)).astype(BF16)
        part_ref[pl.ds(at, count), :] = part_in_ref[pl.ds(at, count), :] + nt(dquery, wq) * 0.125


def key_back_kernel(
    group,
    own_ref,
    mate_ref,
    far_ref,
    far_mate_ref,
    qbuf,
    kbuf,
    vbuf,
    back_a_ref,
    back_b_ref,
    part_ref,
    wk_ref,
    wv_ref,
    out_ref,
    abuf,
):
    block = lax.axis_index("blk")
    rows, width = out_ref.shape
    core, chip = block % 2, block // 2
    at_a, at_b = own_rows(block)
    meet_b = partner_offset(block)
    first = block * rows
    columns = slice(group * GROUP * HEAD, (group + 1) * GROUP * HEAD)
    abuf[pl.ds(pl.multiple_of(first, rows), rows), :] = own_ref[:rows, columns]
    abuf[pl.ds(pl.multiple_of((block ^ 1) * rows, rows), rows), :] = mate_ref[:rows, columns]
    far_at = far_place(chip)
    far_first = pl.multiple_of(far_at + SHARE * core, 128)
    far_second = pl.multiple_of(far_at + SHARE * (1 - core), 128)
    abuf[pl.ds(far_first, SHARE), :] = far_ref[:SHARE, columns]
    abuf[pl.ds(far_second, SHARE), :] = far_mate_ref[:SHARE, columns]
    stats = []
    for ref, at in ((own_ref, rows), (mate_ref, rows), (far_ref, SHARE), (far_mate_ref, SHARE)):
        lse = ref[at : at + 16, :].astype(F32)
        delta = ref[at + 16 : at + 32, :].astype(F32)
        stats.append(
            (
                (lse[:, :256] + (lse[:, 256:512] + lse[:, 512:]))[:, :rows],
                (delta[:, :256] + delta[:, 256:512])[:, :rows],
            )
        )

    def in_order(which):
        ordered = []
        for place in range(4):
            pick = stats[place][which]
            for index in range(4):
                pick = jnp.where(block ^ index == place, stats[index][which], pick)
            ordered.append(pick)
        return jnp.concatenate(ordered, axis=1)

    lse_all, delta_all = in_order(0), in_order(1)

    def window(stat, meet):
        stat = stat[group * GROUP : (group + 1) * GROUP]
        if isinstance(meet, int):
            return stat[:, meet : meet + LONG]
        here = stat[:, :LONG]
        for start in (128, 256):
            here = jnp.where(meet == start, stat[:, start : start + LONG], here)
        return here

    for at, count, meet, bias_ref in (
        (at_a, ROWS_A, LONG_AT, back_a_ref),
        (at_b, ROWS_B, meet_b, back_b_ref),
    ):
        queries = qbuf[pl.ds(meet, LONG), :]
        grads = abuf[pl.ds(meet, LONG), :]
        own_at = pl.multiple_of(first + at, 64)
        scores = nt(spread_heads(kbuf[pl.ds(own_at, count), columns]), queries)
        scores = masked(scores, bias_ref[...])
        probs = jnp.exp(less_rows(scores, window(lse_all, meet)))
        dprobs = nt(spread_heads(vbuf[pl.ds(own_at, count), columns]), grads)
        dscores = (probs * less_rows(dprobs, window(delta_all, meet))).astype(BF16)
        dkey = join_heads(nn(dscores, queries)).astype(BF16)
        dvalue = join_heads(nn(probs.astype(BF16), grads)).astype(BF16)
        out_ref[pl.ds(at, count), :] = (
            part_ref[pl.ds(at, count), :]
            + nt(dkey, wk_ref[:, columns])
            + nt(dvalue, wv_ref[:, columns])
        ).astype(out_ref.dtype)


def unpack_kernel(*refs):
    parts, outs = refs[:4], refs[4:]
    block = lax.axis_index("blk")
    core, chip = block % 2, block // 2
    adapt = outs[0].shape[0]
    matrices = (outs[2], outs[0], outs[8], outs[6])
    vectors = ((outs[3], None), (outs[4], outs[5]), (outs[9], None), (outs[10], outs[11]))
    for index in range(4):
        place = (core ^ (index % 2)) + 2 * (chip ^ (index // 2))
        for at, part in enumerate(parts):

            @pl.when(place == at)
            def _(index=index, part=part):
                matrices[index][...] = part[:adapt, :].astype(F32)
                small = part[adapt : adapt + SMALL, :].astype(F32)
                one, two = vectors[index]
                one[...] = small[0]
                if two is not None:
                    two[...] = small[1]
                if index == 0:
                    outs[1][...] = small[1, :adapt]
                    outs[7][...] = small[1, 128 : 128 + adapt]


def params(megabytes):
    return pltpu.CompilerParams(vmem_limit_bytes=megabytes << 20)


def cost(gigaflop, megabytes):
    return pl.CostEstimate(
        flops=int(gigaflop * 1e9), bytes_accessed=int(megabytes * 1e6), transcendentals=0
    )


def after(array, *others):
    return lax.optimization_barrier((array,) + others)[0]


def vmem(dims, dtype):
    return pltpu.VMEM(dims, dtype)


def in_hbm(array):
    return pltpu.with_memory_space_constraint(array, pltpu.HBM)


def shape(dims, dtype):
    return jax.ShapeDtypeStruct(dims, dtype)


def body(
    dp_size,
    tokens,
    w_query,
    w_key,
    w_value,
    w_out,
    w_inner,
    w_outer,
    down_one,
    dbias_one,
    up_one,
    ubias_one,
    gain_one,
    shift_one,
    down_two,
    dbias_two,
    up_two,
    ubias_two,
    gain_two,
    shift_two,
    seg_len,
    seg_valid,
    cotangent,
):
    rows, _, width = tokens.shape
    adapt = up_one.shape[0]
    hidden = w_inner.shape[1]
    block = lax.axis_index("blk")
    own = tokens.reshape(rows, width)
    cot = cotangent.reshape(rows, width)

    def swap(array, mask):
        return lax.ppermute(array, "blk", [(i, i ^ mask) for i in range(4)])

    def swap_all(array, mask):
        return lax.ppermute(
            array, ("dp", "blk"), [(i, i ^ mask) for i in range(4 * dp_size)]
        )

    mate = swap(own, 1)
    def near_share(own, mate):
        choices = (
            (own[128:192], own[64:128], own[:64], mate[128:192]),
            (mate[:64], own[128:192], own[64:128], own[:64]),
        )
        halves = []
        for options in choices:
            half = options[0]
            for index in range(1, 4):
                half = jnp.where(block == index, options[index], half)
            halves.append(half)
        return halves

    far = swap(jnp.concatenate(near_share(own, mate), axis=0), 2)
    mask_shapes = [vmem((count, LONG), F32) for count in (ROWS_A, ROWS_B)] * 2
    (
        q,
        kpair,
        vpair,
        bias_a,
        bias_b,
        back_a,
        back_b,
        wq_here,
        wk_here,
        wv_here,
        wout_here,
        winner_here,
    ) = pl.pallas_call(
        project_kernel,
        in_specs=[SMEM] * 2 + [HBM, VMEM] + [HBM] * 5,
        out_specs=[VMEM] * 12,
        out_shape=[vmem((2 * rows, width), BF16)] * 3
        + mask_shapes
        + [vmem((width, width), BF16)] * 4
        + [vmem((width, hidden), BF16)],
        scratch_shapes=[pltpu.VMEM((rows, width), BF16), pltpu.SemaphoreType.DMA((6,))],
        compiler_params=params(4),
        cost_estimate=cost(2.0, 12.0),
        name="project",
    )(
        in_hbm(seg_len),
        in_hbm(seg_valid),
        in_hbm(own),
        mate,
        in_hbm(w_query),
        in_hbm(w_key),
        in_hbm(w_value),
        in_hbm(w_out),
        in_hbm(w_inner),
    )
    far_mate = swap(after(far, q), 1)

    part_rows = adapt + SMALL
    mixed, kbuf, vbuf, lse, du1, pack, keep, send = pl.pallas_call(
        main_kernel,
        in_specs=[VMEM] * 25 + [HBM],
        out_specs=[HBM] + [VMEM] * 7,
        out_shape=[
            shape((rows, width), BF16),
            vmem((4 * rows, width), BF16),
            vmem((4 * rows, width), BF16),
            vmem((rows, 128), F32),
            vmem((rows, width), F32),
            vmem((rows + 32, width), BF16),
            vmem((2, part_rows, width), BF16),
            vmem((2, part_rows, width), BF16),
        ],
        scratch_shapes=[
            pltpu.VMEM((hidden, width), BF16),
            pltpu.VMEM((rows, hidden), F32),
            pltpu.VMEM((rows, width), BF16),
            pltpu.SemaphoreType.DMA((1 + hidden // CHUNK,)),
        ],
        compiler_params=params(13),
        cost_estimate=cost(8.0, 20.0),
        name="layer",
    )(
        own,
        far,
        far_mate,
        q,
        kpair,
        vpair,
        bias_a,
        bias_b,
        cot,
        down_one.T,
        dbias_one,
        up_one,
        ubias_one,
        gain_one,
        shift_one,
        down_two.T,
        dbias_two,
        up_two,
        ubias_two,
        gain_two,
        shift_two,
        wk_here,
        wv_here,
        wout_here,
        winner_here,
        in_hbm(w_outer),
    )

    def add(left, right):
        return (left.astype(F32) + right.astype(F32)).astype(BF16)

    def query_back(group, part, pack_now):
        return pl.pallas_call(
            functools.partial(query_back_kernel, group),
            in_specs=[VMEM] * 11,
            out_specs=[VMEM] * 2,
            out_shape=[vmem((4 * rows, GROUP * HEAD), BF16), vmem((rows, width), F32)],
            compiler_params=params(4),
            cost_estimate=cost(1.0, 3.0),
            name=f"query_back_{group}",
        )(far, far_mate, q, kbuf, vbuf, bias_a, bias_b, lse, pack_now, part, wq_here)

    def key_back(group, qbuf, part):
        return pl.pallas_call(
            functools.partial(key_back_kernel, group),
            in_specs=[VMEM] * 12,
            out_specs=VMEM,
            out_shape=vmem((rows, width), F32) if group < 2 else shape((rows, width), BF16),
            scratch_shapes=[pltpu.VMEM((4 * rows, GROUP * HEAD), BF16)],
            compiler_params=params(4),
            cost_estimate=cost(1.0, 3.0),
            name=f"key_back_{group}",
        )(
            pack,
            pack_mate,
            pack_far,
            pack_far_mate,
            qbuf,
            kbuf,
            vbuf,
            back_a,
            back_b,
            part,
            wk_here,
            wv_here,
        )

    pack_mate = swap(pack, 1)
    total = add(keep, swap_all(send, 1))
    pack_now, pack_mate, total = lax.optimization_barrier((pack, pack_mate, total))
    share = near_share(pack_now, pack_mate) + [pack_now[rows:]]
    pack_far = swap(jnp.concatenate(share, axis=0), 2)
    arrived = swap_all(total[1], 2)
    qbuf0, part = query_back(0, du1, pack_now)
    total = add(total[0], after(arrived, part))
    arrived = swap_all(total, 4)
    qbuf1, part = query_back(1, after(part, total), pack_now)
    pack_far, part = lax.optimization_barrier((pack_far, part))
    pack_far_mate = swap(pack_far, 1)
    total = add(total, after(arrived, part))
    masks = []
    while 8 << len(masks) < 4 * dp_size:
        masks.append(8 << len(masks))
    arrived = swap_all(total, masks[0])
    qbuf2, part = query_back(2, after(part, total), pack_now)
    total = add(total, after(arrived, part))
    arrived = swap_all(total, masks[1])
    part = key_back(0, qbuf0, after(part, total))
    part = key_back(1, qbuf1, part)
    total = add(total, after(arrived, part))
    for mask in masks[2:]:
        total = add(total, swap_all(total, mask))
    across = swap_all(total, 2)
    input_grad = key_back(2, qbuf2, after(part, total))
    other_half = swap_all(after(jnp.stack([total, across]), input_grad), 1)

    grads = pl.pallas_call(
        unpack_kernel,
        in_specs=[VMEM] * 4,
        out_specs=[VMEM] * 12,
        out_shape=[
            shape(dims, F32)
            for dims in (
                ((adapt, width), (adapt,), (adapt, width), (width,), (width,), (width,)) * 2
            )
        ],
        compiler_params=params(4),
        name="unpack",
    )(total, other_half[0], across, other_half[1])
    return (mixed.reshape(tokens.shape), input_grad.reshape(tokens.shape)) + tuple(
        grad.T if index in (0, 6) else grad for index, grad in enumerate(grads)
    )


def solution(mesh):
    in_specs = (
        (P("blk", "dp", None),) + (P(),) * 18 + (P("dp", None),) * 2 + (P("blk", "dp", None),)
    )
    out_specs = (P("blk", "dp", None),) * 2 + (P(),) * 12
    return jax.shard_map(
        functools.partial(body, mesh.shape["dp"]),
        mesh=mesh,
        in_specs=in_specs,
        out_specs=out_specs,
        check_vma=False,
    )
```

```python
import functools

import jax
import jax.numpy as jnp
from jax import lax
from jax.experimental import pallas as pl
from jax.experimental.pallas import tpu as pltpu
from jax.sharding import PartitionSpec as P

HEAD = 64
GROUP = 4
LONG_AT = 128
LONG = 512
ROWS_A = 64
WIDE = GROUP * HEAD
SHARE = 128
CHUNK = 768
SMALL = 8
ROWS_B = 128
NEG = -1e30
F32 = jnp.float32
BF16 = jnp.bfloat16

VMEM = pl.BlockSpec(memory_space=pltpu.VMEM)
SMEM = pl.BlockSpec(memory_space=pltpu.SMEM)
HBM = pl.BlockSpec(memory_space=pltpu.HBM)


def nn(left, right):
    return lax.dot_general(left, right, (((1,), (0,)), ((), ())), preferred_element_type=F32)


def nt(left, right):
    return lax.dot_general(left, right, (((1,), (1,)), ((), ())), preferred_element_type=F32)


def tn(left, right):
    return lax.dot_general(left, right, (((0,), (0,)), ((), ())), preferred_element_type=F32)


def gelu_both(values):
    phi = 0.5 + 0.5 * lax.erf(values * 0.7071067811865476)
    bell = jnp.exp(-0.5 * values * values)
    return values * phi, phi + values * bell * 0.3989422804014327


def normed(values):
    centre = jnp.mean(values, axis=-1, keepdims=True)
    centred = values - centre
    spread = jnp.mean(centred * centred, axis=-1, keepdims=True)
    scale = lax.rsqrt(spread + 1e-06)
    return centred * scale, scale


def norm_back(incoming, gain, normal, scale):
    scaled = incoming * gain
    first = jnp.mean(scaled, axis=-1, keepdims=True)
    second = jnp.mean(scaled * normal, axis=-1, keepdims=True)
    return scale * (scaled - first - normal * second)


def row_of(ref):
    return ref[...].reshape(1, ref.shape[0])


def own_rows(block):
    return (
        pl.multiple_of(jnp.where(block == 0, 128, 0), 64),
        pl.multiple_of(jnp.where(block == 0, 0, 64), 64),
    )


def far_place(chip):
    return pl.multiple_of(LONG_AT + 2 * SHARE * (1 - chip), 128)


def far_tokens(core, far_ref, far_mate_ref):
    far, far_mate = far_ref[...], far_mate_ref[...]
    first = core == 0
    return jnp.concatenate(
        [jnp.where(first, far, far_mate), jnp.where(first, far_mate, far)], axis=0
    )


def partner_offset(block):
    return pl.multiple_of(jnp.where(block == 0, 0, jnp.where(block == 3, 256, 128)), 128)


def bounds(len_ref, valid_ref, places):
    low = jnp.zeros(places.shape, jnp.int32)
    high = jnp.zeros(places.shape, jnp.int32)
    start = jnp.int32(0)
    for slot in range(len_ref.shape[1]):
        end = start + len_ref[0, slot]
        inside = (places >= start) & (places < end)
        low = jnp.where(inside, start, low)
        high = jnp.where(inside, start + valid_ref[0, slot], high)
        start = end
    return low, high


def bias_of(len_ref, valid_ref, query_at, key_at, rows):
    places = query_at + lax.broadcasted_iota(jnp.int32, (rows, 1), 0)
    low, high = bounds(len_ref, valid_ref, places)
    keys = key_at + lax.broadcasted_iota(jnp.int32, (rows, LONG), 1)
    return jnp.where((keys >= low) & (keys < high), 0.0, NEG)


def bias_back_of(len_ref, valid_ref, key_at, query_at, rows):
    places = query_at + lax.broadcasted_iota(jnp.int32, (1, LONG), 1)
    low, high = bounds(len_ref, valid_ref, places)
    keys = key_at + lax.broadcasted_iota(jnp.int32, (rows, LONG), 0)
    return jnp.where((keys >= low) & (keys < high), 0.0, NEG)


def spread_heads(part):
    lane = lax.broadcasted_iota(jnp.int32, part.shape, 1) // HEAD
    return jnp.concatenate(
        [jnp.where(lane == head, part, jnp.zeros_like(part)) for head in range(GROUP)], axis=0
    )


def join_heads(stacked):
    rows = stacked.shape[0] // GROUP
    lane = lax.broadcasted_iota(jnp.int32, (rows, stacked.shape[1]), 1) // HEAD
    out = stacked[:rows]
    for head in range(1, GROUP):
        out = jnp.where(lane == head, stacked[head * rows : (head + 1) * rows], out)
    return out


def masked(scores, bias):
    split = scores.reshape((GROUP,) + bias.shape)
    return (split + bias).reshape(scores.shape)


def less_rows(stacked, rows):
    count = stacked.shape[0] // GROUP
    return jnp.concatenate(
        [stacked[head * count : (head + 1) * count] - rows[head : head + 1] for head in range(GROUP)],
        axis=0,
    )


def project_kernel(
    len_ref,
    valid_ref,
    own_hbm,
    mate_ref,
    wq_hbm,
    wk_hbm,
    wv_hbm,
    wout_hbm,
    winner_hbm,
    q_ref,
    k_ref,
    v_ref,
    bias_a_ref,
    bias_b_ref,
    back_a_ref,
    back_b_ref,
    wq_ref,
    wk_ref,
    wv_ref,
    wout_ref,
    winner_ref,
    own_ref,
    sems,
):
    moves = (
        (own_hbm, own_ref),
        (wq_hbm, wq_ref),
        (wk_hbm, wk_ref),
        (wv_hbm, wv_ref),
        (wout_hbm, wout_ref),
        (winner_hbm, winner_ref),
    )
    copies = [
        pltpu.make_async_copy(source, target, sems.at[index])
        for index, (source, target) in enumerate(moves)
    ]
    block = lax.axis_index("blk")

    @pl.when(block < 4)
    def _():
        for copy in copies:
            copy.start()

    core = block % 2
    rows = own_ref.shape[0]
    first = block * rows
    at_a, at_b = own_rows(block)
    meet_b = partner_offset(block)
    bias_a_ref[...] = bias_of(len_ref, valid_ref, first + at_a, LONG_AT, ROWS_A)
    bias_b_ref[...] = bias_of(len_ref, valid_ref, first + at_b, meet_b, ROWS_B)
    back_a_ref[...] = bias_back_of(len_ref, valid_ref, first + at_a, LONG_AT, ROWS_A)
    back_b_ref[...] = bias_back_of(len_ref, valid_ref, first + at_b, meet_b, ROWS_B)
    mine = pl.multiple_of(core * rows, rows)
    other = pl.multiple_of((1 - core) * rows, rows)
    copies[0].wait()
    both = jnp.concatenate([own_ref[...], mate_ref[...]], axis=0)
    for copy, weight, out, scale in (
        (copies[1], wq_ref, q_ref, 0.125),
        (copies[2], wk_ref, k_ref, 1.0),
        (copies[3], wv_ref, v_ref, 1.0),
    ):
        copy.wait()
        product = (nn(both, weight[...]) * scale).astype(BF16)
        out[pl.ds(mine, rows), :] = product[:rows]
        out[pl.ds(other, rows), :] = product[rows:]
    copies[4].wait()
    copies[5].wait()


def main_kernel(
    own_ref,
    far_ref,
    far_mate_ref,
    q_ref,
    kpair_ref,
    vpair_ref,
    bias_a_ref,
    bias_b_ref,
    cot_ref,
    down1_ref,
    dbias1_ref,
    up1_ref,
    ubias1_ref,
    gain1_ref,
    shift1_ref,
    down2_ref,
    dbias2_ref,
    up2_ref,
    ubias2_ref,
    gain2_ref,
    shift2_ref,
    wk_ref,
    wv_ref,
    wout_ref,
    winner_ref,
    wouter_hbm,
    mixed_hbm,
    kbuf,
    vbuf,
    lse_ref,
    du1_ref,
    attended_ref,
    dbranch_ref,
    keep_ref,
    send_ref,
    wouter_ref,
    wouter_t_ref,
    winner_t_ref,
    slope_ref,
    mixed_ref,
    sems,
):
    hidden_units = winner_ref.shape[1]

    def outer_copy(index):
        part = pl.ds(pl.multiple_of(index * CHUNK, CHUNK), CHUNK)
        return pltpu.make_async_copy(wouter_hbm.at[part], wouter_ref.at[part], sems.at[1 + index])

    @pl.loop(0, hidden_units // CHUNK)
    def _(index):
        outer_copy(index).start()

    mixed_copy = pltpu.make_async_copy(mixed_ref, mixed_hbm, sems.at[0])
    block = lax.axis_index("blk")
    core = block % 2
    chip = block // 2
    rows, width = own_ref.shape
    at_a, at_b = own_rows(block)
    meet_b = partner_offset(block)

    def mine(ref):
        return jnp.concatenate([ref[pl.ds(at_a, ROWS_A), :], ref[pl.ds(at_b, ROWS_B), :]], axis=0)

    def put(ref, value):
        ref[pl.ds(at_a, ROWS_A), :] = value[:ROWS_A]
        ref[pl.ds(at_b, ROWS_B), :] = value[ROWS_A:]

    near = pl.multiple_of(chip * 2 * rows, 2 * rows)
    kbuf[pl.ds(near, 2 * rows), :] = kpair_ref[...]
    vbuf[pl.ds(near, 2 * rows), :] = vpair_ref[...]
    far = far_tokens(core, far_ref, far_mate_ref)
    kbuf[pl.ds(far_place(chip), 2 * SHARE), :] = nn(far, wk_ref[...]).astype(BF16)
    vbuf[pl.ds(far_place(chip), 2 * SHARE), :] = nn(far, wv_ref[...]).astype(BF16)

    lane = lax.broadcasted_iota(jnp.int32, (1, 128), 1)
    attended_parts = []
    lse_parts = []
    for at, count, meet, bias_ref in (
        (at_a, ROWS_A, LONG_AT, bias_a_ref),
        (at_b, ROWS_B, meet_b, bias_b_ref),
    ):
        pieces = []
        lse = jnp.zeros((count, 128), F32)
        for group in range(width // (GROUP * HEAD)):
            columns = slice(group * GROUP * HEAD, (group + 1) * GROUP * HEAD)
            queries = spread_heads(q_ref[pl.ds(core * rows + at, count), columns])
            scores = masked(nt(queries, kbuf[pl.ds(meet, LONG), columns]), bias_ref[...])
            top = jnp.max(scores, axis=-1, keepdims=True)
            weights = jnp.exp(scores - top)
            total = jnp.sum(weights, axis=-1, keepdims=True)
            mixed_values = nn(weights.astype(BF16), vbuf[pl.ds(meet, LONG), columns])
            pieces.append(join_heads(mixed_values * (1.0 / total)))
            log_total = top + jnp.log(total)
            for head in range(GROUP):
                lse = jnp.where(
                    lane == group * GROUP + head, log_total[head * count : (head + 1) * count], lse
                )
        attended_parts.append(jnp.concatenate(pieces, axis=1))
        lse_parts.append(lse)
    attended_f = jnp.concatenate(attended_parts, axis=0)
    put(lse_ref, jnp.concatenate(lse_parts, axis=0))
    put(attended_ref, attended_f)
    attended = attended_f.astype(BF16)
    branch = nn(attended, wout_ref[...]).astype(BF16)

    pre1 = nt(branch, down1_ref[...]) + row_of(dbias1_ref)
    inner1_f, slope1 = gelu_both(pre1)
    inner1 = inner1_f.astype(BF16)
    summed = (
        mine(own_ref).astype(F32) + branch.astype(F32) + nn(inner1, up1_ref[...]) + row_of(ubias1_ref)
    )
    normal1, scale1 = normed(summed)
    gain1 = row_of(gain1_ref)
    mid = (normal1 * gain1 + row_of(shift1_ref)).astype(BF16)

    for index in range(hidden_units // CHUNK):
        outer_copy(index).wait()
    ffn_f = jnp.zeros((rows, width), F32)
    for at in range(0, hidden_units, CHUNK):
        hidden_f, slope = gelu_both(nn(mid, winner_ref[:, at : at + CHUNK]))
        slope_ref[:, at : at + CHUNK] = slope
        wouter_t_ref[:, at : at + CHUNK] = wouter_ref[at : at + CHUNK, :].T
        winner_t_ref[at : at + CHUNK, :] = winner_ref[:, at : at + CHUNK].T
        ffn_f = ffn_f + nn(hidden_f.astype(BF16), wouter_ref[at : at + CHUNK, :])
    ffn = ffn_f.astype(BF16)

    pre2 = nt(ffn, down2_ref[...]) + row_of(dbias2_ref)
    inner2_f, slope2 = gelu_both(pre2)
    inner2 = inner2_f.astype(BF16)
    summed = mid.astype(F32) + ffn.astype(F32) + nn(inner2, up2_ref[...]) + row_of(ubias2_ref)
    normal2, scale2 = normed(summed)
    gain2 = row_of(gain2_ref)
    put(mixed_ref, (normal2 * gain2 + row_of(shift2_ref)).astype(BF16))
    mixed_copy.start()

    cot = mine(cot_ref).astype(F32)
    grad_gain2 = jnp.sum(cot * normal2, axis=0, keepdims=True)
    grad_shift2 = jnp.sum(cot, axis=0, keepdims=True)
    du2 = norm_back(cot, gain2, normal2, scale2)

    def adapter_back(source, down, up, inner, slope, incoming):
        out_grad = incoming.astype(BF16)
        grad_up = tn(inner, out_grad)
        grad_ubias = jnp.sum(out_grad.astype(F32), axis=0, keepdims=True)
        grad_pre = (nt(out_grad, up) * slope).astype(BF16)
        grad_down = tn(grad_pre, source)
        grad_dbias = jnp.sum(grad_pre.astype(F32), axis=0, keepdims=True)
        return nn(grad_pre, down), grad_down, grad_dbias, grad_up, grad_ubias

    back2, grad_down2, grad_dbias2, grad_up2, grad_ubias2 = adapter_back(
        ffn, down2_ref[...], up2_ref[...], inner2, slope2, du2
    )
    dffn = (du2 + back2).astype(BF16)
    dmid = du2
    for at in range(0, hidden_units, CHUNK):
        dhidden = (nn(dffn, wouter_t_ref[:, at : at + CHUNK]) * slope_ref[:, at : at + CHUNK]).astype(
            BF16
        )
        dmid = dmid + nn(dhidden, winner_t_ref[at : at + CHUNK, :])

    grad_gain1 = jnp.sum(dmid * normal1, axis=0, keepdims=True)
    grad_shift1 = jnp.sum(dmid, axis=0, keepdims=True)
    du1 = norm_back(dmid, gain1, normal1, scale1)
    back1, grad_down1, grad_dbias1, grad_up1, grad_ubias1 = adapter_back(
        branch, down1_ref[...], up1_ref[...], inner1, slope1, du1
    )
    put(du1_ref, du1)

    blank = jnp.zeros((1, width), F32)
    both_dbias = jnp.concatenate(
        [
            grad_dbias1,
            jnp.zeros((1, 128 - grad_dbias1.shape[1]), F32),
            grad_dbias2,
            jnp.zeros((1, width - 128 - grad_dbias2.shape[1]), F32),
        ],
        axis=1,
    )
    quarters = (
        (grad_up1, grad_ubias1, both_dbias),
        (grad_down1, grad_gain1, grad_shift1),
        (grad_up2, grad_ubias2, blank),
        (grad_down2, grad_gain2, grad_shift2),
    )
    for index, (matrix, one, two) in enumerate(quarters):
        small = jnp.concatenate([one, two, jnp.zeros((SMALL - 2, width), F32)], axis=0)
        whole = jnp.concatenate([matrix, small], axis=0).astype(BF16)
        for side in range(2):
            half = whole[:, side * width // 2 : (side + 1) * width // 2]
            place = 2 * (chip ^ (index // 2)) + (lax.axis_index("dp") % 2 ^ side)

            @pl.when(core == index % 2)
            def _(place=place, half=half):
                keep_ref[place] = half

            @pl.when(core != index % 2)
            def _(place=place, half=half):
                send_ref[place] = half

    put(dbranch_ref, (du1 + back1).astype(BF16))
    mixed_copy.wait()


def attended_back_kernel(dbranch_ref, attended_ref, lse_ref, wout_ref, pack_ref, delta_ref):
    rows, width = dbranch_ref.shape
    dattended = nt(dbranch_ref[...], wout_ref[...]).astype(BF16)
    pack_ref[:rows, :] = dattended
    product = dattended.astype(F32) * attended_ref[...]
    product_hi = product.astype(BF16)
    product_lo = (product - product_hi.astype(F32)).astype(BF16)
    head_of = lax.broadcasted_iota(jnp.int32, (128, width), 1) // HEAD
    picks = (head_of == lax.broadcasted_iota(jnp.int32, (128, width), 0)).astype(BF16)
    delta = nt(product_hi, picks) + nt(product_lo, picks)
    delta_ref[...] = delta
    blank = jnp.zeros((256 - rows, 128), F32)
    delta_rows = jnp.transpose(jnp.concatenate([delta, blank], axis=0))[:16]
    lse_rows = jnp.transpose(jnp.concatenate([lse_ref[...], blank], axis=0))[:16]

    def pieces_of(value, count):
        out = []
        for _ in range(count):
            piece = value.astype(BF16)
            value = value - piece.astype(F32)
            out.append(piece)
        return out

    pack_ref[rows : rows + 16, :] = jnp.concatenate(pieces_of(lse_rows, 3), axis=1)
    pack_ref[rows + 16 : rows + 32, :] = jnp.concatenate(
        pieces_of(delta_rows, 2) + [jnp.zeros((16, 256), BF16)], axis=1
    )


def query_back_kernel(
    groups,
    far_ref,
    far_mate_ref,
    q_ref,
    kbuf,
    vbuf,
    bias_a_ref,
    bias_b_ref,
    lse_ref,
    delta_ref,
    pack_ref,
    part_in_ref,
    wq_ref,
    *outs,
):
    block = lax.axis_index("blk")
    rows = q_ref.shape[0] // 2
    core, chip = block % 2, block // 2
    at_a, at_b = own_rows(block)
    meet_b = partner_offset(block)
    all_columns = slice(groups[0] * WIDE, (groups[-1] + 1) * WIDE)
    wq = wq_ref[:, all_columns]
    queries_far = (nn(far_tokens(core, far_ref, far_mate_ref), wq) * 0.125).astype(BF16)
    part_ref = outs[-1]
    for index, (group, qbuf) in enumerate(zip(groups, outs)):
        near = pl.ds(pl.multiple_of(chip * 2 * rows, rows), 2 * rows)
        qbuf[near, :] = q_ref[:, group * WIDE : (group + 1) * WIDE]
        qbuf[pl.ds(far_place(chip), 2 * SHARE), :] = queries_far[
            :, index * WIDE : (index + 1) * WIDE
        ]
    for at, count, meet, bias_ref in (
        (at_a, ROWS_A, LONG_AT, bias_a_ref),
        (at_b, ROWS_B, meet_b, bias_b_ref),
    ):
        lse = lse_ref[pl.ds(at, count), :]
        delta = delta_ref[pl.ds(at, count), :]
        pieces = []
        for group in groups:
            columns = slice(group * WIDE, (group + 1) * WIDE)
            heads = range(group * GROUP, (group + 1) * GROUP)
            log_total = jnp.concatenate([lse[:, head : head + 1] for head in heads], axis=0)
            deltas = jnp.concatenate([delta[:, head : head + 1] for head in heads], axis=0)
            keys = kbuf[pl.ds(meet, LONG), columns]
            scores = nt(spread_heads(q_ref[pl.ds(core * rows + at, count), columns]), keys)
            scores = masked(scores, bias_ref[...])
            probs = jnp.exp(scores - log_total)
            dprobs = nt(
                spread_heads(pack_ref[pl.ds(at, count), columns]), vbuf[pl.ds(meet, LONG), columns]
            )
            dscores = (probs * (dprobs - deltas)).astype(BF16)
            pieces.append(join_heads(nn(dscores, keys)).astype(BF16))
        dquery = jnp.concatenate(pieces, axis=1)
        part_ref[pl.ds(at, count), :] = part_in_ref[pl.ds(at, count), :] + nt(dquery, wq) * 0.125


def gather_kernel(own_ref, mate_ref, far_ref, far_mate_ref, grads_ref, stats_ref):
    block = lax.axis_index("blk")
    rows = own_ref.shape[0] - 32
    core, chip = block % 2, block // 2
    meet_b = partner_offset(block)
    grads_ref[pl.ds(pl.multiple_of(block * rows, rows), rows), :] = own_ref[:rows, :]
    grads_ref[pl.ds(pl.multiple_of((block ^ 1) * rows, rows), rows), :] = mate_ref[:rows, :]
    far_at = far_place(chip)
    far_first = pl.multiple_of(far_at + SHARE * core, 128)
    far_second = pl.multiple_of(far_at + SHARE * (1 - core), 128)
    grads_ref[pl.ds(far_first, SHARE), :] = far_ref[:SHARE, :]
    grads_ref[pl.ds(far_second, SHARE), :] = far_mate_ref[:SHARE, :]
    stats = []
    for ref, at in ((own_ref, rows), (mate_ref, rows), (far_ref, SHARE), (far_mate_ref, SHARE)):
        lse = ref[at : at + 16, :].astype(F32)
        delta = ref[at + 16 : at + 32, :].astype(F32)
        stats.append(
            jnp.concatenate(
                [
                    lse[:, :256] + (lse[:, 256:512] + lse[:, 512:]),
                    delta[:, :256] + delta[:, 256:512],
                ],
                axis=0,
            )[:, :rows]
        )
    ordered = []
    for place in range(4):
        pick = stats[place]
        for index in range(4):
            if index != place:
                pick = jnp.where(block ^ index == place, stats[index], pick)
        ordered.append(pick)
    whole = jnp.concatenate(ordered, axis=1)
    stats_ref[:32, :] = whole[:, LONG_AT : LONG_AT + LONG]
    here = whole[:, :LONG]
    for start in (128, 256):
        here = jnp.where(meet_b == start, whole[:, start : start + LONG], here)
    stats_ref[32:, :] = here


def key_back_kernel(groups, grads_ref, stats_ref, kbuf, vbuf, back_a_ref, back_b_ref, part_ref, *refs):
    qbufs, (wk_ref, wv_ref, out_ref) = refs[:-3], refs[-3:]
    block = lax.axis_index("blk")
    rows = out_ref.shape[0]
    at_a, at_b = own_rows(block)
    first = block * rows
    all_columns = slice(groups[0] * WIDE, (groups[-1] + 1) * WIDE)
    for at, count, meet, bias_ref, at_stats in (
        (at_a, ROWS_A, LONG_AT, back_a_ref, 0),
        (at_b, ROWS_B, partner_offset(block), back_b_ref, 32),
    ):
        own_at = pl.multiple_of(first + at, 64)
        dkeys, dvalues = [], []
        for group, qbuf in zip(groups, qbufs):
            columns = slice(group * WIDE, (group + 1) * WIDE)
            at_lse = at_stats + group * GROUP
            at_delta = at_lse + 16
            queries = qbuf[pl.ds(meet, LONG), :]
            grads = grads_ref[pl.ds(meet, LONG), columns]
            scores = nt(spread_heads(kbuf[pl.ds(own_at, count), columns]), queries)
            scores = masked(scores, bias_ref[...])
            probs = jnp.exp(less_rows(scores, stats_ref[at_lse : at_lse + GROUP, :]))
            dprobs = nt(spread_heads(vbuf[pl.ds(own_at, count), columns]), grads)
            dprobs = less_rows(dprobs, stats_ref[at_delta : at_delta + GROUP, :])
            dscores = (probs * dprobs).astype(BF16)
            dkeys.append(join_heads(nn(dscores, queries)).astype(BF16))
            dvalues.append(join_heads(nn(probs.astype(BF16), grads)).astype(BF16))
        out_ref[pl.ds(at, count), :] = (
            part_ref[pl.ds(at, count), :]
            + nt(jnp.concatenate(dkeys, axis=1), wk_ref[:, all_columns])
            + nt(jnp.concatenate(dvalues, axis=1), wv_ref[:, all_columns])
        ).astype(out_ref.dtype)


def unpack_kernel(here_ref, other_ref, grad_ref, *refs):
    places, outs, sems = refs[:13], refs[13:25], refs[25]
    block = lax.axis_index("blk")
    side_here = lax.axis_index("dp") % 2
    core, chip = block % 2, block // 2
    adapt = outs[0].shape[0]
    copies = [
        pltpu.make_async_copy(source, target, sems.at[index])
        for index, (source, target) in enumerate(zip((grad_ref, *outs), places))
    ]
    copies[0].start()
    matrices = (2, 0, 8, 6)
    vectors = ((3,), (4, 5), (9,), (10, 11))
    for index in range(4):
        halves = []
        for side in range(2):
            place = 2 * (chip ^ (index // 2)) + (side_here ^ side)
            halves.append(jnp.where(core == index % 2, here_ref[place], other_ref[place]))
        whole = jnp.concatenate(halves, axis=1).astype(F32)
        outs[matrices[index]][...] = whole[:adapt]
        ready = [matrices[index], *vectors[index]]
        for row, vector in enumerate(vectors[index]):
            outs[vector][...] = whole[adapt + row]
        if index == 0:
            outs[1][...] = whole[adapt + 1, :adapt]
            outs[7][...] = whole[adapt + 1, 128 : 128 + adapt]
            ready += [1, 7]
        for out in ready:
            copies[1 + out].start()
    for copy in copies:
        copy.wait()


def params(megabytes):
    return pltpu.CompilerParams(vmem_limit_bytes=megabytes << 20)


def cost(gigaflop, megabytes):
    return pl.CostEstimate(
        flops=int(gigaflop * 1e9), bytes_accessed=int(megabytes * 1e6), transcendentals=0
    )


def after(array, *others):
    return lax.optimization_barrier((array,) + others)[0]


def vmem(dims, dtype):
    return pltpu.VMEM(dims, dtype)


def in_hbm(array):
    return pltpu.with_memory_space_constraint(array, pltpu.HBM)


def shape(dims, dtype):
    return jax.ShapeDtypeStruct(dims, dtype)


def body(
    dp_size,
    tokens,
    w_query,
    w_key,
    w_value,
    w_out,
    w_inner,
    w_outer,
    down_one,
    dbias_one,
    up_one,
    ubias_one,
    gain_one,
    shift_one,
    down_two,
    dbias_two,
    up_two,
    ubias_two,
    gain_two,
    shift_two,
    seg_len,
    seg_valid,
    cotangent,
):
    rows, _, width = tokens.shape
    adapt = up_one.shape[0]
    hidden = w_inner.shape[1]
    block = lax.axis_index("blk")
    own = tokens.reshape(rows, width)
    cot = cotangent.reshape(rows, width)

    def swap(array, mask):
        return lax.ppermute(array, "blk", [(i, i ^ mask) for i in range(4)])

    def swap_all(array, mask):
        return lax.ppermute(
            array, ("dp", "blk"), [(i, i ^ mask) for i in range(4 * dp_size)]
        )

    mate = swap(own, 1)
    def near_share(own, mate):
        choices = (
            (own[128:192], own[64:128], own[:64], mate[128:192]),
            (mate[:64], own[128:192], own[64:128], own[:64]),
        )
        halves = []
        for options in choices:
            half = options[0]
            for index in range(1, 4):
                half = jnp.where(block == index, options[index], half)
            halves.append(half)
        return halves

    far = swap(jnp.concatenate(near_share(own, mate), axis=0), 2)
    mask_shapes = [vmem((count, LONG), F32) for count in (ROWS_A, ROWS_B)] * 2
    (
        q,
        kpair,
        vpair,
        bias_a,
        bias_b,
        back_a,
        back_b,
        wq_here,
        wk_here,
        wv_here,
        wout_here,
        winner_here,
    ) = pl.pallas_call(
        project_kernel,
        in_specs=[SMEM] * 2 + [HBM, VMEM] + [HBM] * 5,
        out_specs=[VMEM] * 12,
        out_shape=[vmem((2 * rows, width), BF16)] * 3
        + mask_shapes
        + [vmem((width, width), BF16)] * 4
        + [vmem((width, hidden), BF16)],
        scratch_shapes=[pltpu.VMEM((rows, width), BF16), pltpu.SemaphoreType.DMA((6,))],
        compiler_params=params(4),
        cost_estimate=cost(2.0, 12.0),
        name="project",
    )(
        in_hbm(seg_len),
        in_hbm(seg_valid),
        in_hbm(own),
        mate,
        in_hbm(w_query),
        in_hbm(w_key),
        in_hbm(w_value),
        in_hbm(w_out),
        in_hbm(w_inner),
    )
    far_mate = swap(after(far, q), 1)

    part_rows = adapt + SMALL
    mixed, kbuf, vbuf, lse, du1, attended, dbranch, keep, send = pl.pallas_call(
        main_kernel,
        in_specs=[VMEM] * 25 + [HBM],
        out_specs=[HBM] + [VMEM] * 8,
        out_shape=[
            shape((rows, width), BF16),
            vmem((4 * rows, width), BF16),
            vmem((4 * rows, width), BF16),
            vmem((rows, 128), F32),
            vmem((rows, width), F32),
            vmem((rows, width), F32),
            vmem((rows, width), BF16),
            vmem((4, part_rows, width // 2), BF16),
            vmem((4, part_rows, width // 2), BF16),
        ],
        scratch_shapes=[
            pltpu.VMEM((hidden, width), BF16),
            pltpu.VMEM((width, hidden), BF16),
            pltpu.VMEM((hidden, width), BF16),
            pltpu.VMEM((rows, hidden), F32),
            pltpu.VMEM((rows, width), BF16),
            pltpu.SemaphoreType.DMA((1 + hidden // CHUNK,)),
        ],
        compiler_params=params(30),
        cost_estimate=cost(8.0, 20.0),
        name="layer",
    )(
        own,
        far,
        far_mate,
        q,
        kpair,
        vpair,
        bias_a,
        bias_b,
        cot,
        down_one.T,
        dbias_one,
        up_one,
        ubias_one,
        gain_one,
        shift_one,
        down_two.T,
        dbias_two,
        up_two,
        ubias_two,
        gain_two,
        shift_two,
        wk_here,
        wv_here,
        wout_here,
        winner_here,
        in_hbm(w_outer),
    )

    def add(*terms):
        return functools.reduce(jnp.add, [term.astype(F32) for term in terms]).astype(BF16)

    pack, delta = pl.pallas_call(
        attended_back_kernel,
        in_specs=[VMEM] * 4,
        out_specs=[VMEM] * 2,
        out_shape=[vmem((rows + 32, width), BF16), vmem((rows, 128), F32)],
        compiler_params=params(5),
        cost_estimate=cost(0.5, 2.0),
        name="attended_back",
    )(dbranch, attended, lse, wout_here)

    def query_back(groups, part):
        return pl.pallas_call(
            functools.partial(query_back_kernel, groups),
            in_specs=[VMEM] * 12,
            out_specs=[VMEM] * (len(groups) + 1),
            out_shape=[vmem((4 * rows, WIDE), BF16)] * len(groups) + [vmem((rows, width), F32)],
            compiler_params=params(5),
            cost_estimate=cost(1.0 * len(groups), 3.0),
            name=f"query_back_{groups[0]}",
        )(far, far_mate, q, kbuf, vbuf, bias_a, bias_b, lse, delta, pack, part, wq_here)

    def key_back(groups, qbufs, part, dtype):
        return pl.pallas_call(
            functools.partial(key_back_kernel, groups),
            in_specs=[VMEM] * (9 + len(groups)),
            out_specs=VMEM,
            out_shape=vmem((rows, width), dtype),
            compiler_params=params(5),
            cost_estimate=cost(1.0 * len(groups), 3.0),
            name=f"key_back_{groups[0]}",
        )(grads_row, stats_row, kbuf, vbuf, back_a, back_b, part, *qbufs, wk_here, wv_here)

    total = add(keep, after(swap_all(send, 1), pack))
    arrived = [swap_all(total[index], mask) for index, mask in ((1, 4), (2, 2), (3, 6))]
    pack_mate = swap(after(pack, total), 1)
    qbuf0, qbuf1, part = query_back((0, 1), after(du1, total))
    total = add(total[0], *lax.optimization_barrier((*arrived, part, pack_mate))[:3])
    masks = []
    while 8 << len(masks) < 4 * dp_size:
        masks.append(8 << len(masks))
    arrived = swap_all(total, masks[0])
    pack_now = after(pack, total)
    share = near_share(pack_now, pack_mate) + [pack_now[rows:]]
    pack_far = swap(jnp.concatenate(share, axis=0), 2)
    total = add(total, arrived)
    arrived = swap_all(total, masks[1])
    qbuf2, part = query_back((2,), after(part, total))
    pack_far, part = lax.optimization_barrier((pack_far, part))
    pack_far_mate = swap(pack_far, 1)
    total = add(total, after(arrived, part))
    for mask in masks[2:]:
        total = add(total, swap_all(total, mask))
    others = [swap_all(total, mask) for mask in (4, 2, 6)]
    grads_row, stats_row = pl.pallas_call(
        gather_kernel,
        in_specs=[VMEM] * 4,
        out_specs=[VMEM] * 2,
        out_shape=[vmem((4 * rows, width), BF16), vmem((64, LONG), F32)],
        compiler_params=params(3),
        cost_estimate=cost(0.1, 1.0),
        name="gather",
    )(pack, pack_mate, pack_far, after(pack_far_mate, total))
    part = key_back((0, 1), (qbuf0, qbuf1), after(part, total), F32)
    here = jnp.stack([total, *lax.optimization_barrier((*others, part))[:3]])
    other = swap_all(here, 1)
    input_grad = key_back((2,), (qbuf2,), after(part, here), BF16)

    grad_dims = ((adapt, width), (adapt,), (adapt, width), (width,), (width,), (width,)) * 2
    input_grad, *grads = pl.pallas_call(
        unpack_kernel,
        in_specs=[VMEM] * 3,
        out_specs=[HBM] * 13,
        out_shape=[shape((rows, width), BF16)] + [shape(dims, F32) for dims in grad_dims],
        scratch_shapes=[pltpu.VMEM(dims, F32) for dims in grad_dims]
        + [pltpu.SemaphoreType.DMA((13,))],
        compiler_params=params(5),
        name="unpack",
    )(here, other, input_grad)
    return (mixed.reshape(tokens.shape), input_grad.reshape(tokens.shape)) + tuple(
        grad.T if index in (0, 6) else grad for index, grad in enumerate(grads)
    )


def solution(mesh):
    in_specs = (
        (P("blk", "dp", None),) + (P(),) * 18 + (P("dp", None),) * 2 + (P("blk", "dp", None),)
    )
    out_specs = (P("blk", "dp", None),) * 2 + (P(),) * 12
    return jax.shard_map(
        functools.partial(body, mesh.shape["dp"]),
        mesh=mesh,
        in_specs=in_specs,
        out_specs=out_specs,
        check_vma=False,
    )
```

```python
import functools

import jax
import jax.numpy as jnp
from jax import lax
from jax.experimental import pallas as pl
from jax.experimental.pallas import tpu as pltpu
from jax.sharding import PartitionSpec as P

HEAD = 64
GROUP = 4
LONG_AT = 128
LONG = 512
ROWS_A = 64
WIDE = GROUP * HEAD
HALF = 256
SHARE = 128
CHUNK = 768
SMALL = 8
ROWS_B = 128
NEG = -1e30
F32 = jnp.float32
BF16 = jnp.bfloat16

VMEM = pl.BlockSpec(memory_space=pltpu.VMEM)
SMEM = pl.BlockSpec(memory_space=pltpu.SMEM)
HBM = pl.BlockSpec(memory_space=pltpu.HBM)


def nn(left, right):
    return lax.dot_general(left, right, (((1,), (0,)), ((), ())), preferred_element_type=F32)


def nt(left, right):
    return lax.dot_general(left, right, (((1,), (1,)), ((), ())), preferred_element_type=F32)


def tn(left, right):
    return lax.dot_general(left, right, (((0,), (0,)), ((), ())), preferred_element_type=F32)


def gelu_both(values):
    phi = 0.5 + 0.5 * lax.erf(values * 0.7071067811865476)
    bell = jnp.exp(-0.5 * values * values)
    return values * phi, phi + values * bell * 0.3989422804014327


def normed(values):
    centre = jnp.mean(values, axis=-1, keepdims=True)
    centred = values - centre
    spread = jnp.mean(centred * centred, axis=-1, keepdims=True)
    scale = lax.rsqrt(spread + 1e-06)
    return centred * scale, scale


def norm_back(incoming, gain, normal, scale):
    scaled = incoming * gain
    first = jnp.mean(scaled, axis=-1, keepdims=True)
    second = jnp.mean(scaled * normal, axis=-1, keepdims=True)
    return scale * (scaled - first - normal * second)


def row_of(ref):
    return ref[...].reshape(1, ref.shape[0])


def own_rows(block):
    return (
        pl.multiple_of(jnp.where(block == 0, 128, 0), 64),
        pl.multiple_of(jnp.where(block == 0, 0, 64), 64),
    )


def far_place(chip):
    return pl.multiple_of(LONG_AT + 2 * SHARE * (1 - chip), 128)


def near_places(block):
    chip = block // 2
    long_at = LONG_AT * (1 - chip)
    short_at = LONG_AT * chip
    outer = (block == 0) | (block == 3)
    return (
        pl.multiple_of(long_at, 128),
        pl.multiple_of(jnp.where(outer, short_at, long_at), 128),
    )


def far_tokens(core, far_ref, far_mate_ref):
    far, far_mate = far_ref[...], far_mate_ref[...]
    first = core == 0
    return jnp.concatenate(
        [jnp.where(first, far, far_mate), jnp.where(first, far_mate, far)], axis=0
    )


def partner_offset(block):
    return pl.multiple_of(jnp.where(block == 0, 0, jnp.where(block == 3, 256, 128)), 128)


def bounds(len_ref, valid_ref, places):
    low = jnp.zeros(places.shape, jnp.int32)
    high = jnp.zeros(places.shape, jnp.int32)
    start = jnp.int32(0)
    for slot in range(len_ref.shape[1]):
        end = start + len_ref[0, slot]
        inside = (places >= start) & (places < end)
        low = jnp.where(inside, start, low)
        high = jnp.where(inside, start + valid_ref[0, slot], high)
        start = end
    return low, high


def bias_of(len_ref, valid_ref, query_at, key_at, rows, columns=LONG):
    places = query_at + lax.broadcasted_iota(jnp.int32, (rows, 1), 0)
    low, high = bounds(len_ref, valid_ref, places)
    keys = key_at + lax.broadcasted_iota(jnp.int32, (rows, columns), 1)
    return jnp.where((keys >= low) & (keys < high), 0.0, NEG)


def bias_back_of(len_ref, valid_ref, key_at, query_at, rows):
    places = query_at + lax.broadcasted_iota(jnp.int32, (1, LONG), 1)
    low, high = bounds(len_ref, valid_ref, places)
    keys = key_at + lax.broadcasted_iota(jnp.int32, (rows, LONG), 0)
    return jnp.where((keys >= low) & (keys < high), 0.0, NEG)


def spread_heads(part):
    lane = lax.broadcasted_iota(jnp.int32, part.shape, 1) // HEAD
    return jnp.concatenate(
        [jnp.where(lane == head, part, jnp.zeros_like(part)) for head in range(GROUP)], axis=0
    )


def join_heads(stacked):
    rows = stacked.shape[0] // GROUP
    lane = lax.broadcasted_iota(jnp.int32, (rows, stacked.shape[1]), 1) // HEAD
    out = stacked[:rows]
    for head in range(1, GROUP):
        out = jnp.where(lane == head, stacked[head * rows : (head + 1) * rows], out)
    return out


def masked(scores, bias):
    split = scores.reshape((GROUP,) + bias.shape)
    return (split + bias).reshape(scores.shape)


def less_rows(stacked, rows):
    count = stacked.shape[0] // GROUP
    return jnp.concatenate(
        [stacked[head * count : (head + 1) * count] - rows[head : head + 1] for head in range(GROUP)],
        axis=0,
    )


def fetch_kernel(source, target, sem):
    copy = pltpu.make_async_copy(source, target, sem)
    copy.start()
    copy.wait()


def project_kernel(
    len_ref,
    valid_ref,
    own_ref,
    mate_ref,
    wq_hbm,
    wk_hbm,
    wv_hbm,
    wout_hbm,
    winner_hbm,
    q_ref,
    k_ref,
    v_ref,
    bias_a_ref,
    bias_b_ref,
    back_a_ref,
    back_b_ref,
    near_a_ref,
    near_b_ref,
    far_a_ref,
    far_b_ref,
    wq_ref,
    wk_ref,
    wv_ref,
    wout_ref,
    winner_ref,
    sems,
):
    moves = (
        (wq_hbm, wq_ref),
        (wk_hbm, wk_ref),
        (wv_hbm, wv_ref),
        (wout_hbm, wout_ref),
        (winner_hbm, winner_ref),
    )
    copies = [
        pltpu.make_async_copy(source, target, sems.at[index])
        for index, (source, target) in enumerate(moves)
    ]
    block = lax.axis_index("blk")

    @pl.when(block < 4)
    def _():
        for copy in copies:
            copy.start()

    core = block % 2
    rows = own_ref.shape[0]
    first = block * rows
    at_a, at_b = own_rows(block)
    meet_b = partner_offset(block)
    bias_a_ref[...] = bias_of(len_ref, valid_ref, first + at_a, LONG_AT, ROWS_A)
    bias_b_ref[...] = bias_of(len_ref, valid_ref, first + at_b, meet_b, ROWS_B)
    chip = block // 2
    near_a, near_b = near_places(block)
    pair_at = chip * 2 * rows
    far_at = far_place(chip)
    for at, count, near, near_ref, far_ref in (
        (at_a, ROWS_A, near_a, near_a_ref, far_a_ref),
        (at_b, ROWS_B, near_b, near_b_ref, far_b_ref),
    ):
        near_ref[...] = bias_of(len_ref, valid_ref, first + at, pair_at + near, count, HALF)
        far_ref[...] = bias_of(len_ref, valid_ref, first + at, far_at, count, HALF)
    back_a_ref[...] = bias_back_of(len_ref, valid_ref, first + at_a, LONG_AT, ROWS_A)
    back_b_ref[...] = bias_back_of(len_ref, valid_ref, first + at_b, meet_b, ROWS_B)
    mine = pl.multiple_of(core * rows, rows)
    other = pl.multiple_of((1 - core) * rows, rows)
    both = jnp.concatenate([own_ref[...], mate_ref[...]], axis=0)
    for copy, weight, out, scale in (
        (copies[0], wq_ref, q_ref, 0.125),
        (copies[1], wk_ref, k_ref, 1.0),
        (copies[2], wv_ref, v_ref, 1.0),
    ):
        copy.wait()
        product = (nn(both, weight[...]) * scale).astype(BF16)
        out[pl.ds(mine, rows), :] = product[:rows]
        out[pl.ds(other, rows), :] = product[rows:]
    copies[3].wait()
    copies[4].wait()


def over_heads(stat):
    count = stat.shape[0] // GROUP
    parts = [stat[head * count : (head + 1) * count] for head in range(GROUP)]
    left = lax.broadcasted_iota(jnp.int32, (1, 128), 1) < HEAD
    return jnp.concatenate(
        [jnp.where(left, parts[0], parts[1]), jnp.where(left, parts[2], parts[3])], axis=1
    )


def near_kernel(
    far_ref,
    q_ref,
    kpair_ref,
    vpair_ref,
    near_a_ref,
    near_b_ref,
    wk_ref,
    wv_ref,
    kfar_ref,
    vfar_ref,
    sums_ref,
    tops_ref,
    totals_ref,
):
    kfar_ref[...] = nn(far_ref[...], wk_ref[...]).astype(BF16)
    vfar_ref[...] = nn(far_ref[...], wv_ref[...]).astype(BF16)
    block = lax.axis_index("blk")
    rows, width = sums_ref.shape
    core = block % 2
    at_a, at_b = own_rows(block)
    near_a, near_b = near_places(block)
    for at, count, near, bias_ref, at_stat in (
        (at_a, ROWS_A, near_a, near_a_ref, 0),
        (at_b, ROWS_B, near_b, near_b_ref, GROUP * ROWS_A),
    ):
        stacked = pl.ds(at_stat, GROUP * count)
        for group in range(width // WIDE):
            columns = slice(group * WIDE, (group + 1) * WIDE)
            queries = spread_heads(q_ref[pl.ds(core * rows + at, count), columns])
            scores = masked(nt(queries, kpair_ref[pl.ds(near, HALF), columns]), bias_ref[...])
            top = jnp.max(scores, axis=-1, keepdims=True)
            weights = jnp.exp(scores - top)
            total = jnp.sum(weights, axis=-1, keepdims=True)
            sums = nn(weights.astype(BF16), vpair_ref[pl.ds(near, HALF), columns])
            sums_ref[pl.ds(at, count), columns] = join_heads(sums)
            tops_ref[group, stacked, :] = jnp.broadcast_to(top, (GROUP * count, 128))
            totals_ref[group, stacked, :] = jnp.broadcast_to(total, (GROUP * count, 128))


def main_kernel(
    own_ref,
    far_mate_ref,
    q_ref,
    kpair_ref,
    vpair_ref,
    kfar_ref,
    vfar_ref,
    sums_ref,
    tops_ref,
    totals_ref,
    far_a_ref,
    far_b_ref,
    cot_ref,
    down1_ref,
    dbias1_ref,
    up1_ref,
    ubias1_ref,
    gain1_ref,
    shift1_ref,
    down2_ref,
    dbias2_ref,
    up2_ref,
    ubias2_ref,
    gain2_ref,
    shift2_ref,
    wk_ref,
    wv_ref,
    wout_ref,
    winner_ref,
    wouter_hbm,
    mixed_hbm,
    kbuf,
    vbuf,
    lse_ref,
    du1_ref,
    attended_ref,
    grad_pre_ref,
    keep_ref,
    send_ref,
    wouter_ref,
    wouter_t_ref,
    winner_t_ref,
    slope_ref,
    mixed_ref,
    sems,
):
    hidden_units = winner_ref.shape[1]

    def outer_copy(index):
        part = pl.ds(pl.multiple_of(index * CHUNK, CHUNK), CHUNK)
        return pltpu.make_async_copy(wouter_hbm.at[part], wouter_ref.at[part], sems.at[1 + index])

    @pl.loop(0, hidden_units // CHUNK)
    def _(index):
        outer_copy(index).start()

    mixed_copy = pltpu.make_async_copy(mixed_ref, mixed_hbm, sems.at[0])
    block = lax.axis_index("blk")
    core = block % 2
    chip = block // 2
    rows, width = own_ref.shape
    at_a, at_b = own_rows(block)

    def mine(ref):
        return jnp.concatenate([ref[pl.ds(at_a, ROWS_A), :], ref[pl.ds(at_b, ROWS_B), :]], axis=0)

    def put(ref, value):
        ref[pl.ds(at_a, ROWS_A), :] = value[:ROWS_A]
        ref[pl.ds(at_b, ROWS_B), :] = value[ROWS_A:]

    near = pl.multiple_of(chip * 2 * rows, 2 * rows)
    kbuf[pl.ds(near, 2 * rows), :] = kpair_ref[...]
    vbuf[pl.ds(near, 2 * rows), :] = vpair_ref[...]
    far_at = far_place(chip)
    far_first = pl.multiple_of(far_at + SHARE * core, 128)
    far_second = pl.multiple_of(far_at + SHARE * (1 - core), 128)
    kbuf[pl.ds(far_first, SHARE), :] = kfar_ref[...]
    vbuf[pl.ds(far_first, SHARE), :] = vfar_ref[...]
    kbuf[pl.ds(far_second, SHARE), :] = nn(far_mate_ref[...], wk_ref[...]).astype(BF16)
    vbuf[pl.ds(far_second, SHARE), :] = nn(far_mate_ref[...], wv_ref[...]).astype(BF16)

    lane = lax.broadcasted_iota(jnp.int32, (1, 128), 1)
    attended_parts = []
    lse_parts = []
    for at, count, bias_ref, at_stat in (
        (at_a, ROWS_A, far_a_ref, 0),
        (at_b, ROWS_B, far_b_ref, GROUP * ROWS_A),
    ):
        pieces = []
        lse = jnp.zeros((count, 128), F32)
        stacked = pl.ds(at_stat, GROUP * count)
        for group in range(width // WIDE):
            columns = slice(group * WIDE, (group + 1) * WIDE)
            queries = spread_heads(q_ref[pl.ds(core * rows + at, count), columns])
            scores = masked(nt(queries, kbuf[pl.ds(far_at, HALF), columns]), bias_ref[...])
            top_near = tops_ref[group, stacked, :]
            top = jnp.maximum(top_near, jnp.max(scores, axis=-1, keepdims=True))
            weights = jnp.exp(scores - jnp.concatenate([top, top], axis=1))
            shrink = jnp.exp(top_near - top)
            total = shrink * totals_ref[group, stacked, :] + jnp.sum(
                weights, axis=-1, keepdims=True
            )
            sums = join_heads(nn(weights.astype(BF16), vbuf[pl.ds(far_at, HALF), columns]))
            sums = sums + sums_ref[pl.ds(at, count), columns] * over_heads(shrink)
            pieces.append(sums * over_heads(1.0 / total))
            log_total = top + jnp.log(total)
            for head in range(GROUP):
                one = log_total[head * count : (head + 1) * count]
                lse = jnp.where(lane == group * GROUP + head, one, lse)
        attended_parts.append(jnp.concatenate(pieces, axis=1))
        lse_parts.append(lse)
    attended_f = jnp.concatenate(attended_parts, axis=0)
    put(lse_ref, jnp.concatenate(lse_parts, axis=0))
    put(attended_ref, attended_f)
    attended = attended_f.astype(BF16)
    branch = nn(attended, wout_ref[...]).astype(BF16)

    pre1 = nt(branch, down1_ref[...]) + row_of(dbias1_ref)
    inner1_f, slope1 = gelu_both(pre1)
    inner1 = inner1_f.astype(BF16)
    summed = (
        mine(own_ref).astype(F32) + branch.astype(F32) + nn(inner1, up1_ref[...]) + row_of(ubias1_ref)
    )
    normal1, scale1 = normed(summed)
    gain1 = row_of(gain1_ref)
    mid = (normal1 * gain1 + row_of(shift1_ref)).astype(BF16)

    for index in range(hidden_units // CHUNK):
        outer_copy(index).wait()
    ffn_f = jnp.zeros((rows, width), F32)
    for at in range(0, hidden_units, CHUNK):
        hidden_f, slope = gelu_both(nn(mid, winner_ref[:, at : at + CHUNK]))
        slope_ref[:, at : at + CHUNK] = slope
        wouter_t_ref[:, at : at + CHUNK] = wouter_ref[at : at + CHUNK, :].T
        winner_t_ref[at : at + CHUNK, :] = winner_ref[:, at : at + CHUNK].T
        ffn_f = ffn_f + nn(hidden_f.astype(BF16), wouter_ref[at : at + CHUNK, :])
    ffn = ffn_f.astype(BF16)

    pre2 = nt(ffn, down2_ref[...]) + row_of(dbias2_ref)
    inner2_f, slope2 = gelu_both(pre2)
    inner2 = inner2_f.astype(BF16)
    summed = mid.astype(F32) + ffn.astype(F32) + nn(inner2, up2_ref[...]) + row_of(ubias2_ref)
    normal2, scale2 = normed(summed)
    gain2 = row_of(gain2_ref)
    put(mixed_ref, (normal2 * gain2 + row_of(shift2_ref)).astype(BF16))
    mixed_copy.start()

    cot = mine(cot_ref).astype(F32)
    grad_gain2 = jnp.sum(cot * normal2, axis=0, keepdims=True)
    grad_shift2 = jnp.sum(cot, axis=0, keepdims=True)
    du2 = norm_back(cot, gain2, normal2, scale2)

    def adapter_back(source, up, inner, slope, incoming):
        out_grad = incoming.astype(BF16)
        grad_up = tn(inner, out_grad)
        grad_ubias = jnp.sum(out_grad.astype(F32), axis=0, keepdims=True)
        grad_pre = (nt(out_grad, up) * slope).astype(BF16)
        grad_down = tn(grad_pre, source)
        grad_dbias = jnp.sum(grad_pre.astype(F32), axis=0, keepdims=True)
        return grad_pre, grad_down, grad_dbias, grad_up, grad_ubias

    grad_pre2, grad_down2, grad_dbias2, grad_up2, grad_ubias2 = adapter_back(
        ffn, up2_ref[...], inner2, slope2, du2
    )
    dffn = (du2 + nn(grad_pre2, down2_ref[...])).astype(BF16)
    dmid = du2
    for at in range(0, hidden_units, CHUNK):
        dhidden = (nn(dffn, wouter_t_ref[:, at : at + CHUNK]) * slope_ref[:, at : at + CHUNK]).astype(
            BF16
        )
        dmid = dmid + nn(dhidden, winner_t_ref[at : at + CHUNK, :])

    grad_gain1 = jnp.sum(dmid * normal1, axis=0, keepdims=True)
    grad_shift1 = jnp.sum(dmid, axis=0, keepdims=True)
    du1 = norm_back(dmid, gain1, normal1, scale1)
    grad_pre1, grad_down1, grad_dbias1, grad_up1, grad_ubias1 = adapter_back(
        branch, up1_ref[...], inner1, slope1, du1
    )
    put(du1_ref, du1)
    put(grad_pre_ref, grad_pre1)

    blank = jnp.zeros((1, width), F32)
    both_dbias = jnp.concatenate(
        [
            grad_dbias1,
            jnp.zeros((1, 128 - grad_dbias1.shape[1]), F32),
            grad_dbias2,
            jnp.zeros((1, width - 128 - grad_dbias2.shape[1]), F32),
        ],
        axis=1,
    )
    quarters = (
        (grad_up1, grad_ubias1, both_dbias),
        (grad_down1, grad_gain1, grad_shift1),
        (grad_up2, grad_ubias2, blank),
        (grad_down2, grad_gain2, grad_shift2),
    )
    filler = jnp.zeros((SMALL - 2, width), F32)
    wholes = [
        jnp.concatenate([matrix, one, two, filler], axis=0).astype(BF16)
        for matrix, one, two in quarters
    ]
    side_here = lax.axis_index("dp") % 2
    for chip_of in range(2):
        even, odd = wholes[2 * chip_of], wholes[2 * chip_of + 1]
        kept = jnp.where(core == 0, even, odd)
        sent = jnp.where(core == 0, odd, even)
        for side in range(2):
            half = slice(side * width // 2, (side + 1) * width // 2)
            place = 2 * (chip ^ chip_of) + (side_here ^ side)
            keep_ref[place] = kept[:, half]
            send_ref[place] = sent[:, half]

    mixed_copy.wait()


def attended_back_kernel(
    du1_ref, grad_pre_ref, down1_ref, attended_ref, lse_ref, wout_ref, pack_ref, delta_ref
):
    rows, width = du1_ref.shape
    dbranch = (du1_ref[...] + nn(grad_pre_ref[...], down1_ref[...])).astype(BF16)
    dattended = nt(dbranch, wout_ref[...]).astype(BF16)
    pack_ref[:rows, :] = dattended
    product = dattended.astype(F32) * attended_ref[...]
    product_hi = product.astype(BF16)
    product_lo = (product - product_hi.astype(F32)).astype(BF16)
    head_of = lax.broadcasted_iota(jnp.int32, (128, width), 1) // HEAD
    picks = (head_of == lax.broadcasted_iota(jnp.int32, (128, width), 0)).astype(BF16)
    delta = nt(product_hi, picks) + nt(product_lo, picks)
    delta_ref[...] = delta
    blank = jnp.zeros((256 - rows, 128), F32)
    delta_rows = jnp.transpose(jnp.concatenate([delta, blank], axis=0))[:16]
    lse_rows = jnp.transpose(jnp.concatenate([lse_ref[...], blank], axis=0))[:16]

    def pieces_of(value, count):
        out = []
        for _ in range(count):
            piece = value.astype(BF16)
            value = value - piece.astype(F32)
            out.append(piece)
        return out

    pack_ref[rows : rows + 16, :] = jnp.concatenate(pieces_of(lse_rows, 3), axis=1)
    pack_ref[rows + 16 : rows + 32, :] = jnp.concatenate(
        pieces_of(delta_rows, 2) + [jnp.zeros((16, 256), BF16)], axis=1
    )


def query_back_kernel(
    groups,
    far_ref,
    far_mate_ref,
    q_ref,
    kbuf,
    vbuf,
    bias_a_ref,
    bias_b_ref,
    lse_ref,
    delta_ref,
    pack_ref,
    part_in_ref,
    wq_ref,
    *outs,
):
    block = lax.axis_index("blk")
    rows = q_ref.shape[0] // 2
    core, chip = block % 2, block // 2
    at_a, at_b = own_rows(block)
    meet_b = partner_offset(block)
    all_columns = slice(groups[0] * WIDE, (groups[-1] + 1) * WIDE)
    wq = wq_ref[:, all_columns]
    queries_far = (nn(far_tokens(core, far_ref, far_mate_ref), wq) * 0.125).astype(BF16)
    part_ref = outs[-1]
    for index, (group, qbuf) in enumerate(zip(groups, outs)):
        near = pl.ds(pl.multiple_of(chip * 2 * rows, rows), 2 * rows)
        qbuf[near, :] = q_ref[:, group * WIDE : (group + 1) * WIDE]
        qbuf[pl.ds(far_place(chip), 2 * SHARE), :] = queries_far[
            :, index * WIDE : (index + 1) * WIDE
        ]
    parts = []
    for at, count, meet, bias_ref in (
        (at_a, ROWS_A, LONG_AT, bias_a_ref),
        (at_b, ROWS_B, meet_b, bias_b_ref),
    ):
        lse = lse_ref[pl.ds(at, count), :]
        delta = delta_ref[pl.ds(at, count), :]
        pieces = []
        for group in groups:
            columns = slice(group * WIDE, (group + 1) * WIDE)
            heads = range(group * GROUP, (group + 1) * GROUP)
            log_total = jnp.concatenate([lse[:, head : head + 1] for head in heads], axis=0)
            deltas = jnp.concatenate([delta[:, head : head + 1] for head in heads], axis=0)
            keys = kbuf[pl.ds(meet, LONG), columns]
            scores = nt(spread_heads(q_ref[pl.ds(core * rows + at, count), columns]), keys)
            scores = masked(scores, bias_ref[...])
            probs = jnp.exp(scores - log_total)
            dprobs = nt(
                spread_heads(pack_ref[pl.ds(at, count), columns]), vbuf[pl.ds(meet, LONG), columns]
            )
            dscores = (probs * (dprobs - deltas)).astype(BF16)
            pieces.append(join_heads(nn(dscores, keys)).astype(BF16))
        parts.append(jnp.concatenate(pieces, axis=1))
    added = nt(jnp.concatenate(parts, axis=0), wq) * 0.125
    for at, rows_of in ((at_a, slice(0, ROWS_A)), (at_b, slice(ROWS_A, rows))):
        place = pl.ds(at, rows_of.stop - rows_of.start)
        part_ref[place, :] = part_in_ref[place, :] + added[rows_of]


def gather_kernel(own_ref, mate_ref, far_ref, far_mate_ref, grads_ref, stats_ref):
    block = lax.axis_index("blk")
    rows = own_ref.shape[0] - 32
    core, chip = block % 2, block // 2
    meet_b = partner_offset(block)
    grads_ref[pl.ds(pl.multiple_of(block * rows, rows), rows), :] = own_ref[:rows, :]
    grads_ref[pl.ds(pl.multiple_of((block ^ 1) * rows, rows), rows), :] = mate_ref[:rows, :]
    far_at = far_place(chip)
    far_first = pl.multiple_of(far_at + SHARE * core, 128)
    far_second = pl.multiple_of(far_at + SHARE * (1 - core), 128)
    grads_ref[pl.ds(far_first, SHARE), :] = far_ref[:SHARE, :]
    grads_ref[pl.ds(far_second, SHARE), :] = far_mate_ref[:SHARE, :]
    stats = []
    for ref, at in ((own_ref, rows), (mate_ref, rows), (far_ref, SHARE), (far_mate_ref, SHARE)):
        lse = ref[at : at + 16, :].astype(F32)
        delta = ref[at + 16 : at + 32, :].astype(F32)
        stats.append(
            jnp.concatenate(
                [
                    lse[:, :256] + (lse[:, 256:512] + lse[:, 512:]),
                    delta[:, :256] + delta[:, 256:512],
                ],
                axis=0,
            )[:, :rows]
        )
    ordered = []
    for place in range(4):
        pick = stats[place]
        for index in range(4):
            if index != place:
                pick = jnp.where(block ^ index == place, stats[index], pick)
        ordered.append(pick)
    whole = jnp.concatenate(ordered, axis=1)
    stats_ref[:32, :] = whole[:, LONG_AT : LONG_AT + LONG]
    here = whole[:, :LONG]
    for start in (128, 256):
        here = jnp.where(meet_b == start, whole[:, start : start + LONG], here)
    stats_ref[32:, :] = here


def key_back_kernel(groups, grads_ref, stats_ref, kbuf, vbuf, back_a_ref, back_b_ref, part_ref, *refs):
    qbufs, (wk_ref, wv_ref, out_ref) = refs[:-3], refs[-3:]
    block = lax.axis_index("blk")
    rows = out_ref.shape[0]
    at_a, at_b = own_rows(block)
    first = block * rows
    all_columns = slice(groups[0] * WIDE, (groups[-1] + 1) * WIDE)
    parts = []
    for at, count, meet, bias_ref, at_stats in (
        (at_a, ROWS_A, LONG_AT, back_a_ref, 0),
        (at_b, ROWS_B, partner_offset(block), back_b_ref, 32),
    ):
        own_at = pl.multiple_of(first + at, 64)
        dkeys, dvalues = [], []
        for group, qbuf in zip(groups, qbufs):
            columns = slice(group * WIDE, (group + 1) * WIDE)
            at_lse = at_stats + group * GROUP
            at_delta = at_lse + 16
            queries = qbuf[pl.ds(meet, LONG), :]
            grads = grads_ref[pl.ds(meet, LONG), columns]
            scores = nt(spread_heads(kbuf[pl.ds(own_at, count), columns]), queries)
            scores = masked(scores, bias_ref[...])
            probs = jnp.exp(less_rows(scores, stats_ref[at_lse : at_lse + GROUP, :]))
            dprobs = nt(spread_heads(vbuf[pl.ds(own_at, count), columns]), grads)
            dprobs = less_rows(dprobs, stats_ref[at_delta : at_delta + GROUP, :])
            dscores = (probs * dprobs).astype(BF16)
            dkeys.append(join_heads(nn(dscores, queries)).astype(BF16))
            dvalues.append(join_heads(nn(probs.astype(BF16), grads)).astype(BF16))
        parts.append((jnp.concatenate(dkeys, axis=1), jnp.concatenate(dvalues, axis=1)))
    dkey, dvalue = (jnp.concatenate(both, axis=0) for both in zip(*parts))
    added = nt(dkey, wk_ref[:, all_columns]) + nt(dvalue, wv_ref[:, all_columns])
    for at, rows_of in ((at_a, slice(0, ROWS_A)), (at_b, slice(ROWS_A, rows))):
        place = pl.ds(at, rows_of.stop - rows_of.start)
        out_ref[place, :] = (part_ref[place, :] + added[rows_of]).astype(out_ref.dtype)


def unpack_kernel(here_ref, other_ref, grad_ref, *refs):
    places, outs, sems = refs[:13], refs[13:25], refs[25]
    block = lax.axis_index("blk")
    side_here = lax.axis_index("dp") % 2
    core, chip = block % 2, block // 2
    adapt = outs[0].shape[0]
    copies = [
        pltpu.make_async_copy(source, target, sems.at[index])
        for index, (source, target) in enumerate(zip((grad_ref, *outs), places))
    ]
    copies[0].start()
    matrices = (2, 0, 8, 6)
    vectors = ((3,), (4, 5), (9,), (10, 11))
    for index in range(4):
        halves = []
        for side in range(2):
            place = 2 * (chip ^ (index // 2)) + (side_here ^ side)
            halves.append(jnp.where(core == index % 2, here_ref[place], other_ref[place]))
        whole = jnp.concatenate(halves, axis=1).astype(F32)
        outs[matrices[index]][...] = whole[:adapt]
        ready = [matrices[index], *vectors[index]]
        for row, vector in enumerate(vectors[index]):
            outs[vector][...] = whole[adapt + row]
        if index == 0:
            outs[1][...] = whole[adapt + 1, :adapt]
            outs[7][...] = whole[adapt + 1, 128 : 128 + adapt]
            ready += [1, 7]
        for out in ready:
            copies[1 + out].start()
    for copy in copies:
        copy.wait()


def params(megabytes):
    return pltpu.CompilerParams(vmem_limit_bytes=megabytes << 20)


def cost(gigaflop, megabytes):
    return pl.CostEstimate(
        flops=int(gigaflop * 1e9), bytes_accessed=int(megabytes * 1e6), transcendentals=0
    )


def after(array, *others):
    return lax.optimization_barrier((array,) + others)[0]


def vmem(dims, dtype):
    return pltpu.VMEM(dims, dtype)


def in_hbm(array):
    return pltpu.with_memory_space_constraint(array, pltpu.HBM)


def shape(dims, dtype):
    return jax.ShapeDtypeStruct(dims, dtype)


def body(
    dp_size,
    tokens,
    w_query,
    w_key,
    w_value,
    w_out,
    w_inner,
    w_outer,
    down_one,
    dbias_one,
    up_one,
    ubias_one,
    gain_one,
    shift_one,
    down_two,
    dbias_two,
    up_two,
    ubias_two,
    gain_two,
    shift_two,
    seg_len,
    seg_valid,
    cotangent,
):
    rows, _, width = tokens.shape
    adapt = up_one.shape[0]
    hidden = w_inner.shape[1]
    block = lax.axis_index("blk")
    own = tokens.reshape(rows, width)
    cot = cotangent.reshape(rows, width)

    def swap(array, mask):
        return lax.ppermute(array, "blk", [(i, i ^ mask) for i in range(4)])

    def swap_all(array, mask):
        return lax.ppermute(
            array, ("dp", "blk"), [(i, i ^ mask) for i in range(4 * dp_size)]
        )

    mate = swap(own, 1)
    own = pl.pallas_call(
        fetch_kernel,
        in_specs=[HBM],
        out_specs=VMEM,
        out_shape=vmem((rows, width), BF16),
        scratch_shapes=[pltpu.SemaphoreType.DMA],
        compiler_params=params(1),
        cost_estimate=cost(0.1, 1.0),
        name="fetch",
    )(in_hbm(own))
    def near_share(own, mate):
        choices = (
            (own[128:192], own[64:128], own[:64], mate[128:192]),
            (mate[:64], own[128:192], own[64:128], own[:64]),
        )
        halves = []
        for options in choices:
            half = options[0]
            for index in range(1, 4):
                half = jnp.where(block == index, options[index], half)
            halves.append(half)
        return halves

    far = swap(jnp.concatenate(near_share(own, mate), axis=0), 2)
    half_mask_shapes = [vmem((count, HALF), F32) for count in (ROWS_A, ROWS_B)] * 2
    mask_shapes = [vmem((count, LONG), F32) for count in (ROWS_A, ROWS_B)] * 2
    (
        q,
        kpair,
        vpair,
        bias_a,
        bias_b,
        back_a,
        back_b,
        near_a,
        near_b,
        far_a,
        far_b,
        wq_here,
        wk_here,
        wv_here,
        wout_here,
        winner_here,
    ) = pl.pallas_call(
        project_kernel,
        in_specs=[SMEM] * 2 + [VMEM] * 2 + [HBM] * 5,
        out_specs=[VMEM] * 16,
        out_shape=[vmem((2 * rows, width), BF16)] * 3
        + mask_shapes
        + half_mask_shapes
        + [vmem((width, width), BF16)] * 4
        + [vmem((width, hidden), BF16)],
        scratch_shapes=[pltpu.SemaphoreType.DMA((5,))],
        compiler_params=params(4),
        cost_estimate=cost(2.0, 12.0),
        name="project",
    )(
        in_hbm(seg_len),
        in_hbm(seg_valid),
        own,
        mate,
        in_hbm(w_query),
        in_hbm(w_key),
        in_hbm(w_value),
        in_hbm(w_out),
        in_hbm(w_inner),
    )
    far_mate = swap(after(far, q), 1)
    kfar, vfar, sums, tops, totals = pl.pallas_call(
        near_kernel,
        in_specs=[VMEM] * 8,
        out_specs=[VMEM] * 5,
        out_shape=[vmem((SHARE, width), BF16)] * 2
        + [vmem((rows, width), F32)]
        + [vmem((width // WIDE, GROUP * rows, 128), F32)] * 2,
        compiler_params=params(5),
        cost_estimate=cost(1.0, 2.0),
        name="near",
    )(far, q, kpair, vpair, near_a, near_b, wk_here, wv_here)

    part_rows = adapt + SMALL
    mixed, kbuf, vbuf, lse, du1, attended, grad_pre, keep, send = pl.pallas_call(
        main_kernel,
        in_specs=[VMEM] * 29 + [HBM],
        out_specs=[HBM] + [VMEM] * 8,
        out_shape=[
            shape((rows, width), BF16),
            vmem((4 * rows, width), BF16),
            vmem((4 * rows, width), BF16),
            vmem((rows, 128), F32),
            vmem((rows, width), F32),
            vmem((rows, width), F32),
            vmem((rows, adapt), BF16),
            vmem((4, part_rows, width // 2), BF16),
            vmem((4, part_rows, width // 2), BF16),
        ],
        scratch_shapes=[
            pltpu.VMEM((hidden, width), BF16),
            pltpu.VMEM((width, hidden), BF16),
            pltpu.VMEM((hidden, width), BF16),
            pltpu.VMEM((rows, hidden), F32),
            pltpu.VMEM((rows, width), BF16),
            pltpu.SemaphoreType.DMA((1 + hidden // CHUNK,)),
        ],
        compiler_params=params(22),
        cost_estimate=cost(8.0, 20.0),
        name="layer",
    )(
        own,
        far_mate,
        q,
        kpair,
        vpair,
        kfar,
        vfar,
        sums,
        tops,
        totals,
        far_a,
        far_b,
        cot,
        down_one.T,
        dbias_one,
        up_one,
        ubias_one,
        gain_one,
        shift_one,
        down_two.T,
        dbias_two,
        up_two,
        ubias_two,
        gain_two,
        shift_two,
        wk_here,
        wv_here,
        wout_here,
        winner_here,
        in_hbm(w_outer),
    )

    def add(*terms):
        return functools.reduce(jnp.add, [term.astype(F32) for term in terms]).astype(BF16)

    pack, delta = pl.pallas_call(
        attended_back_kernel,
        in_specs=[VMEM] * 6,
        out_specs=[VMEM] * 2,
        out_shape=[vmem((rows + 32, width), BF16), vmem((rows, 128), F32)],
        compiler_params=params(5),
        cost_estimate=cost(0.5, 2.0),
        name="attended_back",
    )(du1, grad_pre, down_one.T, attended, lse, wout_here)

    def query_back(groups, part):
        return pl.pallas_call(
            functools.partial(query_back_kernel, groups),
            in_specs=[VMEM] * 12,
            out_specs=[VMEM] * (len(groups) + 1),
            out_shape=[vmem((4 * rows, WIDE), BF16)] * len(groups) + [vmem((rows, width), F32)],
            compiler_params=params(5),
            cost_estimate=cost(1.0 * len(groups), 3.0),
            name=f"query_back_{groups[0]}",
        )(far, far_mate, q, kbuf, vbuf, bias_a, bias_b, lse, delta, pack, part, wq_here)

    def key_back(groups, qbufs, part, dtype):
        return pl.pallas_call(
            functools.partial(key_back_kernel, groups),
            in_specs=[VMEM] * (9 + len(groups)),
            out_specs=VMEM,
            out_shape=vmem((rows, width), dtype),
            compiler_params=params(5),
            cost_estimate=cost(1.0 * len(groups), 3.0),
            name=f"key_back_{groups[0]}",
        )(grads_row, stats_row, kbuf, vbuf, back_a, back_b, part, *qbufs, wk_here, wv_here)

    total = add(keep, after(swap_all(send, 1), pack))
    arrived = [swap_all(total[index], mask) for index, mask in ((1, 4), (2, 2), (3, 6))]
    pack_mate = swap(after(pack, total), 1)
    qbuf0, qbuf1, part = query_back((0, 1), after(du1, total))
    total = add(total[0], *lax.optimization_barrier((*arrived, part, pack_mate))[:3])
    masks = []
    while 8 << len(masks) < 4 * dp_size:
        masks.append(8 << len(masks))
    arrived = swap_all(total, masks[0])
    pack_now = after(pack, total)
    share = near_share(pack_now, pack_mate) + [pack_now[rows:]]
    pack_far = swap(jnp.concatenate(share, axis=0), 2)
    total = add(total, arrived)
    arrived = swap_all(total, masks[1])
    qbuf2, part = query_back((2,), after(part, total))
    pack_far, part = lax.optimization_barrier((pack_far, part))
    pack_far_mate = swap(pack_far, 1)
    total = add(total, after(arrived, part))
    for mask in masks[2:]:
        total = add(total, swap_all(total, mask))
    others = [swap_all(total, mask) for mask in (4, 2, 6)]
    grads_row, stats_row = pl.pallas_call(
        gather_kernel,
        in_specs=[VMEM] * 4,
        out_specs=[VMEM] * 2,
        out_shape=[vmem((4 * rows, width), BF16), vmem((64, LONG), F32)],
        compiler_params=params(3),
        cost_estimate=cost(0.1, 1.0),
        name="gather",
    )(pack, pack_mate, pack_far, after(pack_far_mate, total))
    part = key_back((0, 1), (qbuf0, qbuf1), after(part, total), F32)
    here = jnp.stack([total, *lax.optimization_barrier((*others, part))[:3]])
    other = swap_all(here, 1)
    input_grad = key_back((2,), (qbuf2,), after(part, here), BF16)

    grad_dims = ((adapt, width), (adapt,), (adapt, width), (width,), (width,), (width,)) * 2
    input_grad, *grads = pl.pallas_call(
        unpack_kernel,
        in_specs=[VMEM] * 3,
        out_specs=[HBM] * 13,
        out_shape=[shape((rows, width), BF16)] + [shape(dims, F32) for dims in grad_dims],
        scratch_shapes=[pltpu.VMEM(dims, F32) for dims in grad_dims]
        + [pltpu.SemaphoreType.DMA((13,))],
        compiler_params=params(5),
        name="unpack",
    )(here, other, input_grad)
    return (mixed.reshape(tokens.shape), input_grad.reshape(tokens.shape)) + tuple(
        grad.T if index in (0, 6) else grad for index, grad in enumerate(grads)
    )


def solution(mesh):
    in_specs = (
        (P("blk", "dp", None),) + (P(),) * 18 + (P("dp", None),) * 2 + (P("blk", "dp", None),)
    )
    out_specs = (P("blk", "dp", None),) * 2 + (P(),) * 12
    return jax.shard_map(
        functools.partial(body, mesh.shape["dp"]),
        mesh=mesh,
        in_specs=in_specs,
        out_specs=out_specs,
        check_vma=False,
    )
```

```python
import functools

import jax
import jax.numpy as jnp
from jax import lax
from jax.experimental import pallas as pl
from jax.experimental.pallas import tpu as pltpu
from jax.sharding import PartitionSpec as P

HEAD = 64
GROUP = 4
LONG_AT = 128
LONG = 512
ROWS_A = 64
WIDE = GROUP * HEAD
HALF = 256
SHARE = 128
CHUNK = 768
SMALL = 8
ROWS_B = 128
NEG = -1e30
F32 = jnp.float32
BF16 = jnp.bfloat16

VMEM = pl.BlockSpec(memory_space=pltpu.VMEM)
SMEM = pl.BlockSpec(memory_space=pltpu.SMEM)
HBM = pl.BlockSpec(memory_space=pltpu.HBM)


def nn(left, right):
    return lax.dot_general(left, right, (((1,), (0,)), ((), ())), preferred_element_type=F32)


def nt(left, right):
    return lax.dot_general(left, right, (((1,), (1,)), ((), ())), preferred_element_type=F32)


def tn(left, right):
    return lax.dot_general(left, right, (((0,), (0,)), ((), ())), preferred_element_type=F32)


def gelu_both(values):
    phi = 0.5 + 0.5 * lax.erf(values * 0.7071067811865476)
    bell = jnp.exp(-0.5 * values * values)
    return values * phi, phi + values * bell * 0.3989422804014327


def normed(values):
    centre = jnp.mean(values, axis=-1, keepdims=True)
    centred = values - centre
    spread = jnp.mean(centred * centred, axis=-1, keepdims=True)
    scale = lax.rsqrt(spread + 1e-06)
    return centred * scale, scale


def norm_back(incoming, gain, normal, scale):
    scaled = incoming * gain
    first = jnp.mean(scaled, axis=-1, keepdims=True)
    second = jnp.mean(scaled * normal, axis=-1, keepdims=True)
    return scale * (scaled - first - normal * second)


def row_of(ref):
    return ref[...].reshape(1, ref.shape[0])


def own_rows(block):
    return (
        pl.multiple_of(jnp.where(block == 0, 128, 0), 64),
        pl.multiple_of(jnp.where(block == 0, 0, 64), 64),
    )


def far_place(chip):
    return pl.multiple_of(LONG_AT + 2 * SHARE * (1 - chip), 128)


def near_places(block):
    chip = block // 2
    long_at = LONG_AT * (1 - chip)
    short_at = LONG_AT * chip
    outer = (block == 0) | (block == 3)
    return (
        pl.multiple_of(long_at, 128),
        pl.multiple_of(jnp.where(outer, short_at, long_at), 128),
    )


def far_tokens(core, far_ref, far_mate_ref):
    far, far_mate = far_ref[...], far_mate_ref[...]
    first = core == 0
    return jnp.concatenate(
        [jnp.where(first, far, far_mate), jnp.where(first, far_mate, far)], axis=0
    )


def partner_offset(block):
    return pl.multiple_of(jnp.where(block == 0, 0, jnp.where(block == 3, 256, 128)), 128)


def bounds(len_ref, valid_ref, places):
    low = jnp.zeros(places.shape, jnp.int32)
    high = jnp.zeros(places.shape, jnp.int32)
    start = jnp.int32(0)
    for slot in range(len_ref.shape[1]):
        end = start + len_ref[0, slot]
        inside = (places >= start) & (places < end)
        low = jnp.where(inside, start, low)
        high = jnp.where(inside, start + valid_ref[0, slot], high)
        start = end
    return low, high


def bias_of(len_ref, valid_ref, query_at, key_at, rows, columns=LONG):
    places = query_at + lax.broadcasted_iota(jnp.int32, (rows, 1), 0)
    low, high = bounds(len_ref, valid_ref, places)
    keys = key_at + lax.broadcasted_iota(jnp.int32, (rows, columns), 1)
    return jnp.where((keys >= low) & (keys < high), 0.0, NEG)


def bias_back_of(len_ref, valid_ref, key_at, query_at, rows):
    places = query_at + lax.broadcasted_iota(jnp.int32, (1, LONG), 1)
    low, high = bounds(len_ref, valid_ref, places)
    keys = key_at + lax.broadcasted_iota(jnp.int32, (rows, LONG), 0)
    return jnp.where((keys >= low) & (keys < high), 0.0, NEG)


def spread_heads(part):
    lane = lax.broadcasted_iota(jnp.int32, part.shape, 1) // HEAD
    return jnp.concatenate(
        [jnp.where(lane == head, part, jnp.zeros_like(part)) for head in range(GROUP)], axis=0
    )


def join_heads(stacked):
    rows = stacked.shape[0] // GROUP
    lane = lax.broadcasted_iota(jnp.int32, (rows, stacked.shape[1]), 1) // HEAD
    out = stacked[:rows]
    for head in range(1, GROUP):
        out = jnp.where(lane == head, stacked[head * rows : (head + 1) * rows], out)
    return out


def masked(scores, bias):
    split = scores.reshape((GROUP,) + bias.shape)
    return (split + bias).reshape(scores.shape)


def less_rows(stacked, rows):
    count = stacked.shape[0] // GROUP
    return jnp.concatenate(
        [stacked[head * count : (head + 1) * count] - rows[head : head + 1] for head in range(GROUP)],
        axis=0,
    )


def fetch_kernel(source, target, sem):
    copy = pltpu.make_async_copy(source, target, sem)
    copy.start()
    copy.wait()


def project_kernel(
    len_ref,
    valid_ref,
    own_ref,
    mate_ref,
    wq_hbm,
    wk_hbm,
    wv_hbm,
    wout_hbm,
    winner_hbm,
    *refs,
):
    rest = (len(refs) - 17) // 2
    smalls_hbm, refs, sems = refs[:rest], refs[rest:-1], refs[-1]
    project_rows(
        len_ref,
        valid_ref,
        own_ref,
        mate_ref,
        (wq_hbm, wk_hbm, wv_hbm, wout_hbm, winner_hbm),
        *refs[:16],
        tuple(zip(smalls_hbm, refs[16:])),
        sems,
    )


def project_rows(
    len_ref,
    valid_ref,
    own_ref,
    mate_ref,
    weights_hbm,
    q_ref,
    k_ref,
    v_ref,
    bias_a_ref,
    bias_b_ref,
    back_a_ref,
    back_b_ref,
    near_a_ref,
    near_b_ref,
    far_a_ref,
    far_b_ref,
    wq_ref,
    wk_ref,
    wv_ref,
    wout_ref,
    winner_ref,
    smalls,
    sems,
):
    weights = (wq_ref, wk_ref, wv_ref, wout_ref, winner_ref)
    moves = tuple(zip(weights_hbm, weights)) + smalls
    copies = [
        pltpu.make_async_copy(source, target, sems.at[index])
        for index, (source, target) in enumerate(moves)
    ]
    block = lax.axis_index("blk")

    @pl.when(block < 4)
    def _():
        for copy in copies:
            copy.start()

    core = block % 2
    rows = own_ref.shape[0]
    first = block * rows
    at_a, at_b = own_rows(block)
    meet_b = partner_offset(block)
    bias_a_ref[...] = bias_of(len_ref, valid_ref, first + at_a, LONG_AT, ROWS_A)
    bias_b_ref[...] = bias_of(len_ref, valid_ref, first + at_b, meet_b, ROWS_B)
    chip = block // 2
    near_a, near_b = near_places(block)
    pair_at = chip * 2 * rows
    far_at = far_place(chip)
    for at, count, near, near_ref, far_ref in (
        (at_a, ROWS_A, near_a, near_a_ref, far_a_ref),
        (at_b, ROWS_B, near_b, near_b_ref, far_b_ref),
    ):
        near_ref[...] = bias_of(len_ref, valid_ref, first + at, pair_at + near, count, HALF)
        far_ref[...] = bias_of(len_ref, valid_ref, first + at, far_at, count, HALF)
    back_a_ref[...] = bias_back_of(len_ref, valid_ref, first + at_a, LONG_AT, ROWS_A)
    back_b_ref[...] = bias_back_of(len_ref, valid_ref, first + at_b, meet_b, ROWS_B)
    mine = pl.multiple_of(core * rows, rows)
    other = pl.multiple_of((1 - core) * rows, rows)
    both = jnp.concatenate([own_ref[...], mate_ref[...]], axis=0)
    for copy, weight, out, scale in (
        (copies[0], wq_ref, q_ref, 0.125),
        (copies[1], wk_ref, k_ref, 1.0),
        (copies[2], wv_ref, v_ref, 1.0),
    ):
        copy.wait()
        product = (nn(both, weight[...]) * scale).astype(BF16)
        out[pl.ds(mine, rows), :] = product[:rows]
        out[pl.ds(other, rows), :] = product[rows:]
    for copy in copies[3:]:
        copy.wait()


def over_heads(stat):
    count = stat.shape[0] // GROUP
    parts = [stat[head * count : (head + 1) * count] for head in range(GROUP)]
    left = lax.broadcasted_iota(jnp.int32, (1, 128), 1) < HEAD
    return jnp.concatenate(
        [jnp.where(left, parts[0], parts[1]), jnp.where(left, parts[2], parts[3])], axis=1
    )


def near_kernel(
    far_ref,
    q_ref,
    kpair_ref,
    vpair_ref,
    near_a_ref,
    near_b_ref,
    wk_ref,
    wv_ref,
    kfar_ref,
    vfar_ref,
    sums_ref,
    tops_ref,
    totals_ref,
):
    kfar_ref[...] = nn(far_ref[...], wk_ref[...]).astype(BF16)
    vfar_ref[...] = nn(far_ref[...], wv_ref[...]).astype(BF16)
    block = lax.axis_index("blk")
    rows, width = sums_ref.shape
    core = block % 2
    at_a, at_b = own_rows(block)
    near_a, near_b = near_places(block)
    for at, count, near, bias_ref, at_stat in (
        (at_a, ROWS_A, near_a, near_a_ref, 0),
        (at_b, ROWS_B, near_b, near_b_ref, GROUP * ROWS_A),
    ):
        stacked = pl.ds(at_stat, GROUP * count)
        for group in range(width // WIDE):
            columns = slice(group * WIDE, (group + 1) * WIDE)
            queries = spread_heads(q_ref[pl.ds(core * rows + at, count), columns])
            scores = masked(nt(queries, kpair_ref[pl.ds(near, HALF), columns]), bias_ref[...])
            top = jnp.max(scores, axis=-1, keepdims=True)
            weights = jnp.exp(scores - top)
            total = jnp.sum(weights, axis=-1, keepdims=True)
            sums = nn(weights.astype(BF16), vpair_ref[pl.ds(near, HALF), columns])
            sums_ref[pl.ds(at, count), columns] = join_heads(sums)
            tops_ref[group, stacked, :] = jnp.broadcast_to(top, (GROUP * count, 128))
            totals_ref[group, stacked, :] = jnp.broadcast_to(total, (GROUP * count, 128))


def main_kernel(
    own_ref,
    far_mate_ref,
    q_ref,
    kpair_ref,
    vpair_ref,
    kfar_ref,
    vfar_ref,
    sums_ref,
    tops_ref,
    totals_ref,
    far_a_ref,
    far_b_ref,
    cot_ref,
    down1_ref,
    dbias1_ref,
    up1_ref,
    ubias1_ref,
    gain1_ref,
    shift1_ref,
    down2_ref,
    dbias2_ref,
    up2_ref,
    ubias2_ref,
    gain2_ref,
    shift2_ref,
    wk_ref,
    wv_ref,
    wout_ref,
    winner_ref,
    wouter_hbm,
    mixed_hbm,
    kbuf,
    vbuf,
    lse_ref,
    du1_ref,
    attended_ref,
    grad_pre_ref,
    keep_ref,
    send_ref,
    wouter_ref,
    wouter_t_ref,
    winner_t_ref,
    slope_ref,
    mixed_ref,
    sems,
):
    hidden_units = winner_ref.shape[1]

    def outer_copy(index):
        part = pl.ds(pl.multiple_of(index * CHUNK, CHUNK), CHUNK)
        return pltpu.make_async_copy(wouter_hbm.at[part], wouter_ref.at[part], sems.at[1 + index])

    @pl.loop(0, hidden_units // CHUNK)
    def _(index):
        outer_copy(index).start()

    mixed_copy = pltpu.make_async_copy(mixed_ref, mixed_hbm, sems.at[0])
    block = lax.axis_index("blk")
    core = block % 2
    chip = block // 2
    rows, width = own_ref.shape
    at_a, at_b = own_rows(block)

    def mine(ref):
        return jnp.concatenate([ref[pl.ds(at_a, ROWS_A), :], ref[pl.ds(at_b, ROWS_B), :]], axis=0)

    def put(ref, value):
        ref[pl.ds(at_a, ROWS_A), :] = value[:ROWS_A]
        ref[pl.ds(at_b, ROWS_B), :] = value[ROWS_A:]

    near = pl.multiple_of(chip * 2 * rows, 2 * rows)
    kbuf[pl.ds(near, 2 * rows), :] = kpair_ref[...]
    vbuf[pl.ds(near, 2 * rows), :] = vpair_ref[...]
    far_at = far_place(chip)
    far_first = pl.multiple_of(far_at + SHARE * core, 128)
    far_second = pl.multiple_of(far_at + SHARE * (1 - core), 128)
    kbuf[pl.ds(far_first, SHARE), :] = kfar_ref[...]
    vbuf[pl.ds(far_first, SHARE), :] = vfar_ref[...]
    kbuf[pl.ds(far_second, SHARE), :] = nn(far_mate_ref[...], wk_ref[...]).astype(BF16)
    vbuf[pl.ds(far_second, SHARE), :] = nn(far_mate_ref[...], wv_ref[...]).astype(BF16)

    lane = lax.broadcasted_iota(jnp.int32, (1, 128), 1)
    attended_parts = []
    lse_parts = []
    for at, count, bias_ref, at_stat in (
        (at_a, ROWS_A, far_a_ref, 0),
        (at_b, ROWS_B, far_b_ref, GROUP * ROWS_A),
    ):
        pieces = []
        lse = jnp.zeros((count, 128), F32)
        stacked = pl.ds(at_stat, GROUP * count)
        for group in range(width // WIDE):
            columns = slice(group * WIDE, (group + 1) * WIDE)
            queries = spread_heads(q_ref[pl.ds(core * rows + at, count), columns])
            scores = masked(nt(queries, kbuf[pl.ds(far_at, HALF), columns]), bias_ref[...])
            top_near = tops_ref[group, stacked, :]
            top = jnp.maximum(top_near, jnp.max(scores, axis=-1, keepdims=True))
            weights = jnp.exp(scores - jnp.concatenate([top, top], axis=1))
            shrink = jnp.exp(top_near - top)
            total = shrink * totals_ref[group, stacked, :] + jnp.sum(
                weights, axis=-1, keepdims=True
            )
            sums = join_heads(nn(weights.astype(BF16), vbuf[pl.ds(far_at, HALF), columns]))
            sums = sums + sums_ref[pl.ds(at, count), columns] * over_heads(shrink)
            pieces.append(sums * over_heads(1.0 / total))
            log_total = top + jnp.log(total)
            for head in range(GROUP):
                one = log_total[head * count : (head + 1) * count]
                lse = jnp.where(lane == group * GROUP + head, one, lse)
        attended_parts.append(jnp.concatenate(pieces, axis=1))
        lse_parts.append(lse)
    attended_f = jnp.concatenate(attended_parts, axis=0)
    put(lse_ref, jnp.concatenate(lse_parts, axis=0))
    put(attended_ref, attended_f)
    attended = attended_f.astype(BF16)
    branch = nn(attended, wout_ref[...]).astype(BF16)

    pre1 = nt(branch, down1_ref[...]) + row_of(dbias1_ref)
    inner1_f, slope1 = gelu_both(pre1)
    inner1 = inner1_f.astype(BF16)
    summed = (
        mine(own_ref).astype(F32) + branch.astype(F32) + nn(inner1, up1_ref[...]) + row_of(ubias1_ref)
    )
    normal1, scale1 = normed(summed)
    gain1 = row_of(gain1_ref)
    mid = (normal1 * gain1 + row_of(shift1_ref)).astype(BF16)

    for index in range(hidden_units // CHUNK):
        outer_copy(index).wait()
    ffn_f = jnp.zeros((rows, width), F32)
    for at in range(0, hidden_units, CHUNK):
        hidden_f, slope = gelu_both(nn(mid, winner_ref[:, at : at + CHUNK]))
        slope_ref[:, at : at + CHUNK] = slope
        wouter_t_ref[:, at : at + CHUNK] = wouter_ref[at : at + CHUNK, :].T
        winner_t_ref[at : at + CHUNK, :] = winner_ref[:, at : at + CHUNK].T
        ffn_f = ffn_f + nn(hidden_f.astype(BF16), wouter_ref[at : at + CHUNK, :])
    ffn = ffn_f.astype(BF16)

    pre2 = nt(ffn, down2_ref[...]) + row_of(dbias2_ref)
    inner2_f, slope2 = gelu_both(pre2)
    inner2 = inner2_f.astype(BF16)
    summed = mid.astype(F32) + ffn.astype(F32) + nn(inner2, up2_ref[...]) + row_of(ubias2_ref)
    normal2, scale2 = normed(summed)
    gain2 = row_of(gain2_ref)
    put(mixed_ref, (normal2 * gain2 + row_of(shift2_ref)).astype(BF16))
    mixed_copy.start()

    cot = mine(cot_ref).astype(F32)
    grad_gain2 = jnp.sum(cot * normal2, axis=0, keepdims=True)
    grad_shift2 = jnp.sum(cot, axis=0, keepdims=True)
    du2 = norm_back(cot, gain2, normal2, scale2)

    def adapter_back(source, up, inner, slope, incoming):
        out_grad = incoming.astype(BF16)
        grad_up = tn(inner, out_grad)
        grad_ubias = jnp.sum(out_grad.astype(F32), axis=0, keepdims=True)
        grad_pre = (nt(out_grad, up) * slope).astype(BF16)
        grad_down = tn(grad_pre, source)
        grad_dbias = jnp.sum(grad_pre.astype(F32), axis=0, keepdims=True)
        return grad_pre, grad_down, grad_dbias, grad_up, grad_ubias

    grad_pre2, grad_down2, grad_dbias2, grad_up2, grad_ubias2 = adapter_back(
        ffn, up2_ref[...], inner2, slope2, du2
    )
    dffn = (du2 + nn(grad_pre2, down2_ref[...])).astype(BF16)
    dmid = du2
    for at in range(0, hidden_units, CHUNK):
        dhidden = (nn(dffn, wouter_t_ref[:, at : at + CHUNK]) * slope_ref[:, at : at + CHUNK]).astype(
            BF16
        )
        dmid = dmid + nn(dhidden, winner_t_ref[at : at + CHUNK, :])

    grad_gain1 = jnp.sum(dmid * normal1, axis=0, keepdims=True)
    grad_shift1 = jnp.sum(dmid, axis=0, keepdims=True)
    du1 = norm_back(dmid, gain1, normal1, scale1)
    grad_pre1, grad_down1, grad_dbias1, grad_up1, grad_ubias1 = adapter_back(
        branch, up1_ref[...], inner1, slope1, du1
    )
    put(du1_ref, du1)
    put(grad_pre_ref, grad_pre1)

    blank = jnp.zeros((1, width), F32)
    both_dbias = jnp.concatenate(
        [
            grad_dbias1,
            jnp.zeros((1, 128 - grad_dbias1.shape[1]), F32),
            grad_dbias2,
            jnp.zeros((1, width - 128 - grad_dbias2.shape[1]), F32),
        ],
        axis=1,
    )
    quarters = (
        (grad_up1, grad_ubias1, both_dbias),
        (grad_down1, grad_gain1, grad_shift1),
        (grad_up2, grad_ubias2, blank),
        (grad_down2, grad_gain2, grad_shift2),
    )
    filler = jnp.zeros((SMALL - 2, width), F32)
    wholes = [
        jnp.concatenate([matrix, one, two, filler], axis=0).astype(BF16)
        for matrix, one, two in quarters
    ]
    side_here = lax.axis_index("dp") % 2
    for chip_of in range(2):
        even, odd = wholes[2 * chip_of], wholes[2 * chip_of + 1]
        kept = jnp.where(core == 0, even, odd)
        sent = jnp.where(core == 0, odd, even)
        for side in range(2):
            half = slice(side * width // 2, (side + 1) * width // 2)
            place = 2 * (chip ^ chip_of) + (side_here ^ side)
            keep_ref[place] = kept[:, half]
            send_ref[place] = sent[:, half]

    mixed_copy.wait()


def attended_back_kernel(
    du1_ref, grad_pre_ref, down1_ref, attended_ref, lse_ref, wout_ref, pack_ref, delta_ref
):
    rows, width = du1_ref.shape
    dbranch = (du1_ref[...] + nn(grad_pre_ref[...], down1_ref[...])).astype(BF16)
    dattended = nt(dbranch, wout_ref[...]).astype(BF16)
    pack_ref[:rows, :] = dattended
    product = dattended.astype(F32) * attended_ref[...]
    product_hi = product.astype(BF16)
    product_lo = (product - product_hi.astype(F32)).astype(BF16)
    head_of = lax.broadcasted_iota(jnp.int32, (128, width), 1) // HEAD
    picks = (head_of == lax.broadcasted_iota(jnp.int32, (128, width), 0)).astype(BF16)
    delta = nt(product_hi, picks) + nt(product_lo, picks)
    delta_ref[...] = delta
    blank = jnp.zeros((256 - rows, 128), F32)
    delta_rows = jnp.transpose(jnp.concatenate([delta, blank], axis=0))[:16]
    lse_rows = jnp.transpose(jnp.concatenate([lse_ref[...], blank], axis=0))[:16]

    def pieces_of(value, count):
        out = []
        for _ in range(count):
            piece = value.astype(BF16)
            value = value - piece.astype(F32)
            out.append(piece)
        return out

    pack_ref[rows : rows + 16, :] = jnp.concatenate(pieces_of(lse_rows, 3), axis=1)
    pack_ref[rows + 16 : rows + 32, :] = jnp.concatenate(
        pieces_of(delta_rows, 2) + [jnp.zeros((16, 256), BF16)], axis=1
    )


def query_back_kernel(
    groups,
    far_ref,
    far_mate_ref,
    q_ref,
    kbuf,
    vbuf,
    bias_a_ref,
    bias_b_ref,
    lse_ref,
    delta_ref,
    pack_ref,
    part_in_ref,
    wq_ref,
    *outs,
):
    block = lax.axis_index("blk")
    rows = q_ref.shape[0] // 2
    core, chip = block % 2, block // 2
    at_a, at_b = own_rows(block)
    meet_b = partner_offset(block)
    all_columns = slice(groups[0] * WIDE, (groups[-1] + 1) * WIDE)
    wq = wq_ref[:, all_columns]
    queries_far = (nn(far_tokens(core, far_ref, far_mate_ref), wq) * 0.125).astype(BF16)
    part_ref = outs[-1]
    for index, (group, qbuf) in enumerate(zip(groups, outs)):
        near = pl.ds(pl.multiple_of(chip * 2 * rows, rows), 2 * rows)
        qbuf[near, :] = q_ref[:, group * WIDE : (group + 1) * WIDE]
        qbuf[pl.ds(far_place(chip), 2 * SHARE), :] = queries_far[
            :, index * WIDE : (index + 1) * WIDE
        ]
    parts = []
    for at, count, meet, bias_ref in (
        (at_a, ROWS_A, LONG_AT, bias_a_ref),
        (at_b, ROWS_B, meet_b, bias_b_ref),
    ):
        lse = lse_ref[pl.ds(at, count), :]
        delta = delta_ref[pl.ds(at, count), :]
        pieces = []
        for group in groups:
            columns = slice(group * WIDE, (group + 1) * WIDE)
            heads = range(group * GROUP, (group + 1) * GROUP)
            log_total = jnp.concatenate([lse[:, head : head + 1] for head in heads], axis=0)
            deltas = jnp.concatenate([delta[:, head : head + 1] for head in heads], axis=0)
            keys = kbuf[pl.ds(meet, LONG), columns]
            scores = nt(spread_heads(q_ref[pl.ds(core * rows + at, count), columns]), keys)
            scores = masked(scores, bias_ref[...])
            probs = jnp.exp(scores - log_total)
            dprobs = nt(
                spread_heads(pack_ref[pl.ds(at, count), columns]), vbuf[pl.ds(meet, LONG), columns]
            )
            dscores = (probs * (dprobs - deltas)).astype(BF16)
            pieces.append(join_heads(nn(dscores, keys)).astype(BF16))
        parts.append(jnp.concatenate(pieces, axis=1))
    added = nt(jnp.concatenate(parts, axis=0), wq) * 0.125
    for at, rows_of in ((at_a, slice(0, ROWS_A)), (at_b, slice(ROWS_A, rows))):
        place = pl.ds(at, rows_of.stop - rows_of.start)
        part_ref[place, :] = part_in_ref[place, :] + added[rows_of]


def gather_kernel(own_ref, mate_ref, far_ref, far_mate_ref, grads_ref, stats_ref):
    block = lax.axis_index("blk")
    rows = own_ref.shape[0] - 32
    core, chip = block % 2, block // 2
    meet_b = partner_offset(block)
    grads_ref[pl.ds(pl.multiple_of(block * rows, rows), rows), :] = own_ref[:rows, :]
    grads_ref[pl.ds(pl.multiple_of((block ^ 1) * rows, rows), rows), :] = mate_ref[:rows, :]
    far_at = far_place(chip)
    far_first = pl.multiple_of(far_at + SHARE * core, 128)
    far_second = pl.multiple_of(far_at + SHARE * (1 - core), 128)
    grads_ref[pl.ds(far_first, SHARE), :] = far_ref[:SHARE, :]
    grads_ref[pl.ds(far_second, SHARE), :] = far_mate_ref[:SHARE, :]
    stats = []
    for ref, at in ((own_ref, rows), (mate_ref, rows), (far_ref, SHARE), (far_mate_ref, SHARE)):
        lse = ref[at : at + 16, :].astype(F32)
        delta = ref[at + 16 : at + 32, :].astype(F32)
        stats.append(
            jnp.concatenate(
                [
                    lse[:, :256] + (lse[:, 256:512] + lse[:, 512:]),
                    delta[:, :256] + delta[:, 256:512],
                ],
                axis=0,
            )[:, :rows]
        )
    ordered = []
    for place in range(4):
        pick = stats[place]
        for index in range(4):
            if index != place:
                pick = jnp.where(block ^ index == place, stats[index], pick)
        ordered.append(pick)
    whole = jnp.concatenate(ordered, axis=1)
    stats_ref[:32, :] = whole[:, LONG_AT : LONG_AT + LONG]
    here = whole[:, :LONG]
    for start in (128, 256):
        here = jnp.where(meet_b == start, whole[:, start : start + LONG], here)
    stats_ref[32:, :] = here


def key_back_kernel(groups, grads_ref, stats_ref, kbuf, vbuf, back_a_ref, back_b_ref, part_ref, *refs):
    qbufs, (wk_ref, wv_ref, out_ref) = refs[:-3], refs[-3:]
    block = lax.axis_index("blk")
    rows = out_ref.shape[0]
    at_a, at_b = own_rows(block)
    first = block * rows
    all_columns = slice(groups[0] * WIDE, (groups[-1] + 1) * WIDE)
    parts = []
    for at, count, meet, bias_ref, at_stats in (
        (at_a, ROWS_A, LONG_AT, back_a_ref, 0),
        (at_b, ROWS_B, partner_offset(block), back_b_ref, 32),
    ):
        own_at = pl.multiple_of(first + at, 64)
        dkeys, dvalues = [], []
        for group, qbuf in zip(groups, qbufs):
            columns = slice(group * WIDE, (group + 1) * WIDE)
            at_lse = at_stats + group * GROUP
            at_delta = at_lse + 16
            queries = qbuf[pl.ds(meet, LONG), :]
            grads = grads_ref[pl.ds(meet, LONG), columns]
            scores = nt(spread_heads(kbuf[pl.ds(own_at, count), columns]), queries)
            scores = masked(scores, bias_ref[...])
            probs = jnp.exp(less_rows(scores, stats_ref[at_lse : at_lse + GROUP, :]))
            dprobs = nt(spread_heads(vbuf[pl.ds(own_at, count), columns]), grads)
            dprobs = less_rows(dprobs, stats_ref[at_delta : at_delta + GROUP, :])
            dscores = (probs * dprobs).astype(BF16)
            dkeys.append(join_heads(nn(dscores, queries)).astype(BF16))
            dvalues.append(join_heads(nn(probs.astype(BF16), grads)).astype(BF16))
        parts.append((jnp.concatenate(dkeys, axis=1), jnp.concatenate(dvalues, axis=1)))
    dkey, dvalue = (jnp.concatenate(both, axis=0) for both in zip(*parts))
    added = nt(dkey, wk_ref[:, all_columns]) + nt(dvalue, wv_ref[:, all_columns])
    for at, rows_of in ((at_a, slice(0, ROWS_A)), (at_b, slice(ROWS_A, rows))):
        place = pl.ds(at, rows_of.stop - rows_of.start)
        out_ref[place, :] = (part_ref[place, :] + added[rows_of]).astype(out_ref.dtype)


def unpack_kernel(here_ref, other_ref, grad_ref, *refs):
    places, outs, sems = refs[:13], refs[13:25], refs[25]
    block = lax.axis_index("blk")
    side_here = lax.axis_index("dp") % 2
    core, chip = block % 2, block // 2
    adapt = outs[0].shape[0]
    copies = [
        pltpu.make_async_copy(source, target, sems.at[index])
        for index, (source, target) in enumerate(zip((grad_ref, *outs), places))
    ]
    copies[0].start()
    matrices = (2, 0, 8, 6)
    vectors = ((3,), (4, 5), (9,), (10, 11))
    for index in range(4):
        halves = []
        for side in range(2):
            place = 2 * (chip ^ (index // 2)) + (side_here ^ side)
            halves.append(jnp.where(core == index % 2, here_ref[place], other_ref[place]))
        whole = jnp.concatenate(halves, axis=1).astype(F32)
        outs[matrices[index]][...] = whole[:adapt]
        ready = [matrices[index], *vectors[index]]
        for row, vector in enumerate(vectors[index]):
            outs[vector][...] = whole[adapt + row]
        if index == 0:
            outs[1][...] = whole[adapt + 1, :adapt]
            outs[7][...] = whole[adapt + 1, 128 : 128 + adapt]
            ready += [1, 7]
        for out in ready:
            copies[1 + out].start()
    for copy in copies:
        copy.wait()


def params(megabytes):
    return pltpu.CompilerParams(vmem_limit_bytes=megabytes << 20)


def cost(gigaflop, megabytes):
    return pl.CostEstimate(
        flops=int(gigaflop * 1e9), bytes_accessed=int(megabytes * 1e6), transcendentals=0
    )


def after(array, *others):
    return lax.optimization_barrier((array,) + others)[0]


def vmem(dims, dtype):
    return pltpu.VMEM(dims, dtype)


def in_hbm(array):
    return pltpu.with_memory_space_constraint(array, pltpu.HBM)


def shape(dims, dtype):
    return jax.ShapeDtypeStruct(dims, dtype)


def body(
    dp_size,
    tokens,
    w_query,
    w_key,
    w_value,
    w_out,
    w_inner,
    w_outer,
    down_one,
    dbias_one,
    up_one,
    ubias_one,
    gain_one,
    shift_one,
    down_two,
    dbias_two,
    up_two,
    ubias_two,
    gain_two,
    shift_two,
    seg_len,
    seg_valid,
    cotangent,
):
    rows, _, width = tokens.shape
    adapt = up_one.shape[0]
    hidden = w_inner.shape[1]
    block = lax.axis_index("blk")
    own = tokens.reshape(rows, width)
    cot = cotangent.reshape(rows, width)

    def swap(array, mask):
        return lax.ppermute(array, "blk", [(i, i ^ mask) for i in range(4)])

    def swap_all(array, mask):
        return lax.ppermute(
            array, ("dp", "blk"), [(i, i ^ mask) for i in range(4 * dp_size)]
        )

    mate = swap(own, 1)
    own = pl.pallas_call(
        fetch_kernel,
        in_specs=[HBM],
        out_specs=VMEM,
        out_shape=vmem((rows, width), BF16),
        scratch_shapes=[pltpu.SemaphoreType.DMA],
        compiler_params=params(1),
        cost_estimate=cost(0.1, 1.0),
        name="fetch",
    )(in_hbm(own))
    def near_share(own, mate):
        choices = (
            (own[128:192], own[64:128], own[:64], mate[128:192]),
            (mate[:64], own[128:192], own[64:128], own[:64]),
        )
        halves = []
        for options in choices:
            half = options[0]
            for index in range(1, 4):
                half = jnp.where(block == index, options[index], half)
            halves.append(half)
        return halves

    far = swap(jnp.concatenate(near_share(own, mate), axis=0), 2)
    smalls = (
        cot,
        down_one.T,
        dbias_one,
        up_one,
        ubias_one,
        gain_one,
        shift_one,
        down_two.T,
        dbias_two,
        up_two,
        ubias_two,
        gain_two,
        shift_two,
    )
    half_mask_shapes = [vmem((count, HALF), F32) for count in (ROWS_A, ROWS_B)] * 2
    mask_shapes = [vmem((count, LONG), F32) for count in (ROWS_A, ROWS_B)] * 2
    (
        q,
        kpair,
        vpair,
        bias_a,
        bias_b,
        back_a,
        back_b,
        near_a,
        near_b,
        far_a,
        far_b,
        wq_here,
        wk_here,
        wv_here,
        wout_here,
        winner_here,
        *smalls_here,
    ) = pl.pallas_call(
        project_kernel,
        in_specs=[SMEM] * 2 + [VMEM] * 2 + [HBM] * (5 + len(smalls)),
        out_specs=[VMEM] * (16 + len(smalls)),
        out_shape=[vmem((2 * rows, width), BF16)] * 3
        + mask_shapes
        + half_mask_shapes
        + [vmem((width, width), BF16)] * 4
        + [vmem((width, hidden), BF16)]
        + [vmem(small.shape, small.dtype) for small in smalls],
        scratch_shapes=[pltpu.SemaphoreType.DMA((5 + len(smalls),))],
        compiler_params=params(4),
        cost_estimate=cost(2.0, 12.0),
        name="project",
    )(
        in_hbm(seg_len),
        in_hbm(seg_valid),
        own,
        mate,
        in_hbm(w_query),
        in_hbm(w_key),
        in_hbm(w_value),
        in_hbm(w_out),
        in_hbm(w_inner),
        *(in_hbm(small) for small in smalls),
    )
    far_mate = swap(after(far, q), 1)
    kfar, vfar, sums, tops, totals = pl.pallas_call(
        near_kernel,
        in_specs=[VMEM] * 8,
        out_specs=[VMEM] * 5,
        out_shape=[vmem((SHARE, width), BF16)] * 2
        + [vmem((rows, width), F32)]
        + [vmem((width // WIDE, GROUP * rows, 128), F32)] * 2,
        compiler_params=params(5),
        cost_estimate=cost(1.0, 2.0),
        name="near",
    )(far, q, kpair, vpair, near_a, near_b, wk_here, wv_here)

    part_rows = adapt + SMALL
    mixed, kbuf, vbuf, lse, du1, attended, grad_pre, keep, send = pl.pallas_call(
        main_kernel,
        in_specs=[VMEM] * 29 + [HBM],
        out_specs=[HBM] + [VMEM] * 8,
        out_shape=[
            shape((rows, width), BF16),
            vmem((4 * rows, width), BF16),
            vmem((4 * rows, width), BF16),
            vmem((rows, 128), F32),
            vmem((rows, width), F32),
            vmem((rows, width), F32),
            vmem((rows, adapt), BF16),
            vmem((4, part_rows, width // 2), BF16),
            vmem((4, part_rows, width // 2), BF16),
        ],
        scratch_shapes=[
            pltpu.VMEM((hidden, width), BF16),
            pltpu.VMEM((width, hidden), BF16),
            pltpu.VMEM((hidden, width), BF16),
            pltpu.VMEM((rows, hidden), F32),
            pltpu.VMEM((rows, width), BF16),
            pltpu.SemaphoreType.DMA((1 + hidden // CHUNK,)),
        ],
        compiler_params=params(22),
        cost_estimate=cost(8.0, 20.0),
        name="layer",
    )(
        own,
        far_mate,
        q,
        kpair,
        vpair,
        kfar,
        vfar,
        sums,
        tops,
        totals,
        far_a,
        far_b,
        *smalls_here,
        wk_here,
        wv_here,
        wout_here,
        winner_here,
        in_hbm(w_outer),
    )

    def add(*terms):
        return functools.reduce(jnp.add, [term.astype(F32) for term in terms]).astype(BF16)

    pack, delta = pl.pallas_call(
        attended_back_kernel,
        in_specs=[VMEM] * 6,
        out_specs=[VMEM] * 2,
        out_shape=[vmem((rows + 32, width), BF16), vmem((rows, 128), F32)],
        compiler_params=params(5),
        cost_estimate=cost(0.5, 2.0),
        name="attended_back",
    )(du1, grad_pre, smalls_here[1], attended, lse, wout_here)

    def query_back(groups, part):
        return pl.pallas_call(
            functools.partial(query_back_kernel, groups),
            in_specs=[VMEM] * 12,
            out_specs=[VMEM] * (len(groups) + 1),
            out_shape=[vmem((4 * rows, WIDE), BF16)] * len(groups) + [vmem((rows, width), F32)],
            compiler_params=params(5),
            cost_estimate=cost(1.0 * len(groups), 3.0),
            name=f"query_back_{groups[0]}",
        )(far, far_mate, q, kbuf, vbuf, bias_a, bias_b, lse, delta, pack, part, wq_here)

    def key_back(groups, qbufs, part, dtype):
        return pl.pallas_call(
            functools.partial(key_back_kernel, groups),
            in_specs=[VMEM] * (9 + len(groups)),
            out_specs=VMEM,
            out_shape=vmem((rows, width), dtype),
            compiler_params=params(5),
            cost_estimate=cost(1.0 * len(groups), 3.0),
            name=f"key_back_{groups[0]}",
        )(grads_row, stats_row, kbuf, vbuf, back_a, back_b, part, *qbufs, wk_here, wv_here)

    total = add(keep, after(swap_all(send, 1), pack))
    arrived = [swap_all(total[index], mask) for index, mask in ((1, 4), (2, 2), (3, 6))]
    pack_mate = swap(after(pack, total), 1)
    qbuf0, qbuf1, part = query_back((0, 1), after(du1, total))
    total = add(total[0], *lax.optimization_barrier((*arrived, part, pack_mate))[:3])
    masks = []
    while 8 << len(masks) < 4 * dp_size:
        masks.append(8 << len(masks))
    arrived = swap_all(total, masks[0])
    pack_now = after(pack, total)
    share = near_share(pack_now, pack_mate) + [pack_now[rows:]]
    pack_far = swap(jnp.concatenate(share, axis=0), 2)
    total = add(total, arrived)
    arrived = swap_all(total, masks[1])
    qbuf2, part = query_back((2,), after(part, total))
    pack_far, part = lax.optimization_barrier((pack_far, part))
    pack_far_mate = swap(pack_far, 1)
    total = add(total, after(arrived, part))
    for mask in masks[2:]:
        total = add(total, swap_all(total, mask))
    others = [swap_all(total, mask) for mask in (4, 2, 6)]
    grads_row, stats_row = pl.pallas_call(
        gather_kernel,
        in_specs=[VMEM] * 4,
        out_specs=[VMEM] * 2,
        out_shape=[vmem((4 * rows, width), BF16), vmem((64, LONG), F32)],
        compiler_params=params(3),
        cost_estimate=cost(0.1, 1.0),
        name="gather",
    )(pack, pack_mate, pack_far, after(pack_far_mate, total))
    part = key_back((0, 1), (qbuf0, qbuf1), after(part, total), F32)
    here = jnp.stack([total, *lax.optimization_barrier((*others, part))[:3]])
    other = swap_all(here, 1)
    input_grad = key_back((2,), (qbuf2,), after(part, here), BF16)

    grad_dims = ((adapt, width), (adapt,), (adapt, width), (width,), (width,), (width,)) * 2
    input_grad, *grads = pl.pallas_call(
        unpack_kernel,
        in_specs=[VMEM] * 3,
        out_specs=[HBM] * 13,
        out_shape=[shape((rows, width), BF16)] + [shape(dims, F32) for dims in grad_dims],
        scratch_shapes=[pltpu.VMEM(dims, F32) for dims in grad_dims]
        + [pltpu.SemaphoreType.DMA((13,))],
        compiler_params=params(5),
        name="unpack",
    )(here, other, input_grad)
    return (mixed.reshape(tokens.shape), input_grad.reshape(tokens.shape)) + tuple(
        grad.T if index in (0, 6) else grad for index, grad in enumerate(grads)
    )


def solution(mesh):
    in_specs = (
        (P("blk", "dp", None),) + (P(),) * 18 + (P("dp", None),) * 2 + (P("blk", "dp", None),)
    )
    out_specs = (P("blk", "dp", None),) * 2 + (P(),) * 12
    return jax.shard_map(
        functools.partial(body, mesh.shape["dp"]),
        mesh=mesh,
        in_specs=in_specs,
        out_specs=out_specs,
        check_vma=False,
    )
```

```python
import functools

import jax
import jax.numpy as jnp
from jax import lax
from jax.experimental import pallas as pl
from jax.experimental.pallas import tpu as pltpu
from jax.sharding import PartitionSpec as P

HEAD = 64
GROUP = 4
LONG_AT = 128
LONG = 512
ROWS_A = 64
WIDE = GROUP * HEAD
HALF = 256
SHARE = 128
CHUNK = 768
ROWS_B = 128
NEG = -1e30
F32 = jnp.float32
BF16 = jnp.bfloat16

VMEM = pl.BlockSpec(memory_space=pltpu.VMEM)
SMEM = pl.BlockSpec(memory_space=pltpu.SMEM)
HBM = pl.BlockSpec(memory_space=pltpu.HBM)


def nn(left, right):
    return lax.dot_general(left, right, (((1,), (0,)), ((), ())), preferred_element_type=F32)


def nt(left, right):
    return lax.dot_general(left, right, (((1,), (1,)), ((), ())), preferred_element_type=F32)


def tn(left, right):
    return lax.dot_general(left, right, (((0,), (0,)), ((), ())), preferred_element_type=F32)


def gelu_both(values):
    phi = 0.5 + 0.5 * lax.erf(values * 0.7071067811865476)
    bell = jnp.exp(-0.5 * values * values)
    return values * phi, phi + values * bell * 0.3989422804014327


def normed(values):
    centre = jnp.mean(values, axis=-1, keepdims=True)
    centred = values - centre
    spread = jnp.mean(centred * centred, axis=-1, keepdims=True)
    scale = lax.rsqrt(spread + 1e-06)
    return centred * scale, scale


def norm_back(incoming, gain, normal, scale):
    scaled = incoming * gain
    first = jnp.mean(scaled, axis=-1, keepdims=True)
    second = jnp.mean(scaled * normal, axis=-1, keepdims=True)
    return scale * (scaled - first - normal * second)


def row_of(ref):
    return ref[...].reshape(1, ref.shape[0])


def own_rows(block):
    return (
        pl.multiple_of(jnp.where(block == 0, 128, 0), 64),
        pl.multiple_of(jnp.where(block == 0, 0, 64), 64),
    )


def far_place(chip):
    return pl.multiple_of(LONG_AT + 2 * SHARE * (1 - chip), 128)


def near_places(block):
    chip = block // 2
    long_at = LONG_AT * (1 - chip)
    short_at = LONG_AT * chip
    outer = (block == 0) | (block == 3)
    return (
        pl.multiple_of(long_at, 128),
        pl.multiple_of(jnp.where(outer, short_at, long_at), 128),
    )


def far_tokens(core, far_ref, far_mate_ref):
    far, far_mate = far_ref[...], far_mate_ref[...]
    first = core == 0
    return jnp.concatenate(
        [jnp.where(first, far, far_mate), jnp.where(first, far_mate, far)], axis=0
    )


def partner_offset(block):
    return pl.multiple_of(jnp.where(block == 0, 0, jnp.where(block == 3, 256, 128)), 128)


def bounds(len_ref, valid_ref, places):
    low = jnp.zeros(places.shape, jnp.int32)
    high = jnp.zeros(places.shape, jnp.int32)
    start = jnp.int32(0)
    for slot in range(len_ref.shape[1]):
        end = start + len_ref[0, slot]
        inside = (places >= start) & (places < end)
        low = jnp.where(inside, start, low)
        high = jnp.where(inside, start + valid_ref[0, slot], high)
        start = end
    return low, high


def bias_of(len_ref, valid_ref, query_at, key_at, rows, columns=LONG):
    places = query_at + lax.broadcasted_iota(jnp.int32, (rows, 1), 0)
    low, high = bounds(len_ref, valid_ref, places)
    keys = key_at + lax.broadcasted_iota(jnp.int32, (rows, columns), 1)
    return jnp.where((keys >= low) & (keys < high), 0.0, NEG)


def bias_back_of(len_ref, valid_ref, key_at, query_at, rows):
    places = query_at + lax.broadcasted_iota(jnp.int32, (1, LONG), 1)
    low, high = bounds(len_ref, valid_ref, places)
    keys = key_at + lax.broadcasted_iota(jnp.int32, (rows, LONG), 0)
    return jnp.where((keys >= low) & (keys < high), 0.0, NEG)


def spread_heads(part):
    lane = lax.broadcasted_iota(jnp.int32, part.shape, 1) // HEAD
    return jnp.concatenate(
        [jnp.where(lane == head, part, jnp.zeros_like(part)) for head in range(GROUP)], axis=0
    )


def join_heads(stacked):
    rows = stacked.shape[0] // GROUP
    lane = lax.broadcasted_iota(jnp.int32, (rows, stacked.shape[1]), 1) // HEAD
    out = stacked[:rows]
    for head in range(1, GROUP):
        out = jnp.where(lane == head, stacked[head * rows : (head + 1) * rows], out)
    return out


def masked(scores, bias):
    split = scores.reshape((GROUP,) + bias.shape)
    return (split + bias).reshape(scores.shape)


def less_rows(stacked, rows):
    count = stacked.shape[0] // GROUP
    return jnp.concatenate(
        [stacked[head * count : (head + 1) * count] - rows[head : head + 1] for head in range(GROUP)],
        axis=0,
    )


def fetch_kernel(source, target, sem):
    copy = pltpu.make_async_copy(source, target, sem)
    copy.start()
    copy.wait()


def project_kernel(
    len_ref,
    valid_ref,
    own_ref,
    mate_ref,
    wq_hbm,
    wk_hbm,
    wv_hbm,
    wout_hbm,
    winner_hbm,
    *refs,
):
    rest = (len(refs) - 17) // 2
    smalls_hbm, refs, sems = refs[:rest], refs[rest:-1], refs[-1]
    project_rows(
        len_ref,
        valid_ref,
        own_ref,
        mate_ref,
        (wq_hbm, wk_hbm, wv_hbm, wout_hbm, winner_hbm),
        *refs[:16],
        tuple(zip(smalls_hbm, refs[16:])),
        sems,
    )


def project_rows(
    len_ref,
    valid_ref,
    own_ref,
    mate_ref,
    weights_hbm,
    q_ref,
    k_ref,
    v_ref,
    bias_a_ref,
    bias_b_ref,
    back_a_ref,
    back_b_ref,
    near_a_ref,
    near_b_ref,
    far_a_ref,
    far_b_ref,
    wq_ref,
    wk_ref,
    wv_ref,
    wout_ref,
    winner_ref,
    smalls,
    sems,
):
    weights = (wq_ref, wk_ref, wv_ref, wout_ref, winner_ref)
    moves = tuple(zip(weights_hbm, weights)) + smalls
    copies = [
        pltpu.make_async_copy(source, target, sems.at[index])
        for index, (source, target) in enumerate(moves)
    ]
    block = lax.axis_index("blk")

    @pl.when(block < 4)
    def _():
        for copy in copies:
            copy.start()

    core = block % 2
    rows = own_ref.shape[0]
    first = block * rows
    at_a, at_b = own_rows(block)
    meet_b = partner_offset(block)
    bias_a_ref[...] = bias_of(len_ref, valid_ref, first + at_a, LONG_AT, ROWS_A)
    bias_b_ref[...] = bias_of(len_ref, valid_ref, first + at_b, meet_b, ROWS_B)
    chip = block // 2
    near_a, near_b = near_places(block)
    pair_at = chip * 2 * rows
    far_at = far_place(chip)
    for at, count, near, near_ref, far_ref in (
        (at_a, ROWS_A, near_a, near_a_ref, far_a_ref),
        (at_b, ROWS_B, near_b, near_b_ref, far_b_ref),
    ):
        near_ref[...] = bias_of(len_ref, valid_ref, first + at, pair_at + near, count, HALF)
        far_ref[...] = bias_of(len_ref, valid_ref, first + at, far_at, count, HALF)
    back_a_ref[...] = bias_back_of(len_ref, valid_ref, first + at_a, LONG_AT, ROWS_A)
    back_b_ref[...] = bias_back_of(len_ref, valid_ref, first + at_b, meet_b, ROWS_B)
    mine = pl.multiple_of(core * rows, rows)
    other = pl.multiple_of((1 - core) * rows, rows)
    both = jnp.concatenate([own_ref[...], mate_ref[...]], axis=0)
    for copy, weight, out, scale in (
        (copies[0], wq_ref, q_ref, 0.125),
        (copies[1], wk_ref, k_ref, 1.0),
        (copies[2], wv_ref, v_ref, 1.0),
    ):
        copy.wait()
        product = (nn(both, weight[...]) * scale).astype(BF16)
        out[pl.ds(mine, rows), :] = product[:rows]
        out[pl.ds(other, rows), :] = product[rows:]
    for copy in copies[3:]:
        copy.wait()


def over_heads(stat):
    count = stat.shape[0] // GROUP
    parts = [stat[head * count : (head + 1) * count] for head in range(GROUP)]
    left = lax.broadcasted_iota(jnp.int32, (1, 128), 1) < HEAD
    return jnp.concatenate(
        [jnp.where(left, parts[0], parts[1]), jnp.where(left, parts[2], parts[3])], axis=1
    )


def near_kernel(
    far_ref,
    q_ref,
    kpair_ref,
    vpair_ref,
    near_a_ref,
    near_b_ref,
    wk_ref,
    wv_ref,
    kfar_ref,
    vfar_ref,
    sums_ref,
    tops_ref,
    totals_ref,
):
    kfar_ref[...] = nn(far_ref[...], wk_ref[...]).astype(BF16)
    vfar_ref[...] = nn(far_ref[...], wv_ref[...]).astype(BF16)
    block = lax.axis_index("blk")
    rows, width = sums_ref.shape
    core = block % 2
    at_a, at_b = own_rows(block)
    near_a, near_b = near_places(block)
    for at, count, near, bias_ref, at_stat in (
        (at_a, ROWS_A, near_a, near_a_ref, 0),
        (at_b, ROWS_B, near_b, near_b_ref, GROUP * ROWS_A),
    ):
        stacked = pl.ds(at_stat, GROUP * count)
        for group in range(width // WIDE):
            columns = slice(group * WIDE, (group + 1) * WIDE)
            queries = spread_heads(q_ref[pl.ds(core * rows + at, count), columns])
            scores = masked(nt(queries, kpair_ref[pl.ds(near, HALF), columns]), bias_ref[...])
            top = jnp.max(scores, axis=-1, keepdims=True)
            weights = jnp.exp(scores - top)
            total = jnp.sum(weights, axis=-1, keepdims=True)
            sums = nn(weights.astype(BF16), vpair_ref[pl.ds(near, HALF), columns])
            sums_ref[pl.ds(at, count), columns] = join_heads(sums)
            tops_ref[group, stacked, :] = jnp.broadcast_to(top, (GROUP * count, 128))
            totals_ref[group, stacked, :] = jnp.broadcast_to(total, (GROUP * count, 128))


def main_kernel(
    own_ref,
    far_mate_ref,
    q_ref,
    kpair_ref,
    vpair_ref,
    kfar_ref,
    vfar_ref,
    sums_ref,
    tops_ref,
    totals_ref,
    far_a_ref,
    far_b_ref,
    cot_ref,
    down1_ref,
    dbias1_ref,
    up1_ref,
    ubias1_ref,
    gain1_ref,
    shift1_ref,
    down2_ref,
    dbias2_ref,
    up2_ref,
    ubias2_ref,
    gain2_ref,
    shift2_ref,
    wk_ref,
    wv_ref,
    wout_ref,
    winner_ref,
    wouter_hbm,
    mixed_hbm,
    kbuf,
    vbuf,
    lse_ref,
    du1_ref,
    attended_ref,
    grad_pre_ref,
    keep_ref,
    send_ref,
    wouter_ref,
    wouter_t_ref,
    winner_t_ref,
    slope_ref,
    mixed_ref,
    sems,
):
    hidden_units = winner_ref.shape[1]

    def outer_copy(index):
        part = pl.ds(pl.multiple_of(index * CHUNK, CHUNK), CHUNK)
        return pltpu.make_async_copy(wouter_hbm.at[part], wouter_ref.at[part], sems.at[1 + index])

    @pl.loop(0, hidden_units // CHUNK)
    def _(index):
        outer_copy(index).start()

    mixed_copy = pltpu.make_async_copy(mixed_ref, mixed_hbm, sems.at[0])
    block = lax.axis_index("blk")
    core = block % 2
    chip = block // 2
    rows, width = own_ref.shape
    at_a, at_b = own_rows(block)

    def mine(ref):
        return jnp.concatenate([ref[pl.ds(at_a, ROWS_A), :], ref[pl.ds(at_b, ROWS_B), :]], axis=0)

    def put(ref, value):
        ref[pl.ds(at_a, ROWS_A), :] = value[:ROWS_A]
        ref[pl.ds(at_b, ROWS_B), :] = value[ROWS_A:]

    near = pl.multiple_of(chip * 2 * rows, 2 * rows)
    kbuf[pl.ds(near, 2 * rows), :] = kpair_ref[...]
    vbuf[pl.ds(near, 2 * rows), :] = vpair_ref[...]
    far_at = far_place(chip)
    far_first = pl.multiple_of(far_at + SHARE * core, 128)
    far_second = pl.multiple_of(far_at + SHARE * (1 - core), 128)
    kbuf[pl.ds(far_first, SHARE), :] = kfar_ref[...]
    vbuf[pl.ds(far_first, SHARE), :] = vfar_ref[...]
    kbuf[pl.ds(far_second, SHARE), :] = nn(far_mate_ref[...], wk_ref[...]).astype(BF16)
    vbuf[pl.ds(far_second, SHARE), :] = nn(far_mate_ref[...], wv_ref[...]).astype(BF16)

    lane = lax.broadcasted_iota(jnp.int32, (1, 128), 1)
    attended_parts = []
    lse_parts = []
    for at, count, bias_ref, at_stat in (
        (at_a, ROWS_A, far_a_ref, 0),
        (at_b, ROWS_B, far_b_ref, GROUP * ROWS_A),
    ):
        pieces = []
        lse = jnp.zeros((count, 128), F32)
        stacked = pl.ds(at_stat, GROUP * count)
        for group in range(width // WIDE):
            columns = slice(group * WIDE, (group + 1) * WIDE)
            queries = spread_heads(q_ref[pl.ds(core * rows + at, count), columns])
            scores = masked(nt(queries, kbuf[pl.ds(far_at, HALF), columns]), bias_ref[...])
            top_near = tops_ref[group, stacked, :]
            top = jnp.maximum(top_near, jnp.max(scores, axis=-1, keepdims=True))
            weights = jnp.exp(scores - jnp.concatenate([top, top], axis=1))
            shrink = jnp.exp(top_near - top)
            total = shrink * totals_ref[group, stacked, :] + jnp.sum(
                weights, axis=-1, keepdims=True
            )
            sums = join_heads(nn(weights.astype(BF16), vbuf[pl.ds(far_at, HALF), columns]))
            sums = sums + sums_ref[pl.ds(at, count), columns] * over_heads(shrink)
            pieces.append(sums * over_heads(1.0 / total))
            log_total = top + jnp.log(total)
            for head in range(GROUP):
                one = log_total[head * count : (head + 1) * count]
                lse = jnp.where(lane == group * GROUP + head, one, lse)
        attended_parts.append(jnp.concatenate(pieces, axis=1))
        lse_parts.append(lse)
    attended_f = jnp.concatenate(attended_parts, axis=0)
    put(lse_ref, jnp.concatenate(lse_parts, axis=0))
    put(attended_ref, attended_f)
    attended = attended_f.astype(BF16)
    branch = nn(attended, wout_ref[...]).astype(BF16)

    pre1 = nt(branch, down1_ref[...]) + row_of(dbias1_ref)
    inner1_f, slope1 = gelu_both(pre1)
    inner1 = inner1_f.astype(BF16)
    summed = (
        mine(own_ref).astype(F32) + branch.astype(F32) + nn(inner1, up1_ref[...]) + row_of(ubias1_ref)
    )
    normal1, scale1 = normed(summed)
    gain1 = row_of(gain1_ref)
    mid = (normal1 * gain1 + row_of(shift1_ref)).astype(BF16)

    for index in range(hidden_units // CHUNK):
        outer_copy(index).wait()
    ffn_f = jnp.zeros((rows, width), F32)
    for at in range(0, hidden_units, CHUNK):
        hidden_f, slope = gelu_both(nn(mid, winner_ref[:, at : at + CHUNK]))
        slope_ref[:, at : at + CHUNK] = slope
        wouter_t_ref[:, at : at + CHUNK] = wouter_ref[at : at + CHUNK, :].T
        winner_t_ref[at : at + CHUNK, :] = winner_ref[:, at : at + CHUNK].T
        ffn_f = ffn_f + nn(hidden_f.astype(BF16), wouter_ref[at : at + CHUNK, :])
    ffn = ffn_f.astype(BF16)

    pre2 = nt(ffn, down2_ref[...]) + row_of(dbias2_ref)
    inner2_f, slope2 = gelu_both(pre2)
    inner2 = inner2_f.astype(BF16)
    summed = mid.astype(F32) + ffn.astype(F32) + nn(inner2, up2_ref[...]) + row_of(ubias2_ref)
    normal2, scale2 = normed(summed)
    gain2 = row_of(gain2_ref)
    put(mixed_ref, (normal2 * gain2 + row_of(shift2_ref)).astype(BF16))
    mixed_copy.start()

    cot = mine(cot_ref).astype(F32)
    grad_gain2 = jnp.sum(cot * normal2, axis=0, keepdims=True)
    grad_shift2 = jnp.sum(cot, axis=0, keepdims=True)
    du2 = norm_back(cot, gain2, normal2, scale2)

    def adapter_back(source, up, inner, slope, incoming):
        out_grad = incoming.astype(BF16)
        grad_up = tn(inner, out_grad)
        grad_ubias = jnp.sum(out_grad.astype(F32), axis=0, keepdims=True)
        grad_pre = (nt(out_grad, up) * slope).astype(BF16)
        grad_down = tn(grad_pre, source)
        grad_dbias = jnp.sum(grad_pre.astype(F32), axis=0, keepdims=True)
        return grad_pre, grad_down, grad_dbias, grad_up, grad_ubias

    grad_pre2, grad_down2, grad_dbias2, grad_up2, grad_ubias2 = adapter_back(
        ffn, up2_ref[...], inner2, slope2, du2
    )
    dffn = (du2 + nn(grad_pre2, down2_ref[...])).astype(BF16)
    dmid = du2
    for at in range(0, hidden_units, CHUNK):
        dhidden = (nn(dffn, wouter_t_ref[:, at : at + CHUNK]) * slope_ref[:, at : at + CHUNK]).astype(
            BF16
        )
        dmid = dmid + nn(dhidden, winner_t_ref[at : at + CHUNK, :])

    grad_gain1 = jnp.sum(dmid * normal1, axis=0, keepdims=True)
    grad_shift1 = jnp.sum(dmid, axis=0, keepdims=True)
    du1 = norm_back(dmid, gain1, normal1, scale1)
    grad_pre1, grad_down1, grad_dbias1, grad_up1, grad_ubias1 = adapter_back(
        branch, up1_ref[...], inner1, slope1, du1
    )
    put(du1_ref, du1)
    put(grad_pre_ref, grad_pre1)

    blank = jnp.zeros((1, width), F32)
    both_dbias = jnp.concatenate(
        [
            grad_dbias1,
            jnp.zeros((1, 128 - grad_dbias1.shape[1]), F32),
            grad_dbias2,
            jnp.zeros((1, width - 128 - grad_dbias2.shape[1]), F32),
        ],
        axis=1,
    )
    quarters = (
        (grad_up1, grad_ubias1, both_dbias),
        (grad_down1, grad_gain1, grad_shift1),
        (grad_up2, grad_ubias2, blank),
        (grad_down2, grad_gain2, grad_shift2),
    )
    filler = jnp.zeros((2, 128), F32)

    def part_of(quarter, side):
        pieces = [
            array[:, at : at + 128]
            for array in quarter
            for at in range(side * width // 2, (side + 1) * width // 2, 128)
        ]
        return jnp.concatenate(pieces + [filler], axis=0).astype(BF16)

    side_here = lax.axis_index("dp") % 2
    for chip_of in range(2):
        for side in range(2):
            even, odd = (part_of(quarters[2 * chip_of + index], side) for index in range(2))
            place = 2 * (chip ^ chip_of) + (side_here ^ side)
            keep_ref[place] = jnp.where(core == 0, even, odd)
            send_ref[place] = jnp.where(core == 0, odd, even)
    mixed_copy.wait()


def attended_back_kernel(
    du1_ref, grad_pre_ref, down1_ref, attended_ref, lse_ref, wout_ref, pack_ref, delta_ref
):
    rows, width = du1_ref.shape
    dbranch = (du1_ref[...] + nn(grad_pre_ref[...], down1_ref[...])).astype(BF16)
    dattended = nt(dbranch, wout_ref[...]).astype(BF16)
    pack_ref[:rows, :] = dattended
    product = dattended.astype(F32) * attended_ref[...]
    product_hi = product.astype(BF16)
    product_lo = (product - product_hi.astype(F32)).astype(BF16)
    head_of = lax.broadcasted_iota(jnp.int32, (128, width), 1) // HEAD
    picks = (head_of == lax.broadcasted_iota(jnp.int32, (128, width), 0)).astype(BF16)
    delta = nt(product_hi, picks) + nt(product_lo, picks)
    delta_ref[...] = delta
    blank = jnp.zeros((256 - rows, 128), F32)
    delta_rows = jnp.transpose(jnp.concatenate([delta, blank], axis=0))[:16]
    lse_rows = jnp.transpose(jnp.concatenate([lse_ref[...], blank], axis=0))[:16]

    def pieces_of(value, count):
        out = []
        for _ in range(count):
            piece = value.astype(BF16)
            value = value - piece.astype(F32)
            out.append(piece)
        return out

    pack_ref[rows : rows + 16, :] = jnp.concatenate(pieces_of(lse_rows, 3), axis=1)
    pack_ref[rows + 16 : rows + 32, :] = jnp.concatenate(
        pieces_of(delta_rows, 2) + [jnp.zeros((16, 256), BF16)], axis=1
    )


def query_back_kernel(
    groups,
    far_ref,
    far_mate_ref,
    q_ref,
    kbuf,
    vbuf,
    bias_a_ref,
    bias_b_ref,
    lse_ref,
    delta_ref,
    pack_ref,
    part_in_ref,
    wq_ref,
    *outs,
):
    block = lax.axis_index("blk")
    rows = q_ref.shape[0] // 2
    core, chip = block % 2, block // 2
    at_a, at_b = own_rows(block)
    meet_b = partner_offset(block)
    all_columns = slice(groups[0] * WIDE, (groups[-1] + 1) * WIDE)
    wq = wq_ref[:, all_columns]
    queries_far = (nn(far_tokens(core, far_ref, far_mate_ref), wq) * 0.125).astype(BF16)
    part_ref = outs[-1]
    for index, (group, qbuf) in enumerate(zip(groups, outs)):
        near = pl.ds(pl.multiple_of(chip * 2 * rows, rows), 2 * rows)
        qbuf[near, :] = q_ref[:, group * WIDE : (group + 1) * WIDE]
        qbuf[pl.ds(far_place(chip), 2 * SHARE), :] = queries_far[
            :, index * WIDE : (index + 1) * WIDE
        ]
    parts = []
    for at, count, meet, bias_ref in (
        (at_a, ROWS_A, LONG_AT, bias_a_ref),
        (at_b, ROWS_B, meet_b, bias_b_ref),
    ):
        lse = lse_ref[pl.ds(at, count), :]
        delta = delta_ref[pl.ds(at, count), :]
        pieces = []
        for group in groups:
            columns = slice(group * WIDE, (group + 1) * WIDE)
            heads = range(group * GROUP, (group + 1) * GROUP)
            log_total = jnp.concatenate([lse[:, head : head + 1] for head in heads], axis=0)
            deltas = jnp.concatenate([delta[:, head : head + 1] for head in heads], axis=0)
            keys = kbuf[pl.ds(meet, LONG), columns]
            scores = nt(spread_heads(q_ref[pl.ds(core * rows + at, count), columns]), keys)
            scores = masked(scores, bias_ref[...])
            probs = jnp.exp(scores - log_total)
            dprobs = nt(
                spread_heads(pack_ref[pl.ds(at, count), columns]), vbuf[pl.ds(meet, LONG), columns]
            )
            dscores = (probs * (dprobs - deltas)).astype(BF16)
            pieces.append(join_heads(nn(dscores, keys)).astype(BF16))
        parts.append(jnp.concatenate(pieces, axis=1))
    added = nt(jnp.concatenate(parts, axis=0), wq) * 0.125
    for at, rows_of in ((at_a, slice(0, ROWS_A)), (at_b, slice(ROWS_A, rows))):
        place = pl.ds(at, rows_of.stop - rows_of.start)
        part_ref[place, :] = part_in_ref[place, :] + added[rows_of]


def gather_kernel(own_ref, mate_ref, far_ref, far_mate_ref, grads_ref, stats_ref):
    block = lax.axis_index("blk")
    rows = own_ref.shape[0] - 32
    core, chip = block % 2, block // 2
    meet_b = partner_offset(block)
    grads_ref[pl.ds(pl.multiple_of(block * rows, rows), rows), :] = own_ref[:rows, :]
    grads_ref[pl.ds(pl.multiple_of((block ^ 1) * rows, rows), rows), :] = mate_ref[:rows, :]
    far_at = far_place(chip)
    far_first = pl.multiple_of(far_at + SHARE * core, 128)
    far_second = pl.multiple_of(far_at + SHARE * (1 - core), 128)
    grads_ref[pl.ds(far_first, SHARE), :] = far_ref[:SHARE, :]
    grads_ref[pl.ds(far_second, SHARE), :] = far_mate_ref[:SHARE, :]
    stats = []
    for ref, at in ((own_ref, rows), (mate_ref, rows), (far_ref, SHARE), (far_mate_ref, SHARE)):
        lse = ref[at : at + 16, :].astype(F32)
        delta = ref[at + 16 : at + 32, :].astype(F32)
        stats.append(
            jnp.concatenate(
                [
                    lse[:, :256] + (lse[:, 256:512] + lse[:, 512:]),
                    delta[:, :256] + delta[:, 256:512],
                ],
                axis=0,
            )[:, :rows]
        )
    ordered = []
    for place in range(4):
        pick = stats[place]
        for index in range(4):
            if index != place:
                pick = jnp.where(block ^ index == place, stats[index], pick)
        ordered.append(pick)
    whole = jnp.concatenate(ordered, axis=1)
    stats_ref[:32, :] = whole[:, LONG_AT : LONG_AT + LONG]
    here = whole[:, :LONG]
    for start in (128, 256):
        here = jnp.where(meet_b == start, whole[:, start : start + LONG], here)
    stats_ref[32:, :] = here


def key_back_kernel(groups, grads_ref, stats_ref, kbuf, vbuf, back_a_ref, back_b_ref, part_ref, *refs):
    qbufs, (wk_ref, wv_ref, out_ref) = refs[:-3], refs[-3:]
    block = lax.axis_index("blk")
    rows = out_ref.shape[0]
    at_a, at_b = own_rows(block)
    first = block * rows
    all_columns = slice(groups[0] * WIDE, (groups[-1] + 1) * WIDE)
    parts = []
    for at, count, meet, bias_ref, at_stats in (
        (at_a, ROWS_A, LONG_AT, back_a_ref, 0),
        (at_b, ROWS_B, partner_offset(block), back_b_ref, 32),
    ):
        own_at = pl.multiple_of(first + at, 64)
        dkeys, dvalues = [], []
        for group, qbuf in zip(groups, qbufs):
            columns = slice(group * WIDE, (group + 1) * WIDE)
            at_lse = at_stats + group * GROUP
            at_delta = at_lse + 16
            queries = qbuf[pl.ds(meet, LONG), :]
            grads = grads_ref[pl.ds(meet, LONG), columns]
            scores = nt(spread_heads(kbuf[pl.ds(own_at, count), columns]), queries)
            scores = masked(scores, bias_ref[...])
            probs = jnp.exp(less_rows(scores, stats_ref[at_lse : at_lse + GROUP, :]))
            dprobs = nt(spread_heads(vbuf[pl.ds(own_at, count), columns]), grads)
            dprobs = less_rows(dprobs, stats_ref[at_delta : at_delta + GROUP, :])
            dscores = (probs * dprobs).astype(BF16)
            dkeys.append(join_heads(nn(dscores, queries)).astype(BF16))
            dvalues.append(join_heads(nn(probs.astype(BF16), grads)).astype(BF16))
        parts.append((jnp.concatenate(dkeys, axis=1), jnp.concatenate(dvalues, axis=1)))
    dkey, dvalue = (jnp.concatenate(both, axis=0) for both in zip(*parts))
    added = nt(dkey, wk_ref[:, all_columns]) + nt(dvalue, wv_ref[:, all_columns])
    for at, rows_of in ((at_a, slice(0, ROWS_A)), (at_b, slice(ROWS_A, rows))):
        place = pl.ds(at, rows_of.stop - rows_of.start)
        out_ref[place, :] = (part_ref[place, :] + added[rows_of]).astype(out_ref.dtype)


def unpack_kernel(here_ref, other_ref, grad_ref, *refs):
    places, outs, sems = refs[:13], refs[13:25], refs[25]
    block = lax.axis_index("blk")
    side_here = lax.axis_index("dp") % 2
    core, chip = block % 2, block // 2
    adapt = outs[0].shape[0]
    copies = [
        pltpu.make_async_copy(source, target, sems.at[index])
        for index, (source, target) in enumerate(zip((grad_ref, *outs), places))
    ]
    copies[0].start()
    matrices = (2, 0, 8, 6)
    vectors = ((3,), (4, 5), (9,), (10, 11))
    width = outs[0].shape[1]
    blocks = width // 256
    for index in range(4):
        for side in range(2):
            place = 2 * (chip ^ (index // 2)) + (side_here ^ side)
            part = jnp.where(core == index % 2, here_ref[place], other_ref[place]).astype(F32)
            for block_at in range(blocks):
                lanes = slice(side * width // 2 + 128 * block_at, side * width // 2 + 128 * (block_at + 1))
                outs[matrices[index]][:, lanes] = part[adapt * block_at : adapt * (block_at + 1)]
                for number, vector in enumerate(vectors[index]):
                    outs[vector][lanes] = part[blocks * (adapt + number) + block_at]
            if index == 0 and side == 0:
                outs[1][...] = part[blocks * (adapt + 1), :adapt]
                outs[7][...] = part[blocks * (adapt + 1) + 1, :adapt]
        ready = [matrices[index], *vectors[index]] + ([1, 7] if index == 0 else [])
        for out in ready:
            copies[1 + out].start()
    for copy in copies:
        copy.wait()


def params(megabytes):
    return pltpu.CompilerParams(vmem_limit_bytes=megabytes << 20)


def cost(gigaflop, megabytes):
    return pl.CostEstimate(
        flops=int(gigaflop * 1e9), bytes_accessed=int(megabytes * 1e6), transcendentals=0
    )


def after(array, *others):
    return lax.optimization_barrier((array,) + others)[0]


def vmem(dims, dtype):
    return pltpu.VMEM(dims, dtype)


def in_hbm(array):
    return pltpu.with_memory_space_constraint(array, pltpu.HBM)


def shape(dims, dtype):
    return jax.ShapeDtypeStruct(dims, dtype)


def body(
    dp_size,
    tokens,
    w_query,
    w_key,
    w_value,
    w_out,
    w_inner,
    w_outer,
    down_one,
    dbias_one,
    up_one,
    ubias_one,
    gain_one,
    shift_one,
    down_two,
    dbias_two,
    up_two,
    ubias_two,
    gain_two,
    shift_two,
    seg_len,
    seg_valid,
    cotangent,
):
    rows, _, width = tokens.shape
    adapt = up_one.shape[0]
    hidden = w_inner.shape[1]
    block = lax.axis_index("blk")
    own = tokens.reshape(rows, width)
    cot = cotangent.reshape(rows, width)

    def swap(array, mask):
        return lax.ppermute(array, "blk", [(i, i ^ mask) for i in range(4)])

    def swap_all(array, mask):
        return lax.ppermute(
            array, ("dp", "blk"), [(i, i ^ mask) for i in range(4 * dp_size)]
        )

    mate = swap(own, 1)
    own = pl.pallas_call(
        fetch_kernel,
        in_specs=[HBM],
        out_specs=VMEM,
        out_shape=vmem((rows, width), BF16),
        scratch_shapes=[pltpu.SemaphoreType.DMA],
        compiler_params=params(1),
        cost_estimate=cost(0.1, 1.0),
        name="fetch",
    )(in_hbm(own))
    def near_share(own, mate):
        choices = (
            (own[128:192], own[64:128], own[:64], mate[128:192]),
            (mate[:64], own[128:192], own[64:128], own[:64]),
        )
        halves = []
        for options in choices:
            half = options[0]
            for index in range(1, 4):
                half = jnp.where(block == index, options[index], half)
            halves.append(half)
        return halves

    far = swap(jnp.concatenate(near_share(own, mate), axis=0), 2)
    smalls = (
        cot,
        down_one.T,
        dbias_one,
        up_one,
        ubias_one,
        gain_one,
        shift_one,
        down_two.T,
        dbias_two,
        up_two,
        ubias_two,
        gain_two,
        shift_two,
    )
    half_mask_shapes = [vmem((count, HALF), F32) for count in (ROWS_A, ROWS_B)] * 2
    mask_shapes = [vmem((count, LONG), F32) for count in (ROWS_A, ROWS_B)] * 2
    (
        q,
        kpair,
        vpair,
        bias_a,
        bias_b,
        back_a,
        back_b,
        near_a,
        near_b,
        far_a,
        far_b,
        wq_here,
        wk_here,
        wv_here,
        wout_here,
        winner_here,
        *smalls_here,
    ) = pl.pallas_call(
        project_kernel,
        in_specs=[SMEM] * 2 + [VMEM] * 2 + [HBM] * (5 + len(smalls)),
        out_specs=[VMEM] * (16 + len(smalls)),
        out_shape=[vmem((2 * rows, width), BF16)] * 3
        + mask_shapes
        + half_mask_shapes
        + [vmem((width, width), BF16)] * 4
        + [vmem((width, hidden), BF16)]
        + [vmem(small.shape, small.dtype) for small in smalls],
        scratch_shapes=[pltpu.SemaphoreType.DMA((5 + len(smalls),))],
        compiler_params=params(4),
        cost_estimate=cost(2.0, 12.0),
        name="project",
    )(
        in_hbm(seg_len),
        in_hbm(seg_valid),
        own,
        mate,
        in_hbm(w_query),
        in_hbm(w_key),
        in_hbm(w_value),
        in_hbm(w_out),
        in_hbm(w_inner),
        *(in_hbm(small) for small in smalls),
    )
    far_mate = swap(after(far, q), 1)
    kfar, vfar, sums, tops, totals = pl.pallas_call(
        near_kernel,
        in_specs=[VMEM] * 8,
        out_specs=[VMEM] * 5,
        out_shape=[vmem((SHARE, width), BF16)] * 2
        + [vmem((rows, width), F32)]
        + [vmem((width // WIDE, GROUP * rows, 128), F32)] * 2,
        compiler_params=params(5),
        cost_estimate=cost(1.0, 2.0),
        name="near",
    )(far, q, kpair, vpair, near_a, near_b, wk_here, wv_here)

    part_rows = width // 256 * (adapt + 2) + 2
    mixed, kbuf, vbuf, lse, du1, attended, grad_pre, keep, send = pl.pallas_call(
        main_kernel,
        in_specs=[VMEM] * 29 + [HBM],
        out_specs=[HBM] + [VMEM] * 8,
        out_shape=[
            shape((rows, width), BF16),
            vmem((4 * rows, width), BF16),
            vmem((4 * rows, width), BF16),
            vmem((rows, 128), F32),
            vmem((rows, width), F32),
            vmem((rows, width), F32),
            vmem((rows, adapt), BF16),
            vmem((4, part_rows, 128), BF16),
            vmem((4, part_rows, 128), BF16),
        ],
        scratch_shapes=[
            pltpu.VMEM((hidden, width), BF16),
            pltpu.VMEM((width, hidden), BF16),
            pltpu.VMEM((hidden, width), BF16),
            pltpu.VMEM((rows, hidden), F32),
            pltpu.VMEM((rows, width), BF16),
            pltpu.SemaphoreType.DMA((1 + hidden // CHUNK,)),
        ],
        compiler_params=params(22),
        cost_estimate=cost(8.0, 20.0),
        name="layer",
    )(
        own,
        far_mate,
        q,
        kpair,
        vpair,
        kfar,
        vfar,
        sums,
        tops,
        totals,
        far_a,
        far_b,
        *smalls_here,
        wk_here,
        wv_here,
        wout_here,
        winner_here,
        in_hbm(w_outer),
    )

    def add(*terms):
        return functools.reduce(jnp.add, [term.astype(F32) for term in terms]).astype(BF16)

    pack, delta = pl.pallas_call(
        attended_back_kernel,
        in_specs=[VMEM] * 6,
        out_specs=[VMEM] * 2,
        out_shape=[vmem((rows + 32, width), BF16), vmem((rows, 128), F32)],
        compiler_params=params(5),
        cost_estimate=cost(0.5, 2.0),
        name="attended_back",
    )(du1, grad_pre, smalls_here[1], attended, lse, wout_here)

    def query_back(groups, part):
        return pl.pallas_call(
            functools.partial(query_back_kernel, groups),
            in_specs=[VMEM] * 12,
            out_specs=[VMEM] * (len(groups) + 1),
            out_shape=[vmem((4 * rows, WIDE), BF16)] * len(groups) + [vmem((rows, width), F32)],
            compiler_params=params(5),
            cost_estimate=cost(1.0 * len(groups), 3.0),
            name=f"query_back_{groups[0]}",
        )(far, far_mate, q, kbuf, vbuf, bias_a, bias_b, lse, delta, pack, part, wq_here)

    def key_back(groups, qbufs, part, dtype):
        return pl.pallas_call(
            functools.partial(key_back_kernel, groups),
            in_specs=[VMEM] * (9 + len(groups)),
            out_specs=VMEM,
            out_shape=vmem((rows, width), dtype),
            compiler_params=params(5),
            cost_estimate=cost(1.0 * len(groups), 3.0),
            name=f"key_back_{groups[0]}",
        )(grads_row, stats_row, kbuf, vbuf, back_a, back_b, part, *qbufs, wk_here, wv_here)

    total = add(keep, after(swap_all(send, 1), pack))
    arrived = [swap_all(total[index], mask) for index, mask in ((1, 4), (2, 2), (3, 6))]
    pack_mate = swap(after(pack, total), 1)
    qbuf0, qbuf1, part = query_back((0, 1), after(du1, total))
    total = add(total[0], *lax.optimization_barrier((*arrived, part, pack_mate))[:3])
    masks = []
    while 8 << len(masks) < 4 * dp_size:
        masks.append(8 << len(masks))
    arrived = swap_all(total, masks[0])
    pack_now = after(pack, total)
    share = near_share(pack_now, pack_mate) + [pack_now[rows:]]
    pack_far = swap(jnp.concatenate(share, axis=0), 2)
    total = add(total, arrived)
    arrived = swap_all(total, masks[1])
    qbuf2, part = query_back((2,), after(part, total))
    pack_far, part = lax.optimization_barrier((pack_far, part))
    pack_far_mate = swap(pack_far, 1)
    total = add(total, after(arrived, part))
    for mask in masks[2:]:
        total = add(total, swap_all(total, mask))
    others = [swap_all(total, mask) for mask in (4, 2, 6)]
    grads_row, stats_row = pl.pallas_call(
        gather_kernel,
        in_specs=[VMEM] * 4,
        out_specs=[VMEM] * 2,
        out_shape=[vmem((4 * rows, width), BF16), vmem((64, LONG), F32)],
        compiler_params=params(3),
        cost_estimate=cost(0.1, 1.0),
        name="gather",
    )(pack, pack_mate, pack_far, after(pack_far_mate, total))
    part = key_back((0, 1), (qbuf0, qbuf1), after(part, total), F32)
    here = jnp.stack([total, *lax.optimization_barrier((*others, part))[:3]])
    other = swap_all(here, 1)
    input_grad = key_back((2,), (qbuf2,), after(part, here), BF16)

    grad_dims = ((adapt, width), (adapt,), (adapt, width), (width,), (width,), (width,)) * 2
    input_grad, *grads = pl.pallas_call(
        unpack_kernel,
        in_specs=[VMEM] * 3,
        out_specs=[HBM] * 13,
        out_shape=[shape((rows, width), BF16)] + [shape(dims, F32) for dims in grad_dims],
        scratch_shapes=[pltpu.VMEM(dims, F32) for dims in grad_dims]
        + [pltpu.SemaphoreType.DMA((13,))],
        compiler_params=params(5),
        name="unpack",
    )(here, other, input_grad)
    return (mixed.reshape(tokens.shape), input_grad.reshape(tokens.shape)) + tuple(
        grad.T if index in (0, 6) else grad for index, grad in enumerate(grads)
    )


def solution(mesh):
    in_specs = (
        (P("blk", "dp", None),) + (P(),) * 18 + (P("dp", None),) * 2 + (P("blk", "dp", None),)
    )
    out_specs = (P("blk", "dp", None),) * 2 + (P(),) * 12
    return jax.shard_map(
        functools.partial(body, mesh.shape["dp"]),
        mesh=mesh,
        in_specs=in_specs,
        out_specs=out_specs,
        check_vma=False,
    )
```

```python
import functools

import jax
import jax.numpy as jnp
from jax import lax
from jax.experimental import pallas as pl
from jax.experimental.pallas import tpu as pltpu
from jax.sharding import PartitionSpec as P

HEAD = 64
GROUP = 4
LONG_AT = 128
LONG = 512
ROWS_A = 64
WIDE = GROUP * HEAD
HALF = 256
SHARE = 128
CHUNK = 768
ROWS_B = 128
NEG = -1e30
F32 = jnp.float32
BF16 = jnp.bfloat16

VMEM = pl.BlockSpec(memory_space=pltpu.VMEM)
SMEM = pl.BlockSpec(memory_space=pltpu.SMEM)
HBM = pl.BlockSpec(memory_space=pltpu.HBM)


def nn(left, right):
    return lax.dot_general(left, right, (((1,), (0,)), ((), ())), preferred_element_type=F32)


def nt(left, right):
    return lax.dot_general(left, right, (((1,), (1,)), ((), ())), preferred_element_type=F32)


def tn(left, right):
    return lax.dot_general(left, right, (((0,), (0,)), ((), ())), preferred_element_type=F32)


def gelu_both(values):
    phi = 0.5 + 0.5 * lax.erf(values * 0.7071067811865476)
    bell = jnp.exp(-0.5 * values * values)
    return values * phi, phi + values * bell * 0.3989422804014327


def normed(values):
    centre = jnp.mean(values, axis=-1, keepdims=True)
    centred = values - centre
    spread = jnp.mean(centred * centred, axis=-1, keepdims=True)
    scale = lax.rsqrt(spread + 1e-06)
    return centred * scale, scale


def norm_back(incoming, gain, normal, scale):
    scaled = incoming * gain
    first = jnp.mean(scaled, axis=-1, keepdims=True)
    second = jnp.mean(scaled * normal, axis=-1, keepdims=True)
    return scale * (scaled - first - normal * second)


def row_of(ref):
    return ref[...].reshape(1, ref.shape[0])


def own_rows(block):
    return (
        pl.multiple_of(jnp.where(block == 0, 128, 0), 64),
        pl.multiple_of(jnp.where(block == 0, 0, 64), 64),
    )


def far_place(chip):
    return pl.multiple_of(LONG_AT + 2 * SHARE * (1 - chip), 128)


def near_places(block):
    chip = block // 2
    long_at = LONG_AT * (1 - chip)
    short_at = LONG_AT * chip
    outer = (block == 0) | (block == 3)
    return (
        pl.multiple_of(long_at, 128),
        pl.multiple_of(jnp.where(outer, short_at, long_at), 128),
    )


def far_tokens(core, far_ref, far_mate_ref):
    far, far_mate = far_ref[...], far_mate_ref[...]
    first = core == 0
    return jnp.concatenate(
        [jnp.where(first, far, far_mate), jnp.where(first, far_mate, far)], axis=0
    )


def partner_offset(block):
    return pl.multiple_of(jnp.where(block == 0, 0, jnp.where(block == 3, 256, 128)), 128)


def bounds(len_ref, valid_ref, places):
    low = jnp.zeros(places.shape, jnp.int32)
    high = jnp.zeros(places.shape, jnp.int32)
    start = jnp.int32(0)
    for slot in range(len_ref.shape[1]):
        end = start + len_ref[0, slot]
        inside = (places >= start) & (places < end)
        low = jnp.where(inside, start, low)
        high = jnp.where(inside, start + valid_ref[0, slot], high)
        start = end
    return low, high


def bias_of(len_ref, valid_ref, query_at, key_at, rows, columns=LONG):
    places = query_at + lax.broadcasted_iota(jnp.int32, (rows, 1), 0)
    low, high = bounds(len_ref, valid_ref, places)
    keys = key_at + lax.broadcasted_iota(jnp.int32, (rows, columns), 1)
    return jnp.where((keys >= low) & (keys < high), 0.0, NEG)


def bias_back_of(len_ref, valid_ref, key_at, query_at, rows):
    places = query_at + lax.broadcasted_iota(jnp.int32, (1, LONG), 1)
    low, high = bounds(len_ref, valid_ref, places)
    keys = key_at + lax.broadcasted_iota(jnp.int32, (rows, LONG), 0)
    return jnp.where((keys >= low) & (keys < high), 0.0, NEG)


def spread_heads(part):
    lane = lax.broadcasted_iota(jnp.int32, part.shape, 1) // HEAD
    return jnp.concatenate(
        [jnp.where(lane == head, part, jnp.zeros_like(part)) for head in range(GROUP)], axis=0
    )


def join_heads(stacked):
    rows = stacked.shape[0] // GROUP
    lane = lax.broadcasted_iota(jnp.int32, (rows, stacked.shape[1]), 1) // HEAD
    out = stacked[:rows]
    for head in range(1, GROUP):
        out = jnp.where(lane == head, stacked[head * rows : (head + 1) * rows], out)
    return out


def masked(scores, bias):
    split = scores.reshape((GROUP,) + bias.shape)
    return (split + bias).reshape(scores.shape)


def less_rows(stacked, rows):
    count = stacked.shape[0] // GROUP
    return jnp.concatenate(
        [stacked[head * count : (head + 1) * count] - rows[head : head + 1] for head in range(GROUP)],
        axis=0,
    )


def fetch_kernel(source, target, sem):
    copy = pltpu.make_async_copy(source, target, sem)
    copy.start()
    copy.wait()


def project_kernel(
    len_ref,
    valid_ref,
    own_ref,
    mate_ref,
    wq_hbm,
    wk_hbm,
    wv_hbm,
    wout_hbm,
    winner_hbm,
    *refs,
):
    rest = (len(refs) - 20) // 2
    smalls_hbm, refs, sems = refs[:rest], refs[rest:-1], refs[-1]
    project_rows(
        len_ref,
        valid_ref,
        own_ref,
        mate_ref,
        (wq_hbm, wk_hbm, wv_hbm, wout_hbm, winner_hbm),
        *refs[:19],
        tuple(zip(smalls_hbm, refs[19:])),
        sems,
    )


def project_rows(
    len_ref,
    valid_ref,
    own_ref,
    mate_ref,
    weights_hbm,
    q_ref,
    k_ref,
    v_ref,
    bias_a_ref,
    bias_b_ref,
    back_a_ref,
    back_b_ref,
    near_a_ref,
    near_b_ref,
    far_a_ref,
    far_b_ref,
    wq_ref,
    wk_ref,
    wv_ref,
    wout_ref,
    winner_ref,
    sums_ref,
    tops_ref,
    totals_ref,
    smalls,
    sems,
):
    weights = (wq_ref, wk_ref, wv_ref, wout_ref, winner_ref)
    moves = tuple(zip(weights_hbm, weights)) + smalls
    copies = [
        pltpu.make_async_copy(source, target, sems.at[index])
        for index, (source, target) in enumerate(moves)
    ]
    block = lax.axis_index("blk")

    @pl.when(block < 4)
    def _():
        for copy in copies:
            copy.start()

    core = block % 2
    rows = own_ref.shape[0]
    first = block * rows
    at_a, at_b = own_rows(block)
    meet_b = partner_offset(block)
    bias_a_ref[...] = bias_of(len_ref, valid_ref, first + at_a, LONG_AT, ROWS_A)
    bias_b_ref[...] = bias_of(len_ref, valid_ref, first + at_b, meet_b, ROWS_B)
    chip = block // 2
    near_a, near_b = near_places(block)
    pair_at = chip * 2 * rows
    far_at = far_place(chip)
    for at, count, near, near_ref, far_ref in (
        (at_a, ROWS_A, near_a, near_a_ref, far_a_ref),
        (at_b, ROWS_B, near_b, near_b_ref, far_b_ref),
    ):
        near_ref[...] = bias_of(len_ref, valid_ref, first + at, pair_at + near, count, HALF)
        far_ref[...] = bias_of(len_ref, valid_ref, first + at, far_at, count, HALF)
    back_a_ref[...] = bias_back_of(len_ref, valid_ref, first + at_a, LONG_AT, ROWS_A)
    back_b_ref[...] = bias_back_of(len_ref, valid_ref, first + at_b, meet_b, ROWS_B)
    mine = pl.multiple_of(core * rows, rows)
    other = pl.multiple_of((1 - core) * rows, rows)
    both = jnp.concatenate([own_ref[...], mate_ref[...]], axis=0)
    for copy, weight, out, scale in (
        (copies[0], wq_ref, q_ref, 0.125),
        (copies[1], wk_ref, k_ref, 1.0),
        (copies[2], wv_ref, v_ref, 1.0),
    ):
        copy.wait()
        product = (nn(both, weight[...]) * scale).astype(BF16)
        out[pl.ds(mine, rows), :] = product[:rows]
        out[pl.ds(other, rows), :] = product[rows:]
    near_attention(
        (0,), q_ref, k_ref, v_ref, (near_a_ref, near_b_ref), sums_ref, tops_ref, totals_ref
    )
    for copy in copies[3:]:
        copy.wait()


def over_heads(stat):
    count = stat.shape[0] // GROUP
    parts = [stat[head * count : (head + 1) * count] for head in range(GROUP)]
    left = lax.broadcasted_iota(jnp.int32, (1, 128), 1) < HEAD
    return jnp.concatenate(
        [jnp.where(left, parts[0], parts[1]), jnp.where(left, parts[2], parts[3])], axis=1
    )


def near_attention(groups, q_ref, kpair_ref, vpair_ref, masks, sums_ref, tops_ref, totals_ref):
    block = lax.axis_index("blk")
    rows = sums_ref.shape[0]
    core = block % 2
    at_a, at_b = own_rows(block)
    near_a, near_b = near_places(block)
    near_a_ref, near_b_ref = masks
    for at, count, near, bias_ref, at_stat in (
        (at_a, ROWS_A, near_a, near_a_ref, 0),
        (at_b, ROWS_B, near_b, near_b_ref, GROUP * ROWS_A),
    ):
        stacked = pl.ds(at_stat, GROUP * count)
        for index, group in enumerate(groups):
            columns = slice(group * WIDE, (group + 1) * WIDE)
            queries = spread_heads(q_ref[pl.ds(core * rows + at, count), columns])
            scores = masked(nt(queries, kpair_ref[pl.ds(near, HALF), columns]), bias_ref[...])
            top = jnp.max(scores, axis=-1, keepdims=True)
            weights = jnp.exp(scores - top)
            total = jnp.sum(weights, axis=-1, keepdims=True)
            sums = nn(weights.astype(BF16), vpair_ref[pl.ds(near, HALF), columns])
            sums_ref[pl.ds(at, count), index * WIDE : (index + 1) * WIDE] = join_heads(sums)
            tops_ref[index, stacked, :] = jnp.broadcast_to(top, (GROUP * count, 128))
            totals_ref[index, stacked, :] = jnp.broadcast_to(total, (GROUP * count, 128))


def near_kernel(
    far_ref,
    q_ref,
    kpair_ref,
    vpair_ref,
    near_a_ref,
    near_b_ref,
    wk_ref,
    wv_ref,
    kfar_ref,
    vfar_ref,
    sums_ref,
    tops_ref,
    totals_ref,
):
    kfar_ref[...] = nn(far_ref[...], wk_ref[...]).astype(BF16)
    vfar_ref[...] = nn(far_ref[...], wv_ref[...]).astype(BF16)
    near_attention(
        tuple(range(1, q_ref.shape[1] // WIDE)),
        q_ref,
        kpair_ref,
        vpair_ref,
        (near_a_ref, near_b_ref),
        sums_ref,
        tops_ref,
        totals_ref,
    )


def main_kernel(
    own_ref,
    far_mate_ref,
    q_ref,
    kpair_ref,
    vpair_ref,
    kfar_ref,
    vfar_ref,
    sums0_ref,
    tops0_ref,
    totals0_ref,
    sums_ref,
    tops_ref,
    totals_ref,
    far_a_ref,
    far_b_ref,
    cot_ref,
    down1_ref,
    dbias1_ref,
    up1_ref,
    ubias1_ref,
    gain1_ref,
    shift1_ref,
    down2_ref,
    dbias2_ref,
    up2_ref,
    ubias2_ref,
    gain2_ref,
    shift2_ref,
    wk_ref,
    wv_ref,
    wout_ref,
    winner_ref,
    wouter_hbm,
    mixed_hbm,
    kbuf,
    vbuf,
    lse_ref,
    du1_ref,
    attended_ref,
    grad_pre_ref,
    keep_ref,
    send_ref,
    wouter_ref,
    wouter_t_ref,
    winner_t_ref,
    slope_ref,
    mixed_ref,
    sems,
):
    hidden_units = winner_ref.shape[1]

    def outer_copy(index):
        part = pl.ds(pl.multiple_of(index * CHUNK, CHUNK), CHUNK)
        return pltpu.make_async_copy(wouter_hbm.at[part], wouter_ref.at[part], sems.at[1 + index])

    @pl.loop(0, hidden_units // CHUNK)
    def _(index):
        outer_copy(index).start()

    mixed_copy = pltpu.make_async_copy(mixed_ref, mixed_hbm, sems.at[0])
    block = lax.axis_index("blk")
    core = block % 2
    chip = block // 2
    rows, width = own_ref.shape
    at_a, at_b = own_rows(block)

    def mine(ref):
        return jnp.concatenate([ref[pl.ds(at_a, ROWS_A), :], ref[pl.ds(at_b, ROWS_B), :]], axis=0)

    def put(ref, value):
        ref[pl.ds(at_a, ROWS_A), :] = value[:ROWS_A]
        ref[pl.ds(at_b, ROWS_B), :] = value[ROWS_A:]

    near = pl.multiple_of(chip * 2 * rows, 2 * rows)
    kbuf[pl.ds(near, 2 * rows), :] = kpair_ref[...]
    vbuf[pl.ds(near, 2 * rows), :] = vpair_ref[...]
    far_at = far_place(chip)
    far_first = pl.multiple_of(far_at + SHARE * core, 128)
    far_second = pl.multiple_of(far_at + SHARE * (1 - core), 128)
    kbuf[pl.ds(far_first, SHARE), :] = kfar_ref[...]
    vbuf[pl.ds(far_first, SHARE), :] = vfar_ref[...]
    kbuf[pl.ds(far_second, SHARE), :] = nn(far_mate_ref[...], wk_ref[...]).astype(BF16)
    vbuf[pl.ds(far_second, SHARE), :] = nn(far_mate_ref[...], wv_ref[...]).astype(BF16)

    lane = lax.broadcasted_iota(jnp.int32, (1, 128), 1)
    attended_parts = []
    lse_parts = []
    for at, count, bias_ref, at_stat in (
        (at_a, ROWS_A, far_a_ref, 0),
        (at_b, ROWS_B, far_b_ref, GROUP * ROWS_A),
    ):
        pieces = []
        lse = jnp.zeros((count, 128), F32)
        stacked = pl.ds(at_stat, GROUP * count)
        for group in range(width // WIDE):
            columns = slice(group * WIDE, (group + 1) * WIDE)
            queries = spread_heads(q_ref[pl.ds(core * rows + at, count), columns])
            scores = masked(nt(queries, kbuf[pl.ds(far_at, HALF), columns]), bias_ref[...])
            near_sums = sums0_ref if group == 0 else sums_ref
            near_tops = tops0_ref if group == 0 else tops_ref
            near_totals = totals0_ref if group == 0 else totals_ref
            held = max(group - 1, 0)
            top_near = near_tops[held, stacked, :]
            top = jnp.maximum(top_near, jnp.max(scores, axis=-1, keepdims=True))
            weights = jnp.exp(scores - jnp.concatenate([top, top], axis=1))
            shrink = jnp.exp(top_near - top)
            total = shrink * near_totals[held, stacked, :] + jnp.sum(
                weights, axis=-1, keepdims=True
            )
            sums = join_heads(nn(weights.astype(BF16), vbuf[pl.ds(far_at, HALF), columns]))
            sums = sums + near_sums[
                pl.ds(at, count), held * WIDE : (held + 1) * WIDE
            ] * over_heads(shrink)
            pieces.append(sums * over_heads(1.0 / total))
            log_total = top + jnp.log(total)
            for head in range(GROUP):
                one = log_total[head * count : (head + 1) * count]
                lse = jnp.where(lane == group * GROUP + head, one, lse)
        attended_parts.append(jnp.concatenate(pieces, axis=1))
        lse_parts.append(lse)
    attended_f = jnp.concatenate(attended_parts, axis=0)
    put(lse_ref, jnp.concatenate(lse_parts, axis=0))
    put(attended_ref, attended_f)
    attended = attended_f.astype(BF16)
    branch = nn(attended, wout_ref[...]).astype(BF16)

    pre1 = nt(branch, down1_ref[...]) + row_of(dbias1_ref)
    inner1_f, slope1 = gelu_both(pre1)
    inner1 = inner1_f.astype(BF16)
    summed = (
        mine(own_ref).astype(F32) + branch.astype(F32) + nn(inner1, up1_ref[...]) + row_of(ubias1_ref)
    )
    normal1, scale1 = normed(summed)
    gain1 = row_of(gain1_ref)
    mid = (normal1 * gain1 + row_of(shift1_ref)).astype(BF16)

    for index in range(hidden_units // CHUNK):
        outer_copy(index).wait()
    ffn_f = jnp.zeros((rows, width), F32)
    for at in range(0, hidden_units, CHUNK):
        hidden_f, slope = gelu_both(nn(mid, winner_ref[:, at : at + CHUNK]))
        slope_ref[:, at : at + CHUNK] = slope
        wouter_t_ref[:, at : at + CHUNK] = wouter_ref[at : at + CHUNK, :].T
        winner_t_ref[at : at + CHUNK, :] = winner_ref[:, at : at + CHUNK].T
        ffn_f = ffn_f + nn(hidden_f.astype(BF16), wouter_ref[at : at + CHUNK, :])
    ffn = ffn_f.astype(BF16)

    pre2 = nt(ffn, down2_ref[...]) + row_of(dbias2_ref)
    inner2_f, slope2 = gelu_both(pre2)
    inner2 = inner2_f.astype(BF16)
    summed = mid.astype(F32) + ffn.astype(F32) + nn(inner2, up2_ref[...]) + row_of(ubias2_ref)
    normal2, scale2 = normed(summed)
    gain2 = row_of(gain2_ref)
    put(mixed_ref, (normal2 * gain2 + row_of(shift2_ref)).astype(BF16))
    mixed_copy.start()

    cot = mine(cot_ref).astype(F32)
    grad_gain2 = jnp.sum(cot * normal2, axis=0, keepdims=True)
    grad_shift2 = jnp.sum(cot, axis=0, keepdims=True)
    du2 = norm_back(cot, gain2, normal2, scale2)

    def adapter_back(source, up, inner, slope, incoming):
        out_grad = incoming.astype(BF16)
        grad_up = tn(inner, out_grad)
        grad_ubias = jnp.sum(out_grad.astype(F32), axis=0, keepdims=True)
        grad_pre = (nt(out_grad, up) * slope).astype(BF16)
        grad_down = tn(grad_pre, source)
        grad_dbias = jnp.sum(grad_pre.astype(F32), axis=0, keepdims=True)
        return grad_pre, grad_down, grad_dbias, grad_up, grad_ubias

    grad_pre2, grad_down2, grad_dbias2, grad_up2, grad_ubias2 = adapter_back(
        ffn, up2_ref[...], inner2, slope2, du2
    )
    dffn = (du2 + nn(grad_pre2, down2_ref[...])).astype(BF16)
    dmid = du2
    for at in range(0, hidden_units, CHUNK):
        dhidden = (nn(dffn, wouter_t_ref[:, at : at + CHUNK]) * slope_ref[:, at : at + CHUNK]).astype(
            BF16
        )
        dmid = dmid + nn(dhidden, winner_t_ref[at : at + CHUNK, :])

    grad_gain1 = jnp.sum(dmid * normal1, axis=0, keepdims=True)
    grad_shift1 = jnp.sum(dmid, axis=0, keepdims=True)
    du1 = norm_back(dmid, gain1, normal1, scale1)
    grad_pre1, grad_down1, grad_dbias1, grad_up1, grad_ubias1 = adapter_back(
        branch, up1_ref[...], inner1, slope1, du1
    )
    put(du1_ref, du1)
    put(grad_pre_ref, grad_pre1)

    blank = jnp.zeros((1, width), F32)
    both_dbias = jnp.concatenate(
        [
            grad_dbias1,
            jnp.zeros((1, 128 - grad_dbias1.shape[1]), F32),
            grad_dbias2,
            jnp.zeros((1, width - 128 - grad_dbias2.shape[1]), F32),
        ],
        axis=1,
    )
    quarters = (
        (grad_up1, grad_ubias1, both_dbias),
        (grad_down1, grad_gain1, grad_shift1),
        (grad_up2, grad_ubias2, blank),
        (grad_down2, grad_gain2, grad_shift2),
    )
    filler = jnp.zeros((2, 128), F32)

    def part_of(quarter, side):
        pieces = [
            array[:, at : at + 128]
            for array in quarter
            for at in range(side * width // 2, (side + 1) * width // 2, 128)
        ]
        return jnp.concatenate(pieces + [filler], axis=0).astype(BF16)

    side_here = lax.axis_index("dp") % 2
    for chip_of in range(2):
        for side in range(2):
            even, odd = (part_of(quarters[2 * chip_of + index], side) for index in range(2))
            place = 2 * (chip ^ chip_of) + (side_here ^ side)
            keep_ref[place] = jnp.where(core == 0, even, odd)
            send_ref[place] = jnp.where(core == 0, odd, even)
    mixed_copy.wait()


def attended_back_kernel(
    du1_ref, grad_pre_ref, down1_ref, attended_ref, lse_ref, wout_ref, pack_ref, delta_ref
):
    rows, width = du1_ref.shape
    dbranch = (du1_ref[...] + nn(grad_pre_ref[...], down1_ref[...])).astype(BF16)
    dattended = nt(dbranch, wout_ref[...]).astype(BF16)
    pack_ref[:rows, :] = dattended
    product = dattended.astype(F32) * attended_ref[...]
    product_hi = product.astype(BF16)
    product_lo = (product - product_hi.astype(F32)).astype(BF16)
    head_of = lax.broadcasted_iota(jnp.int32, (128, width), 1) // HEAD
    picks = (head_of == lax.broadcasted_iota(jnp.int32, (128, width), 0)).astype(BF16)
    delta = nt(product_hi, picks) + nt(product_lo, picks)
    delta_ref[...] = delta
    blank = jnp.zeros((256 - rows, 128), F32)
    delta_rows = jnp.transpose(jnp.concatenate([delta, blank], axis=0))[:16]
    lse_rows = jnp.transpose(jnp.concatenate([lse_ref[...], blank], axis=0))[:16]

    def pieces_of(value, count):
        out = []
        for _ in range(count):
            piece = value.astype(BF16)
            value = value - piece.astype(F32)
            out.append(piece)
        return out

    pack_ref[rows : rows + 16, :] = jnp.concatenate(pieces_of(lse_rows, 3), axis=1)
    pack_ref[rows + 16 : rows + 32, :] = jnp.concatenate(
        pieces_of(delta_rows, 2) + [jnp.zeros((16, 256), BF16)], axis=1
    )


def query_back_kernel(
    groups,
    far_ref,
    far_mate_ref,
    q_ref,
    kbuf,
    vbuf,
    bias_a_ref,
    bias_b_ref,
    lse_ref,
    delta_ref,
    pack_ref,
    part_in_ref,
    wq_ref,
    *outs,
):
    block = lax.axis_index("blk")
    rows = q_ref.shape[0] // 2
    core, chip = block % 2, block // 2
    at_a, at_b = own_rows(block)
    meet_b = partner_offset(block)
    all_columns = slice(groups[0] * WIDE, (groups[-1] + 1) * WIDE)
    wq = wq_ref[:, all_columns]
    queries_far = (nn(far_tokens(core, far_ref, far_mate_ref), wq) * 0.125).astype(BF16)
    part_ref = outs[-1]
    for index, (group, qbuf) in enumerate(zip(groups, outs)):
        near = pl.ds(pl.multiple_of(chip * 2 * rows, rows), 2 * rows)
        qbuf[near, :] = q_ref[:, group * WIDE : (group + 1) * WIDE]
        qbuf[pl.ds(far_place(chip), 2 * SHARE), :] = queries_far[
            :, index * WIDE : (index + 1) * WIDE
        ]
    parts = []
    for at, count, meet, bias_ref in (
        (at_a, ROWS_A, LONG_AT, bias_a_ref),
        (at_b, ROWS_B, meet_b, bias_b_ref),
    ):
        lse = lse_ref[pl.ds(at, count), :]
        delta = delta_ref[pl.ds(at, count), :]
        pieces = []
        for group in groups:
            columns = slice(group * WIDE, (group + 1) * WIDE)
            heads = range(group * GROUP, (group + 1) * GROUP)
            log_total = jnp.concatenate([lse[:, head : head + 1] for head in heads], axis=0)
            deltas = jnp.concatenate([delta[:, head : head + 1] for head in heads], axis=0)
            keys = kbuf[pl.ds(meet, LONG), columns]
            scores = nt(spread_heads(q_ref[pl.ds(core * rows + at, count), columns]), keys)
            scores = masked(scores, bias_ref[...])
            probs = jnp.exp(scores - log_total)
            dprobs = nt(
                spread_heads(pack_ref[pl.ds(at, count), columns]), vbuf[pl.ds(meet, LONG), columns]
            )
            dscores = (probs * (dprobs - deltas)).astype(BF16)
            pieces.append(join_heads(nn(dscores, keys)).astype(BF16))
        parts.append(jnp.concatenate(pieces, axis=1))
    added = nt(jnp.concatenate(parts, axis=0), wq) * 0.125
    for at, rows_of in ((at_a, slice(0, ROWS_A)), (at_b, slice(ROWS_A, rows))):
        place = pl.ds(at, rows_of.stop - rows_of.start)
        part_ref[place, :] = part_in_ref[place, :] + added[rows_of]


def gather_kernel(own_ref, mate_ref, far_ref, far_mate_ref, grads_ref, stats_ref):
    block = lax.axis_index("blk")
    rows = own_ref.shape[0] - 32
    core, chip = block % 2, block // 2
    meet_b = partner_offset(block)
    grads_ref[pl.ds(pl.multiple_of(block * rows, rows), rows), :] = own_ref[:rows, :]
    grads_ref[pl.ds(pl.multiple_of((block ^ 1) * rows, rows), rows), :] = mate_ref[:rows, :]
    far_at = far_place(chip)
    far_first = pl.multiple_of(far_at + SHARE * core, 128)
    far_second = pl.multiple_of(far_at + SHARE * (1 - core), 128)
    grads_ref[pl.ds(far_first, SHARE), :] = far_ref[:SHARE, :]
    grads_ref[pl.ds(far_second, SHARE), :] = far_mate_ref[:SHARE, :]
    stats = []
    for ref, at in ((own_ref, rows), (mate_ref, rows), (far_ref, SHARE), (far_mate_ref, SHARE)):
        lse = ref[at : at + 16, :].astype(F32)
        delta = ref[at + 16 : at + 32, :].astype(F32)
        stats.append(
            jnp.concatenate(
                [
                    lse[:, :256] + (lse[:, 256:512] + lse[:, 512:]),
                    delta[:, :256] + delta[:, 256:512],
                ],
                axis=0,
            )[:, :rows]
        )
    ordered = []
    for place in range(4):
        pick = stats[place]
        for index in range(4):
            if index != place:
                pick = jnp.where(block ^ index == place, stats[index], pick)
        ordered.append(pick)
    whole = jnp.concatenate(ordered, axis=1)
    stats_ref[:32, :] = whole[:, LONG_AT : LONG_AT + LONG]
    here = whole[:, :LONG]
    for start in (128, 256):
        here = jnp.where(meet_b == start, whole[:, start : start + LONG], here)
    stats_ref[32:, :] = here


def key_back_kernel(groups, grads_ref, stats_ref, kbuf, vbuf, back_a_ref, back_b_ref, part_ref, *refs):
    qbufs, (wk_ref, wv_ref, out_ref) = refs[:-3], refs[-3:]
    block = lax.axis_index("blk")
    rows = out_ref.shape[0]
    at_a, at_b = own_rows(block)
    first = block * rows
    all_columns = slice(groups[0] * WIDE, (groups[-1] + 1) * WIDE)
    parts = []
    for at, count, meet, bias_ref, at_stats in (
        (at_a, ROWS_A, LONG_AT, back_a_ref, 0),
        (at_b, ROWS_B, partner_offset(block), back_b_ref, 32),
    ):
        own_at = pl.multiple_of(first + at, 64)
        dkeys, dvalues = [], []
        for group, qbuf in zip(groups, qbufs):
            columns = slice(group * WIDE, (group + 1) * WIDE)
            at_lse = at_stats + group * GROUP
            at_delta = at_lse + 16
            queries = qbuf[pl.ds(meet, LONG), :]
            grads = grads_ref[pl.ds(meet, LONG), columns]
            scores = nt(spread_heads(kbuf[pl.ds(own_at, count), columns]), queries)
            scores = masked(scores, bias_ref[...])
            probs = jnp.exp(less_rows(scores, stats_ref[at_lse : at_lse + GROUP, :]))
            dprobs = nt(spread_heads(vbuf[pl.ds(own_at, count), columns]), grads)
            dprobs = less_rows(dprobs, stats_ref[at_delta : at_delta + GROUP, :])
            dscores = (probs * dprobs).astype(BF16)
            dkeys.append(join_heads(nn(dscores, queries)).astype(BF16))
            dvalues.append(join_heads(nn(probs.astype(BF16), grads)).astype(BF16))
        parts.append((jnp.concatenate(dkeys, axis=1), jnp.concatenate(dvalues, axis=1)))
    dkey, dvalue = (jnp.concatenate(both, axis=0) for both in zip(*parts))
    added = nt(dkey, wk_ref[:, all_columns]) + nt(dvalue, wv_ref[:, all_columns])
    for at, rows_of in ((at_a, slice(0, ROWS_A)), (at_b, slice(ROWS_A, rows))):
        place = pl.ds(at, rows_of.stop - rows_of.start)
        out_ref[place, :] = (part_ref[place, :] + added[rows_of]).astype(out_ref.dtype)


def unpack_kernel(here_ref, other_ref, grad_ref, *refs):
    places, outs, sems = refs[:13], refs[13:25], refs[25]
    block = lax.axis_index("blk")
    side_here = lax.axis_index("dp") % 2
    core, chip = block % 2, block // 2
    adapt = outs[0].shape[0]
    copies = [
        pltpu.make_async_copy(source, target, sems.at[index])
        for index, (source, target) in enumerate(zip((grad_ref, *outs), places))
    ]
    copies[0].start()
    matrices = (2, 0, 8, 6)
    vectors = ((3,), (4, 5), (9,), (10, 11))
    width = outs[0].shape[1]
    blocks = width // 256
    for index in range(4):
        for side in range(2):
            place = 2 * (chip ^ (index // 2)) + (side_here ^ side)
            part = jnp.where(core == index % 2, here_ref[place], other_ref[place]).astype(F32)
            for block_at in range(blocks):
                lanes = slice(side * width // 2 + 128 * block_at, side * width // 2 + 128 * (block_at + 1))
                outs[matrices[index]][:, lanes] = part[adapt * block_at : adapt * (block_at + 1)]
                for number, vector in enumerate(vectors[index]):
                    outs[vector][lanes] = part[blocks * (adapt + number) + block_at]
            if index == 0 and side == 0:
                outs[1][...] = part[blocks * (adapt + 1), :adapt]
                outs[7][...] = part[blocks * (adapt + 1) + 1, :adapt]
        ready = [matrices[index], *vectors[index]] + ([1, 7] if index == 0 else [])
        for out in ready:
            copies[1 + out].start()
    for copy in copies:
        copy.wait()


def params(megabytes):
    return pltpu.CompilerParams(vmem_limit_bytes=megabytes << 20)


def cost(gigaflop, megabytes):
    return pl.CostEstimate(
        flops=int(gigaflop * 1e9), bytes_accessed=int(megabytes * 1e6), transcendentals=0
    )


def after(array, *others):
    return lax.optimization_barrier((array,) + others)[0]


def vmem(dims, dtype):
    return pltpu.VMEM(dims, dtype)


def in_hbm(array):
    return pltpu.with_memory_space_constraint(array, pltpu.HBM)


def shape(dims, dtype):
    return jax.ShapeDtypeStruct(dims, dtype)


def body(
    dp_size,
    tokens,
    w_query,
    w_key,
    w_value,
    w_out,
    w_inner,
    w_outer,
    down_one,
    dbias_one,
    up_one,
    ubias_one,
    gain_one,
    shift_one,
    down_two,
    dbias_two,
    up_two,
    ubias_two,
    gain_two,
    shift_two,
    seg_len,
    seg_valid,
    cotangent,
):
    rows, _, width = tokens.shape
    adapt = up_one.shape[0]
    hidden = w_inner.shape[1]
    block = lax.axis_index("blk")
    own = tokens.reshape(rows, width)
    cot = cotangent.reshape(rows, width)

    def swap(array, mask):
        return lax.ppermute(array, "blk", [(i, i ^ mask) for i in range(4)])

    def swap_all(array, mask):
        return lax.ppermute(
            array, ("dp", "blk"), [(i, i ^ mask) for i in range(4 * dp_size)]
        )

    mate = swap(own, 1)
    own = pl.pallas_call(
        fetch_kernel,
        in_specs=[HBM],
        out_specs=VMEM,
        out_shape=vmem((rows, width), BF16),
        scratch_shapes=[pltpu.SemaphoreType.DMA],
        compiler_params=params(1),
        cost_estimate=cost(0.1, 1.0),
        name="fetch",
    )(in_hbm(own))
    def near_share(own, mate):
        choices = (
            (own[128:192], own[64:128], own[:64], mate[128:192]),
            (mate[:64], own[128:192], own[64:128], own[:64]),
        )
        halves = []
        for options in choices:
            half = options[0]
            for index in range(1, 4):
                half = jnp.where(block == index, options[index], half)
            halves.append(half)
        return halves

    far = swap(jnp.concatenate(near_share(own, mate), axis=0), 2)
    smalls = (
        cot,
        down_one.T,
        dbias_one,
        up_one,
        ubias_one,
        gain_one,
        shift_one,
        down_two.T,
        dbias_two,
        up_two,
        ubias_two,
        gain_two,
        shift_two,
    )
    half_mask_shapes = [vmem((count, HALF), F32) for count in (ROWS_A, ROWS_B)] * 2
    mask_shapes = [vmem((count, LONG), F32) for count in (ROWS_A, ROWS_B)] * 2
    (
        q,
        kpair,
        vpair,
        bias_a,
        bias_b,
        back_a,
        back_b,
        near_a,
        near_b,
        far_a,
        far_b,
        wq_here,
        wk_here,
        wv_here,
        wout_here,
        winner_here,
        sums0,
        tops0,
        totals0,
        *smalls_here,
    ) = pl.pallas_call(
        project_kernel,
        in_specs=[SMEM] * 2 + [VMEM] * 2 + [HBM] * (5 + len(smalls)),
        out_specs=[VMEM] * (19 + len(smalls)),
        out_shape=[vmem((2 * rows, width), BF16)] * 3
        + mask_shapes
        + half_mask_shapes
        + [vmem((width, width), BF16)] * 4
        + [vmem((width, hidden), BF16)]
        + [vmem((rows, WIDE), F32)]
        + [vmem((1, GROUP * rows, 128), F32)] * 2
        + [vmem(small.shape, small.dtype) for small in smalls],
        scratch_shapes=[pltpu.SemaphoreType.DMA((5 + len(smalls),))],
        compiler_params=params(4),
        cost_estimate=cost(2.0, 12.0),
        name="project",
    )(
        in_hbm(seg_len),
        in_hbm(seg_valid),
        own,
        mate,
        in_hbm(w_query),
        in_hbm(w_key),
        in_hbm(w_value),
        in_hbm(w_out),
        in_hbm(w_inner),
        *(in_hbm(small) for small in smalls),
    )
    far_mate = swap(after(far, q), 1)
    kfar, vfar, sums, tops, totals = pl.pallas_call(
        near_kernel,
        in_specs=[VMEM] * 8,
        out_specs=[VMEM] * 5,
        out_shape=[vmem((SHARE, width), BF16)] * 2
        + [vmem((rows, width - WIDE), F32)]
        + [vmem((width // WIDE - 1, GROUP * rows, 128), F32)] * 2,
        compiler_params=params(5),
        cost_estimate=cost(1.0, 2.0),
        name="near",
    )(far, q, kpair, vpair, near_a, near_b, wk_here, wv_here)

    part_rows = width // 256 * (adapt + 2) + 2
    mixed, kbuf, vbuf, lse, du1, attended, grad_pre, keep, send = pl.pallas_call(
        main_kernel,
        in_specs=[VMEM] * 32 + [HBM],
        out_specs=[HBM] + [VMEM] * 8,
        out_shape=[
            shape((rows, width), BF16),
            vmem((4 * rows, width), BF16),
            vmem((4 * rows, width), BF16),
            vmem((rows, 128), F32),
            vmem((rows, width), F32),
            vmem((rows, width), F32),
            vmem((rows, adapt), BF16),
            vmem((4, part_rows, 128), BF16),
            vmem((4, part_rows, 128), BF16),
        ],
        scratch_shapes=[
            pltpu.VMEM((hidden, width), BF16),
            pltpu.VMEM((width, hidden), BF16),
            pltpu.VMEM((hidden, width), BF16),
            pltpu.VMEM((rows, hidden), F32),
            pltpu.VMEM((rows, width), BF16),
            pltpu.SemaphoreType.DMA((1 + hidden // CHUNK,)),
        ],
        compiler_params=params(22),
        cost_estimate=cost(8.0, 20.0),
        name="layer",
    )(
        own,
        far_mate,
        q,
        kpair,
        vpair,
        kfar,
        vfar,
        sums0,
        tops0,
        totals0,
        sums,
        tops,
        totals,
        far_a,
        far_b,
        *smalls_here,
        wk_here,
        wv_here,
        wout_here,
        winner_here,
        in_hbm(w_outer),
    )

    def add(*terms):
        return functools.reduce(jnp.add, [term.astype(F32) for term in terms]).astype(BF16)

    pack, delta = pl.pallas_call(
        attended_back_kernel,
        in_specs=[VMEM] * 6,
        out_specs=[VMEM] * 2,
        out_shape=[vmem((rows + 32, width), BF16), vmem((rows, 128), F32)],
        compiler_params=params(5),
        cost_estimate=cost(0.5, 2.0),
        name="attended_back",
    )(du1, grad_pre, smalls_here[1], attended, lse, wout_here)

    def query_back(groups, part):
        return pl.pallas_call(
            functools.partial(query_back_kernel, groups),
            in_specs=[VMEM] * 12,
            out_specs=[VMEM] * (len(groups) + 1),
            out_shape=[vmem((4 * rows, WIDE), BF16)] * len(groups) + [vmem((rows, width), F32)],
            compiler_params=params(5),
            cost_estimate=cost(1.0 * len(groups), 3.0),
            name=f"query_back_{groups[0]}",
        )(far, far_mate, q, kbuf, vbuf, bias_a, bias_b, lse, delta, pack, part, wq_here)

    def key_back(groups, qbufs, part, dtype):
        return pl.pallas_call(
            functools.partial(key_back_kernel, groups),
            in_specs=[VMEM] * (9 + len(groups)),
            out_specs=VMEM,
            out_shape=vmem((rows, width), dtype),
            compiler_params=params(5),
            cost_estimate=cost(1.0 * len(groups), 3.0),
            name=f"key_back_{groups[0]}",
        )(grads_row, stats_row, kbuf, vbuf, back_a, back_b, part, *qbufs, wk_here, wv_here)

    total = add(keep, after(swap_all(send, 1), pack))
    arrived = [swap_all(total[index], mask) for index, mask in ((1, 4), (2, 2), (3, 6))]
    pack_mate = swap(after(pack, total), 1)
    qbuf0, qbuf1, part = query_back((0, 1), after(du1, total))
    total = add(total[0], *lax.optimization_barrier((*arrived, part, pack_mate))[:3])
    masks = []
    while 8 << len(masks) < 4 * dp_size:
        masks.append(8 << len(masks))
    arrived = swap_all(total, masks[0])
    pack_now = after(pack, total)
    share = near_share(pack_now, pack_mate) + [pack_now[rows:]]
    pack_far = swap(jnp.concatenate(share, axis=0), 2)
    total = add(total, arrived)
    arrived = swap_all(total, masks[1])
    qbuf2, part = query_back((2,), after(part, total))
    pack_far, part = lax.optimization_barrier((pack_far, part))
    pack_far_mate = swap(pack_far, 1)
    total = add(total, after(arrived, part))
    for mask in masks[2:]:
        total = add(total, swap_all(total, mask))
    others = [swap_all(total, mask) for mask in (4, 2, 6)]
    grads_row, stats_row = pl.pallas_call(
        gather_kernel,
        in_specs=[VMEM] * 4,
        out_specs=[VMEM] * 2,
        out_shape=[vmem((4 * rows, width), BF16), vmem((64, LONG), F32)],
        compiler_params=params(3),
        cost_estimate=cost(0.1, 1.0),
        name="gather",
    )(pack, pack_mate, pack_far, after(pack_far_mate, total))
    part = key_back((0, 1), (qbuf0, qbuf1), after(part, total), F32)
    here = jnp.stack([total, *lax.optimization_barrier((*others, part))[:3]])
    other = swap_all(here, 1)
    input_grad = key_back((2,), (qbuf2,), after(part, here), BF16)

    grad_dims = ((adapt, width), (adapt,), (adapt, width), (width,), (width,), (width,)) * 2
    input_grad, *grads = pl.pallas_call(
        unpack_kernel,
        in_specs=[VMEM] * 3,
        out_specs=[HBM] * 13,
        out_shape=[shape((rows, width), BF16)] + [shape(dims, F32) for dims in grad_dims],
        scratch_shapes=[pltpu.VMEM(dims, F32) for dims in grad_dims]
        + [pltpu.SemaphoreType.DMA((13,))],
        compiler_params=params(5),
        name="unpack",
    )(here, other, input_grad)
    return (mixed.reshape(tokens.shape), input_grad.reshape(tokens.shape)) + tuple(
        grad.T if index in (0, 6) else grad for index, grad in enumerate(grads)
    )


def solution(mesh):
    in_specs = (
        (P("blk", "dp", None),) + (P(),) * 18 + (P("dp", None),) * 2 + (P("blk", "dp", None),)
    )
    out_specs = (P("blk", "dp", None),) * 2 + (P(),) * 12
    return jax.shard_map(
        functools.partial(body, mesh.shape["dp"]),
        mesh=mesh,
        in_specs=in_specs,
        out_specs=out_specs,
        check_vma=False,
    )
```

```python
import functools

import jax
import jax.numpy as jnp
from jax import lax
from jax.experimental import pallas as pl
from jax.experimental.pallas import tpu as pltpu
from jax.sharding import PartitionSpec as P

HEAD = 64
GROUP = 4
LONG_AT = 128
LONG = 512
ROWS_A = 64
WIDE = GROUP * HEAD
HALF = 256
SHARE = 128
CHUNK = 768
ROWS_B = 128
NEG = -1e30
F32 = jnp.float32
BF16 = jnp.bfloat16

VMEM = pl.BlockSpec(memory_space=pltpu.VMEM)
SMEM = pl.BlockSpec(memory_space=pltpu.SMEM)
HBM = pl.BlockSpec(memory_space=pltpu.HBM)


def nn(left, right):
    return lax.dot_general(left, right, (((1,), (0,)), ((), ())), preferred_element_type=F32)


def nt(left, right):
    return lax.dot_general(left, right, (((1,), (1,)), ((), ())), preferred_element_type=F32)


def tn(left, right):
    return lax.dot_general(left, right, (((0,), (0,)), ((), ())), preferred_element_type=F32)


def gelu_both(values):
    phi = 0.5 + 0.5 * lax.erf(values * 0.7071067811865476)
    bell = jnp.exp(-0.5 * values * values)
    return values * phi, phi + values * bell * 0.3989422804014327


def normed(values):
    centre = jnp.mean(values, axis=-1, keepdims=True)
    centred = values - centre
    spread = jnp.mean(centred * centred, axis=-1, keepdims=True)
    scale = lax.rsqrt(spread + 1e-06)
    return centred * scale, scale


def norm_back(incoming, gain, normal, scale):
    scaled = incoming * gain
    first = jnp.mean(scaled, axis=-1, keepdims=True)
    second = jnp.mean(scaled * normal, axis=-1, keepdims=True)
    return scale * (scaled - first - normal * second)


def row_of(ref):
    return ref[...].reshape(1, ref.shape[0])


def own_rows(block):
    return (
        pl.multiple_of(jnp.where(block == 0, 128, 0), 64),
        pl.multiple_of(jnp.where(block == 0, 0, 64), 64),
    )


def far_place(chip):
    return pl.multiple_of(LONG_AT + 2 * SHARE * (1 - chip), 128)


def near_places(block):
    chip = block // 2
    long_at = LONG_AT * (1 - chip)
    short_at = LONG_AT * chip
    outer = (block == 0) | (block == 3)
    return (
        pl.multiple_of(long_at, 128),
        pl.multiple_of(jnp.where(outer, short_at, long_at), 128),
    )


def far_tokens(core, far_ref, far_mate_ref):
    far, far_mate = far_ref[...], far_mate_ref[...]
    first = core == 0
    return jnp.concatenate(
        [jnp.where(first, far, far_mate), jnp.where(first, far_mate, far)], axis=0
    )


def partner_offset(block):
    return pl.multiple_of(jnp.where(block == 0, 0, jnp.where(block == 3, 256, 128)), 128)


def bounds(len_ref, valid_ref, places):
    low = jnp.zeros(places.shape, jnp.int32)
    high = jnp.zeros(places.shape, jnp.int32)
    start = jnp.int32(0)
    for slot in range(len_ref.shape[1]):
        end = start + len_ref[0, slot]
        inside = (places >= start) & (places < end)
        low = jnp.where(inside, start, low)
        high = jnp.where(inside, start + valid_ref[0, slot], high)
        start = end
    return low, high


def bias_of(len_ref, valid_ref, query_at, key_at, rows, columns=LONG):
    places = query_at + lax.broadcasted_iota(jnp.int32, (rows, 1), 0)
    low, high = bounds(len_ref, valid_ref, places)
    keys = key_at + lax.broadcasted_iota(jnp.int32, (rows, columns), 1)
    return jnp.where((keys >= low) & (keys < high), 0.0, NEG)


def bias_back_of(len_ref, valid_ref, key_at, query_at, rows):
    places = query_at + lax.broadcasted_iota(jnp.int32, (1, LONG), 1)
    low, high = bounds(len_ref, valid_ref, places)
    keys = key_at + lax.broadcasted_iota(jnp.int32, (rows, LONG), 0)
    return jnp.where((keys >= low) & (keys < high), 0.0, NEG)


def spread_heads(part):
    lane = lax.broadcasted_iota(jnp.int32, part.shape, 1) // HEAD
    return jnp.concatenate(
        [jnp.where(lane == head, part, jnp.zeros_like(part)) for head in range(GROUP)], axis=0
    )


def join_heads(stacked):
    rows = stacked.shape[0] // GROUP
    lane = lax.broadcasted_iota(jnp.int32, (rows, stacked.shape[1]), 1) // HEAD
    out = stacked[:rows]
    for head in range(1, GROUP):
        out = jnp.where(lane == head, stacked[head * rows : (head + 1) * rows], out)
    return out


def masked(scores, bias):
    split = scores.reshape((GROUP,) + bias.shape)
    return (split + bias).reshape(scores.shape)


def less_rows(stacked, rows):
    count = stacked.shape[0] // GROUP
    return jnp.concatenate(
        [stacked[head * count : (head + 1) * count] - rows[head : head + 1] for head in range(GROUP)],
        axis=0,
    )


def fetch_kernel(source, target, sem):
    copy = pltpu.make_async_copy(source, target, sem)
    copy.start()
    copy.wait()


def project_kernel(
    len_ref,
    valid_ref,
    own_ref,
    mate_ref,
    wq_hbm,
    wk_hbm,
    wv_hbm,
    wout_hbm,
    winner_hbm,
    *refs,
):
    rest = (len(refs) - 20) // 2
    smalls_hbm, refs, sems = refs[:rest], refs[rest:-1], refs[-1]
    project_rows(
        len_ref,
        valid_ref,
        own_ref,
        mate_ref,
        (wq_hbm, wk_hbm, wv_hbm, wout_hbm, winner_hbm),
        *refs[:19],
        tuple(zip(smalls_hbm, refs[19:])),
        sems,
    )


def project_rows(
    len_ref,
    valid_ref,
    own_ref,
    mate_ref,
    weights_hbm,
    q_ref,
    k_ref,
    v_ref,
    bias_a_ref,
    bias_b_ref,
    back_a_ref,
    back_b_ref,
    near_a_ref,
    near_b_ref,
    far_a_ref,
    far_b_ref,
    wq_ref,
    wk_ref,
    wv_ref,
    wout_ref,
    winner_ref,
    sums_ref,
    tops_ref,
    totals_ref,
    smalls,
    sems,
):
    weights = (wq_ref, wk_ref, wv_ref, wout_ref, winner_ref)
    moves = tuple(zip(weights_hbm, weights)) + smalls
    copies = [
        pltpu.make_async_copy(source, target, sems.at[index])
        for index, (source, target) in enumerate(moves)
    ]
    block = lax.axis_index("blk")

    @pl.when(block < 4)
    def _():
        for copy in copies:
            copy.start()

    core = block % 2
    rows = own_ref.shape[0]
    first = block * rows
    at_a, at_b = own_rows(block)
    meet_b = partner_offset(block)
    bias_a_ref[...] = bias_of(len_ref, valid_ref, first + at_a, LONG_AT, ROWS_A)
    bias_b_ref[...] = bias_of(len_ref, valid_ref, first + at_b, meet_b, ROWS_B)
    chip = block // 2
    near_a, near_b = near_places(block)
    pair_at = chip * 2 * rows
    far_at = far_place(chip)
    for at, count, near, near_ref, far_ref in (
        (at_a, ROWS_A, near_a, near_a_ref, far_a_ref),
        (at_b, ROWS_B, near_b, near_b_ref, far_b_ref),
    ):
        near_ref[...] = bias_of(len_ref, valid_ref, first + at, pair_at + near, count, HALF)
        far_ref[...] = bias_of(len_ref, valid_ref, first + at, far_at, count, HALF)
    back_a_ref[...] = bias_back_of(len_ref, valid_ref, first + at_a, LONG_AT, ROWS_A)
    back_b_ref[...] = bias_back_of(len_ref, valid_ref, first + at_b, meet_b, ROWS_B)
    mine = pl.multiple_of(core * rows, rows)
    other = pl.multiple_of((1 - core) * rows, rows)
    both = jnp.concatenate([own_ref[...], mate_ref[...]], axis=0)
    for copy, weight, out, scale in (
        (copies[0], wq_ref, q_ref, 0.125),
        (copies[1], wk_ref, k_ref, 1.0),
        (copies[2], wv_ref, v_ref, 1.0),
    ):
        copy.wait()
        product = (nn(both, weight[...]) * scale).astype(BF16)
        out[pl.ds(mine, rows), :] = product[:rows]
        out[pl.ds(other, rows), :] = product[rows:]
    near_attention(
        (0,), q_ref, k_ref, v_ref, (near_a_ref, near_b_ref), sums_ref, tops_ref, totals_ref
    )
    for copy in copies[3:]:
        copy.wait()


def over_heads(stat):
    count = stat.shape[0] // GROUP
    parts = [stat[head * count : (head + 1) * count] for head in range(GROUP)]
    left = lax.broadcasted_iota(jnp.int32, (1, 128), 1) < HEAD
    return jnp.concatenate(
        [jnp.where(left, parts[0], parts[1]), jnp.where(left, parts[2], parts[3])], axis=1
    )


def near_attention(groups, q_ref, kpair_ref, vpair_ref, masks, sums_ref, tops_ref, totals_ref):
    block = lax.axis_index("blk")
    rows = sums_ref.shape[0]
    core = block % 2
    at_a, at_b = own_rows(block)
    near_a, near_b = near_places(block)
    near_a_ref, near_b_ref = masks
    for at, count, near, bias_ref, at_stat in (
        (at_a, ROWS_A, near_a, near_a_ref, 0),
        (at_b, ROWS_B, near_b, near_b_ref, GROUP * ROWS_A),
    ):
        stacked = pl.ds(at_stat, GROUP * count)
        for index, group in enumerate(groups):
            columns = slice(group * WIDE, (group + 1) * WIDE)
            queries = spread_heads(q_ref[pl.ds(core * rows + at, count), columns])
            scores = masked(nt(queries, kpair_ref[pl.ds(near, HALF), columns]), bias_ref[...])
            top = jnp.max(scores, axis=-1, keepdims=True)
            weights = jnp.exp(scores - top)
            total = jnp.sum(weights, axis=-1, keepdims=True)
            sums = nn(weights.astype(BF16), vpair_ref[pl.ds(near, HALF), columns])
            sums_ref[pl.ds(at, count), index * WIDE : (index + 1) * WIDE] = join_heads(sums)
            tops_ref[index, stacked, :] = jnp.broadcast_to(top, (GROUP * count, 128))
            totals_ref[index, stacked, :] = jnp.broadcast_to(total, (GROUP * count, 128))


def near_kernel(
    far_ref,
    q_ref,
    kpair_ref,
    vpair_ref,
    near_a_ref,
    near_b_ref,
    wk_ref,
    wv_ref,
    kfar_ref,
    vfar_ref,
    sums_ref,
    tops_ref,
    totals_ref,
):
    kfar_ref[...] = nn(far_ref[...], wk_ref[...]).astype(BF16)
    vfar_ref[...] = nn(far_ref[...], wv_ref[...]).astype(BF16)
    near_attention(
        tuple(range(1, q_ref.shape[1] // WIDE)),
        q_ref,
        kpair_ref,
        vpair_ref,
        (near_a_ref, near_b_ref),
        sums_ref,
        tops_ref,
        totals_ref,
    )


def main_kernel(
    own_ref,
    far_mate_ref,
    q_ref,
    kpair_ref,
    vpair_ref,
    kfar_ref,
    vfar_ref,
    sums0_ref,
    tops0_ref,
    totals0_ref,
    sums_ref,
    tops_ref,
    totals_ref,
    far_a_ref,
    far_b_ref,
    cot_ref,
    down1_ref,
    dbias1_ref,
    up1_ref,
    ubias1_ref,
    gain1_ref,
    shift1_ref,
    down2_ref,
    dbias2_ref,
    up2_ref,
    ubias2_ref,
    gain2_ref,
    shift2_ref,
    wk_ref,
    wv_ref,
    wout_ref,
    winner_ref,
    wouter_hbm,
    mixed_hbm,
    kbuf,
    vbuf,
    lse_ref,
    du1_ref,
    attended_ref,
    grad_pre_ref,
    keep_ref,
    send_ref,
    wouter_ref,
    wouter_t_ref,
    winner_t_ref,
    slope_ref,
    mixed_ref,
    sems,
):
    hidden_units = winner_ref.shape[1]

    def outer_copy(index):
        part = pl.ds(pl.multiple_of(index * CHUNK, CHUNK), CHUNK)
        return pltpu.make_async_copy(wouter_hbm.at[part], wouter_ref.at[part], sems.at[1 + index])

    @pl.loop(0, hidden_units // CHUNK)
    def _(index):
        outer_copy(index).start()

    mixed_copy = pltpu.make_async_copy(mixed_ref, mixed_hbm, sems.at[0])
    block = lax.axis_index("blk")
    core = block % 2
    chip = block // 2
    rows, width = own_ref.shape
    at_a, at_b = own_rows(block)

    def mine(ref):
        return jnp.concatenate([ref[pl.ds(at_a, ROWS_A), :], ref[pl.ds(at_b, ROWS_B), :]], axis=0)

    def put(ref, value):
        ref[pl.ds(at_a, ROWS_A), :] = value[:ROWS_A]
        ref[pl.ds(at_b, ROWS_B), :] = value[ROWS_A:]

    near = pl.multiple_of(chip * 2 * rows, 2 * rows)
    kbuf[pl.ds(near, 2 * rows), :] = kpair_ref[...]
    vbuf[pl.ds(near, 2 * rows), :] = vpair_ref[...]
    far_at = far_place(chip)
    far_first = pl.multiple_of(far_at + SHARE * core, 128)
    far_second = pl.multiple_of(far_at + SHARE * (1 - core), 128)
    kbuf[pl.ds(far_first, SHARE), :] = kfar_ref[...]
    vbuf[pl.ds(far_first, SHARE), :] = vfar_ref[...]
    kbuf[pl.ds(far_second, SHARE), :] = nn(far_mate_ref[...], wk_ref[...]).astype(BF16)
    vbuf[pl.ds(far_second, SHARE), :] = nn(far_mate_ref[...], wv_ref[...]).astype(BF16)

    lane = lax.broadcasted_iota(jnp.int32, (1, 128), 1)
    attended_parts = []
    lse_parts = []
    for at, count, bias_ref, at_stat in (
        (at_a, ROWS_A, far_a_ref, 0),
        (at_b, ROWS_B, far_b_ref, GROUP * ROWS_A),
    ):
        pieces = []
        lse = jnp.zeros((count, 128), F32)
        stacked = pl.ds(at_stat, GROUP * count)
        for group in range(width // WIDE):
            columns = slice(group * WIDE, (group + 1) * WIDE)
            queries = spread_heads(q_ref[pl.ds(core * rows + at, count), columns])
            scores = masked(nt(queries, kbuf[pl.ds(far_at, HALF), columns]), bias_ref[...])
            near_sums = sums0_ref if group == 0 else sums_ref
            near_tops = tops0_ref if group == 0 else tops_ref
            near_totals = totals0_ref if group == 0 else totals_ref
            held = max(group - 1, 0)
            top_near = near_tops[held, stacked, :]
            top = jnp.maximum(top_near, jnp.max(scores, axis=-1, keepdims=True))
            weights = jnp.exp(scores - jnp.concatenate([top, top], axis=1))
            shrink = jnp.exp(top_near - top)
            total = shrink * near_totals[held, stacked, :] + jnp.sum(
                weights, axis=-1, keepdims=True
            )
            sums = join_heads(nn(weights.astype(BF16), vbuf[pl.ds(far_at, HALF), columns]))
            sums = sums + near_sums[
                pl.ds(at, count), held * WIDE : (held + 1) * WIDE
            ] * over_heads(shrink)
            pieces.append(sums * over_heads(1.0 / total))
            log_total = top + jnp.log(total)
            for head in range(GROUP):
                one = log_total[head * count : (head + 1) * count]
                lse = jnp.where(lane == group * GROUP + head, one, lse)
        attended_parts.append(jnp.concatenate(pieces, axis=1))
        lse_parts.append(lse)
    attended_f = jnp.concatenate(attended_parts, axis=0)
    put(lse_ref, jnp.concatenate(lse_parts, axis=0))
    put(attended_ref, attended_f)
    attended = attended_f.astype(BF16)
    branch = nn(attended, wout_ref[...]).astype(BF16)

    pre1 = nt(branch, down1_ref[...]) + row_of(dbias1_ref)
    inner1_f, slope1 = gelu_both(pre1)
    inner1 = inner1_f.astype(BF16)
    summed = (
        mine(own_ref).astype(F32) + branch.astype(F32) + nn(inner1, up1_ref[...]) + row_of(ubias1_ref)
    )
    normal1, scale1 = normed(summed)
    gain1 = row_of(gain1_ref)
    mid = (normal1 * gain1 + row_of(shift1_ref)).astype(BF16)

    for index in range(hidden_units // CHUNK):
        outer_copy(index).wait()
    ffn_f = jnp.zeros((rows, width), F32)
    for at in range(0, hidden_units, CHUNK):
        hidden_f, slope = gelu_both(nn(mid, winner_ref[:, at : at + CHUNK]))
        slope_ref[:, at : at + CHUNK] = slope
        wouter_t_ref[:, at : at + CHUNK] = wouter_ref[at : at + CHUNK, :].T
        winner_t_ref[at : at + CHUNK, :] = winner_ref[:, at : at + CHUNK].T
        ffn_f = ffn_f + nn(hidden_f.astype(BF16), wouter_ref[at : at + CHUNK, :])
    ffn = ffn_f.astype(BF16)

    pre2 = nt(ffn, down2_ref[...]) + row_of(dbias2_ref)
    inner2_f, slope2 = gelu_both(pre2)
    inner2 = inner2_f.astype(BF16)
    summed = mid.astype(F32) + ffn.astype(F32) + nn(inner2, up2_ref[...]) + row_of(ubias2_ref)
    normal2, scale2 = normed(summed)
    gain2 = row_of(gain2_ref)
    put(mixed_ref, (normal2 * gain2 + row_of(shift2_ref)).astype(BF16))
    mixed_copy.start()

    cot = mine(cot_ref).astype(F32)
    grad_gain2 = jnp.sum(cot * normal2, axis=0, keepdims=True)
    grad_shift2 = jnp.sum(cot, axis=0, keepdims=True)
    du2 = norm_back(cot, gain2, normal2, scale2)

    def adapter_back(source, up, inner, slope, incoming):
        out_grad = incoming.astype(BF16)
        grad_up = tn(inner, out_grad)
        grad_ubias = jnp.sum(out_grad.astype(F32), axis=0, keepdims=True)
        grad_pre = (nt(out_grad, up) * slope).astype(BF16)
        grad_down = tn(grad_pre, source)
        grad_dbias = jnp.sum(grad_pre.astype(F32), axis=0, keepdims=True)
        return grad_pre, grad_down, grad_dbias, grad_up, grad_ubias

    grad_pre2, grad_down2, grad_dbias2, grad_up2, grad_ubias2 = adapter_back(
        ffn, up2_ref[...], inner2, slope2, du2
    )
    dffn = (du2 + nn(grad_pre2, down2_ref[...])).astype(BF16)
    dmid = du2
    for at in range(0, hidden_units, CHUNK):
        dhidden = (nn(dffn, wouter_t_ref[:, at : at + CHUNK]) * slope_ref[:, at : at + CHUNK]).astype(
            BF16
        )
        dmid = dmid + nn(dhidden, winner_t_ref[at : at + CHUNK, :])

    grad_gain1 = jnp.sum(dmid * normal1, axis=0, keepdims=True)
    grad_shift1 = jnp.sum(dmid, axis=0, keepdims=True)
    du1 = norm_back(dmid, gain1, normal1, scale1)
    grad_pre1, grad_down1, grad_dbias1, grad_up1, grad_ubias1 = adapter_back(
        branch, up1_ref[...], inner1, slope1, du1
    )
    put(du1_ref, du1)
    put(grad_pre_ref, grad_pre1)

    blank = jnp.zeros((1, width), F32)
    both_dbias = jnp.concatenate(
        [
            grad_dbias1,
            jnp.zeros((1, 128 - grad_dbias1.shape[1]), F32),
            grad_dbias2,
            jnp.zeros((1, width - 128 - grad_dbias2.shape[1]), F32),
        ],
        axis=1,
    )
    quarters = (
        (grad_up1, grad_ubias1, both_dbias),
        (grad_down1, grad_gain1, grad_shift1),
        (grad_up2, grad_ubias2, blank),
        (grad_down2, grad_gain2, grad_shift2),
    )
    filler = jnp.zeros((2, 128), F32)

    def part_of(quarter, side):
        pieces = [
            array[:, at : at + 128]
            for array in quarter
            for at in range(side * width // 2, (side + 1) * width // 2, 128)
        ]
        return jnp.concatenate(pieces + [filler], axis=0).astype(BF16)

    side_here = lax.axis_index("dp") % 2
    for chip_of in range(2):
        for side in range(2):
            even, odd = (part_of(quarters[2 * chip_of + index], side) for index in range(2))
            place = 2 * (chip ^ chip_of) + (side_here ^ side)
            keep_ref[place] = jnp.where(core == 0, even, odd)
            send_ref[place] = jnp.where(core == 0, odd, even)
    mixed_copy.wait()


def attended_back_kernel(
    du1_ref, grad_pre_ref, down1_ref, attended_ref, lse_ref, wout_ref, pack_ref, delta_ref
):
    rows, width = du1_ref.shape
    dbranch = (du1_ref[...] + nn(grad_pre_ref[...], down1_ref[...])).astype(BF16)
    dattended = nt(dbranch, wout_ref[...]).astype(BF16)
    pack_ref[:rows, :] = dattended
    product = dattended.astype(F32) * attended_ref[...]
    product_hi = product.astype(BF16)
    product_lo = (product - product_hi.astype(F32)).astype(BF16)
    head_of = lax.broadcasted_iota(jnp.int32, (128, width), 1) // HEAD
    picks = (head_of == lax.broadcasted_iota(jnp.int32, (128, width), 0)).astype(BF16)
    delta = nt(product_hi, picks) + nt(product_lo, picks)
    delta_ref[...] = delta
    blank = jnp.zeros((256 - rows, 128), F32)
    delta_rows = jnp.transpose(jnp.concatenate([delta, blank], axis=0))[:16]
    lse_rows = jnp.transpose(jnp.concatenate([lse_ref[...], blank], axis=0))[:16]

    def pieces_of(value, count):
        out = []
        for _ in range(count):
            piece = value.astype(BF16)
            value = value - piece.astype(F32)
            out.append(piece)
        return out

    pack_ref[rows : rows + 16, :] = jnp.concatenate(pieces_of(lse_rows, 3), axis=1)
    pack_ref[rows + 16 : rows + 32, :] = jnp.concatenate(
        pieces_of(delta_rows, 2) + [jnp.zeros((16, 256), BF16)], axis=1
    )


def query_back_kernel(
    groups,
    far_ref,
    far_mate_ref,
    q_ref,
    kbuf,
    vbuf,
    bias_a_ref,
    bias_b_ref,
    lse_ref,
    delta_ref,
    pack_ref,
    part_in_ref,
    wq_ref,
    *outs,
):
    block = lax.axis_index("blk")
    rows = q_ref.shape[0] // 2
    core, chip = block % 2, block // 2
    at_a, at_b = own_rows(block)
    meet_b = partner_offset(block)
    all_columns = slice(groups[0] * WIDE, (groups[-1] + 1) * WIDE)
    wq = wq_ref[:, all_columns]
    queries_far = (nn(far_tokens(core, far_ref, far_mate_ref), wq) * 0.125).astype(BF16)
    part_ref = outs[-1]
    for index, (group, qbuf) in enumerate(zip(groups, outs)):
        near = pl.ds(pl.multiple_of(chip * 2 * rows, rows), 2 * rows)
        qbuf[near, :] = q_ref[:, group * WIDE : (group + 1) * WIDE]
        qbuf[pl.ds(far_place(chip), 2 * SHARE), :] = queries_far[
            :, index * WIDE : (index + 1) * WIDE
        ]
    parts = []
    for at, count, meet, bias_ref in (
        (at_a, ROWS_A, LONG_AT, bias_a_ref),
        (at_b, ROWS_B, meet_b, bias_b_ref),
    ):
        lse = lse_ref[pl.ds(at, count), :]
        delta = delta_ref[pl.ds(at, count), :]
        pieces = []
        for group in groups:
            columns = slice(group * WIDE, (group + 1) * WIDE)
            heads = range(group * GROUP, (group + 1) * GROUP)
            log_total = jnp.concatenate([lse[:, head : head + 1] for head in heads], axis=0)
            deltas = jnp.concatenate([delta[:, head : head + 1] for head in heads], axis=0)
            keys = kbuf[pl.ds(meet, LONG), columns]
            scores = nt(spread_heads(q_ref[pl.ds(core * rows + at, count), columns]), keys)
            scores = masked(scores, bias_ref[...])
            probs = jnp.exp(scores - log_total)
            dprobs = nt(
                spread_heads(pack_ref[pl.ds(at, count), columns]), vbuf[pl.ds(meet, LONG), columns]
            )
            dscores = (probs * (dprobs - deltas)).astype(BF16)
            pieces.append(join_heads(nn(dscores, keys)).astype(BF16))
        parts.append(jnp.concatenate(pieces, axis=1))
    added = nt(jnp.concatenate(parts, axis=0), wq) * 0.125
    for at, rows_of in ((at_a, slice(0, ROWS_A)), (at_b, slice(ROWS_A, rows))):
        place = pl.ds(at, rows_of.stop - rows_of.start)
        part_ref[place, :] = part_in_ref[place, :] + added[rows_of]


def gather_kernel(own_ref, mate_ref, far_ref, far_mate_ref, grads_ref, stats_ref):
    block = lax.axis_index("blk")
    rows = own_ref.shape[0] - 32
    core, chip = block % 2, block // 2
    meet_b = partner_offset(block)
    grads_ref[pl.ds(pl.multiple_of(block * rows, rows), rows), :] = own_ref[:rows, :]
    grads_ref[pl.ds(pl.multiple_of((block ^ 1) * rows, rows), rows), :] = mate_ref[:rows, :]
    far_at = far_place(chip)
    far_first = pl.multiple_of(far_at + SHARE * core, 128)
    far_second = pl.multiple_of(far_at + SHARE * (1 - core), 128)
    grads_ref[pl.ds(far_first, SHARE), :] = far_ref[:SHARE, :]
    grads_ref[pl.ds(far_second, SHARE), :] = far_mate_ref[:SHARE, :]
    stats = []
    for ref, at in ((own_ref, rows), (mate_ref, rows), (far_ref, SHARE), (far_mate_ref, SHARE)):
        lse = ref[at : at + 16, :].astype(F32)
        delta = ref[at + 16 : at + 32, :].astype(F32)
        stats.append(
            jnp.concatenate(
                [
                    lse[:, :256] + (lse[:, 256:512] + lse[:, 512:]),
                    delta[:, :256] + delta[:, 256:512],
                ],
                axis=0,
            )[:, :rows]
        )
    ordered = []
    for place in range(4):
        pick = stats[place]
        for index in range(4):
            if index != place:
                pick = jnp.where(block ^ index == place, stats[index], pick)
        ordered.append(pick)
    whole = jnp.concatenate(ordered, axis=1)
    stats_ref[:32, :] = whole[:, LONG_AT : LONG_AT + LONG]
    here = whole[:, :LONG]
    for start in (128, 256):
        here = jnp.where(meet_b == start, whole[:, start : start + LONG], here)
    stats_ref[32:, :] = here


def key_back_kernel(groups, grads_ref, stats_ref, kbuf, vbuf, back_a_ref, back_b_ref, part_ref, *refs):
    qbufs, (wk_ref, wv_ref, out_ref) = refs[:-3], refs[-3:]
    block = lax.axis_index("blk")
    rows = out_ref.shape[0]
    at_a, at_b = own_rows(block)
    first = block * rows
    all_columns = slice(groups[0] * WIDE, (groups[-1] + 1) * WIDE)
    parts = []
    for at, count, meet, bias_ref, at_stats in (
        (at_a, ROWS_A, LONG_AT, back_a_ref, 0),
        (at_b, ROWS_B, partner_offset(block), back_b_ref, 32),
    ):
        own_at = pl.multiple_of(first + at, 64)
        dkeys, dvalues = [], []
        for group, qbuf in zip(groups, qbufs):
            columns = slice(group * WIDE, (group + 1) * WIDE)
            at_lse = at_stats + group * GROUP
            at_delta = at_lse + 16
            queries = qbuf[pl.ds(meet, LONG), :]
            grads = grads_ref[pl.ds(meet, LONG), columns]
            scores = nt(spread_heads(kbuf[pl.ds(own_at, count), columns]), queries)
            scores = masked(scores, bias_ref[...])
            probs = jnp.exp(less_rows(scores, stats_ref[at_lse : at_lse + GROUP, :]))
            dprobs = nt(spread_heads(vbuf[pl.ds(own_at, count), columns]), grads)
            dprobs = less_rows(dprobs, stats_ref[at_delta : at_delta + GROUP, :])
            dscores = (probs * dprobs).astype(BF16)
            dkeys.append(join_heads(nn(dscores, queries)).astype(BF16))
            dvalues.append(join_heads(nn(probs.astype(BF16), grads)).astype(BF16))
        parts.append((jnp.concatenate(dkeys, axis=1), jnp.concatenate(dvalues, axis=1)))
    dkey, dvalue = (jnp.concatenate(both, axis=0) for both in zip(*parts))
    added = nt(dkey, wk_ref[:, all_columns]) + nt(dvalue, wv_ref[:, all_columns])
    for at, rows_of in ((at_a, slice(0, ROWS_A)), (at_b, slice(ROWS_A, rows))):
        place = pl.ds(at, rows_of.stop - rows_of.start)
        out_ref[place, :] = (part_ref[place, :] + added[rows_of]).astype(out_ref.dtype)


def unpack_kernel(here_ref, other_ref, grad_ref, *refs):
    places, outs, sems = refs[:13], refs[13:25], refs[25]
    block = lax.axis_index("blk")
    side_here = lax.axis_index("dp") % 2
    core, chip = block % 2, block // 2
    adapt = outs[0].shape[0]
    copies = [
        pltpu.make_async_copy(source, target, sems.at[index])
        for index, (source, target) in enumerate(zip((grad_ref, *outs), places))
    ]
    copies[0].start()
    matrices = (2, 0, 8, 6)
    vectors = ((3,), (4, 5), (9,), (10, 11))
    width = outs[0].shape[1]
    blocks = width // 256
    for index in range(4):
        for side in range(2):
            place = 2 * (chip ^ (index // 2)) + (side_here ^ side)
            part = jnp.where(core == index % 2, here_ref[place], other_ref[place]).astype(F32)
            for block_at in range(blocks):
                lanes = slice(side * width // 2 + 128 * block_at, side * width // 2 + 128 * (block_at + 1))
                outs[matrices[index]][:, lanes] = part[adapt * block_at : adapt * (block_at + 1)]
                for number, vector in enumerate(vectors[index]):
                    outs[vector][lanes] = part[blocks * (adapt + number) + block_at]
            if index == 0 and side == 0:
                outs[1][...] = part[blocks * (adapt + 1), :adapt]
                outs[7][...] = part[blocks * (adapt + 1) + 1, :adapt]
        ready = [matrices[index], *vectors[index]] + ([1, 7] if index == 0 else [])
        for out in ready:
            copies[1 + out].start()
    for copy in copies:
        copy.wait()


def params(megabytes):
    return pltpu.CompilerParams(vmem_limit_bytes=megabytes << 20)


def cost(gigaflop, megabytes):
    return pl.CostEstimate(
        flops=int(gigaflop * 1e9), bytes_accessed=int(megabytes * 1e6), transcendentals=0
    )


def after(array, *others):
    return lax.optimization_barrier((array,) + others)[0]


def vmem(dims, dtype):
    return pltpu.VMEM(dims, dtype)


def in_hbm(array):
    return pltpu.with_memory_space_constraint(array, pltpu.HBM)


def shape(dims, dtype):
    return jax.ShapeDtypeStruct(dims, dtype)


def body(
    dp_size,
    tokens,
    w_query,
    w_key,
    w_value,
    w_out,
    w_inner,
    w_outer,
    down_one,
    dbias_one,
    up_one,
    ubias_one,
    gain_one,
    shift_one,
    down_two,
    dbias_two,
    up_two,
    ubias_two,
    gain_two,
    shift_two,
    seg_len,
    seg_valid,
    cotangent,
):
    rows, _, width = tokens.shape
    adapt = up_one.shape[0]
    hidden = w_inner.shape[1]
    block = lax.axis_index("blk")
    own = tokens.reshape(rows, width)
    cot = cotangent.reshape(rows, width)

    def swap(array, mask):
        return lax.ppermute(array, "blk", [(i, i ^ mask) for i in range(4)])

    def swap_all(array, mask):
        return lax.ppermute(
            array, ("dp", "blk"), [(i, i ^ mask) for i in range(4 * dp_size)]
        )

    mate = swap(own, 1)
    own = pl.pallas_call(
        fetch_kernel,
        in_specs=[HBM],
        out_specs=VMEM,
        out_shape=vmem((rows, width), BF16),
        scratch_shapes=[pltpu.SemaphoreType.DMA],
        compiler_params=params(1),
        cost_estimate=cost(0.1, 1.0),
        name="fetch",
    )(in_hbm(own))
    def near_share(own, mate):
        choices = (
            (own[128:192], own[64:128], own[:64], mate[128:192]),
            (mate[:64], own[128:192], own[64:128], own[:64]),
        )
        halves = []
        for options in choices:
            half = options[0]
            for index in range(1, 4):
                half = jnp.where(block == index, options[index], half)
            halves.append(half)
        return halves

    far = swap(jnp.concatenate(near_share(own, mate), axis=0), 2)
    smalls = (
        cot,
        down_one.T,
        dbias_one,
        up_one,
        ubias_one,
        gain_one,
        shift_one,
        down_two.T,
        dbias_two,
        up_two,
        ubias_two,
        gain_two,
        shift_two,
    )
    half_mask_shapes = [vmem((count, HALF), F32) for count in (ROWS_A, ROWS_B)] * 2
    mask_shapes = [vmem((count, LONG), F32) for count in (ROWS_A, ROWS_B)] * 2
    (
        q,
        kpair,
        vpair,
        bias_a,
        bias_b,
        back_a,
        back_b,
        near_a,
        near_b,
        far_a,
        far_b,
        wq_here,
        wk_here,
        wv_here,
        wout_here,
        winner_here,
        sums0,
        tops0,
        totals0,
        *smalls_here,
    ) = pl.pallas_call(
        project_kernel,
        in_specs=[SMEM] * 2 + [VMEM] * 2 + [HBM] * (5 + len(smalls)),
        out_specs=[VMEM] * (19 + len(smalls)),
        out_shape=[vmem((2 * rows, width), BF16)] * 3
        + mask_shapes
        + half_mask_shapes
        + [vmem((width, width), BF16)] * 4
        + [vmem((width, hidden), BF16)]
        + [vmem((rows, WIDE), F32)]
        + [vmem((1, GROUP * rows, 128), F32)] * 2
        + [vmem(small.shape, small.dtype) for small in smalls],
        scratch_shapes=[pltpu.SemaphoreType.DMA((5 + len(smalls),))],
        compiler_params=params(4),
        cost_estimate=cost(2.0, 12.0),
        name="project",
    )(
        in_hbm(seg_len),
        in_hbm(seg_valid),
        own,
        mate,
        in_hbm(w_query),
        in_hbm(w_key),
        in_hbm(w_value),
        in_hbm(w_out),
        in_hbm(w_inner),
        *(in_hbm(small) for small in smalls),
    )
    far_mate = swap(after(far, q), 1)
    kfar, vfar, sums, tops, totals = pl.pallas_call(
        near_kernel,
        in_specs=[VMEM] * 8,
        out_specs=[VMEM] * 5,
        out_shape=[vmem((SHARE, width), BF16)] * 2
        + [vmem((rows, width - WIDE), F32)]
        + [vmem((width // WIDE - 1, GROUP * rows, 128), F32)] * 2,
        compiler_params=params(5),
        cost_estimate=cost(1.0, 2.0),
        name="near",
    )(far, q, kpair, vpair, near_a, near_b, wk_here, wv_here)

    part_rows = width // 256 * (adapt + 2) + 2
    mixed, kbuf, vbuf, lse, du1, attended, grad_pre, keep, send = pl.pallas_call(
        main_kernel,
        in_specs=[VMEM] * 32 + [HBM],
        out_specs=[HBM] + [VMEM] * 8,
        out_shape=[
            shape((rows, width), BF16),
            vmem((4 * rows, width), BF16),
            vmem((4 * rows, width), BF16),
            vmem((rows, 128), F32),
            vmem((rows, width), F32),
            vmem((rows, width), F32),
            vmem((rows, adapt), BF16),
            vmem((4, part_rows, 128), BF16),
            vmem((4, part_rows, 128), BF16),
        ],
        scratch_shapes=[
            pltpu.VMEM((hidden, width), BF16),
            pltpu.VMEM((width, hidden), BF16),
            pltpu.VMEM((hidden, width), BF16),
            pltpu.VMEM((rows, hidden), F32),
            pltpu.VMEM((rows, width), BF16),
            pltpu.SemaphoreType.DMA((1 + hidden // CHUNK,)),
        ],
        compiler_params=params(22),
        cost_estimate=cost(8.0, 20.0),
        name="layer",
    )(
        own,
        far_mate,
        q,
        kpair,
        vpair,
        kfar,
        vfar,
        sums0,
        tops0,
        totals0,
        sums,
        tops,
        totals,
        far_a,
        far_b,
        *smalls_here,
        wk_here,
        wv_here,
        wout_here,
        winner_here,
        in_hbm(w_outer),
    )

    def add(*terms):
        return functools.reduce(jnp.add, [term.astype(F32) for term in terms]).astype(BF16)

    pack, delta = pl.pallas_call(
        attended_back_kernel,
        in_specs=[VMEM] * 6,
        out_specs=[VMEM] * 2,
        out_shape=[vmem((rows + 32, width), BF16), vmem((rows, 128), F32)],
        compiler_params=params(5),
        cost_estimate=cost(0.5, 2.0),
        name="attended_back",
    )(du1, grad_pre, smalls_here[1], attended, lse, wout_here)

    def query_back(groups, part):
        return pl.pallas_call(
            functools.partial(query_back_kernel, groups),
            in_specs=[VMEM] * 12,
            out_specs=[VMEM] * (len(groups) + 1),
            out_shape=[vmem((4 * rows, WIDE), BF16)] * len(groups) + [vmem((rows, width), F32)],
            compiler_params=params(5),
            cost_estimate=cost(1.0 * len(groups), 3.0),
            name=f"query_back_{groups[0]}",
        )(far, far_mate, q, kbuf, vbuf, bias_a, bias_b, lse, delta, pack, part, wq_here)

    def key_back(groups, qbufs, part, dtype):
        return pl.pallas_call(
            functools.partial(key_back_kernel, groups),
            in_specs=[VMEM] * (9 + len(groups)),
            out_specs=VMEM,
            out_shape=vmem((rows, width), dtype),
            compiler_params=params(5),
            cost_estimate=cost(1.0 * len(groups), 3.0),
            name=f"key_back_{groups[0]}",
        )(grads_row, stats_row, kbuf, vbuf, back_a, back_b, part, *qbufs, wk_here, wv_here)

    total = add(keep, after(swap_all(send, 1), pack))
    arrived = [swap_all(total[index], mask) for index, mask in ((1, 4), (2, 2), (3, 6))]
    pack_mate = swap(after(pack, total), 1)
    qbuf0, qbuf1, part = query_back((0, 1), after(du1, total))
    total = add(total[0], *lax.optimization_barrier((*arrived, part, pack_mate))[:3])
    masks = []
    while 8 << len(masks) < 4 * dp_size:
        masks.append(8 << len(masks))
    arrived = swap_all(total, masks[0])
    pack_now = after(pack, total)
    share = near_share(pack_now, pack_mate) + [pack_now[rows:]]
    pack_far = swap(jnp.concatenate(share, axis=0), 2)
    total = add(total, arrived)
    arrived = swap_all(total, masks[1])
    qbuf2, part = query_back((2,), after(part, total))
    pack_far, part = lax.optimization_barrier((pack_far, part))
    pack_far_mate = swap(pack_far, 1)
    total = add(total, after(arrived, part))
    for mask in masks[2:]:
        total = add(total, swap_all(total, mask))
    others = [swap_all(total, mask) for mask in (6, 4, 2)]
    grads_row, stats_row = pl.pallas_call(
        gather_kernel,
        in_specs=[VMEM] * 4,
        out_specs=[VMEM] * 2,
        out_shape=[vmem((4 * rows, width), BF16), vmem((64, LONG), F32)],
        compiler_params=params(3),
        cost_estimate=cost(0.1, 1.0),
        name="gather",
    )(pack, pack_mate, pack_far, after(pack_far_mate, total))
    part = key_back((0, 1), (qbuf0, qbuf1), after(part, total), F32)
    others = [others[1], others[2], others[0]]
    here = jnp.stack([total, *lax.optimization_barrier((*others, part))[:3]])
    other = swap_all(here, 1)
    input_grad = key_back((2,), (qbuf2,), after(part, here), BF16)

    grad_dims = ((adapt, width), (adapt,), (adapt, width), (width,), (width,), (width,)) * 2
    input_grad, *grads = pl.pallas_call(
        unpack_kernel,
        in_specs=[VMEM] * 3,
        out_specs=[HBM] * 13,
        out_shape=[shape((rows, width), BF16)] + [shape(dims, F32) for dims in grad_dims],
        scratch_shapes=[pltpu.VMEM(dims, F32) for dims in grad_dims]
        + [pltpu.SemaphoreType.DMA((13,))],
        compiler_params=params(5),
        name="unpack",
    )(here, other, input_grad)
    return (mixed.reshape(tokens.shape), input_grad.reshape(tokens.shape)) + tuple(
        grad.T if index in (0, 6) else grad for index, grad in enumerate(grads)
    )


def solution(mesh):
    in_specs = (
        (P("blk", "dp", None),) + (P(),) * 18 + (P("dp", None),) * 2 + (P("blk", "dp", None),)
    )
    out_specs = (P("blk", "dp", None),) * 2 + (P(),) * 12
    return jax.shard_map(
        functools.partial(body, mesh.shape["dp"]),
        mesh=mesh,
        in_specs=in_specs,
        out_specs=out_specs,
        check_vma=False,
    )
```
